32 devices in a mesh: fsdp: 8 (over z, x), tp: 4 (over y, core).
Axes of the slice: x: 2, y: 2, z: 4, core: 2. Of those that a mesh axis runs over, the one named last changes fastest.
Arguments:
- inputs: bfloat16 [256, 16, 768], P('tp', 'fsdp'), may hold values from -6 to 6
- conditioning: bfloat16 [16, 768], P('fsdp'), may hold values from -6 to 6
- ada_weight: bfloat16 [768, 4608], P('fsdp'), may hold values from -0.21875 to 0.21875
- ada_bias: bfloat16 [4608], P('fsdp'), may hold values from -3 to 3
- query_key_value_weight: bfloat16 [768, 3, 768], P('fsdp', None, 'tp'), may hold values from -0.21875 to 0.21875
- qv_bias: bfloat16 [2, 768], P(None, 'fsdp'), may hold values from -3 to 3
- attention_output_weight: bfloat16 [768, 768], P('tp', 'fsdp'), may hold values from -0.875 to 0.875
- attention_output_bias: bfloat16 [768], P('fsdp'), may hold values from -3 to 3
- expand_weight: bfloat16 [768, 3072], P('fsdp', 'tp'), may hold values from -0.21875 to 0.21875
- hidden_layer_bias: bfloat16 [3072], P('fsdp'), may hold values from -3 to 3
- contract_weight: bfloat16 [3072, 768], P('tp', 'fsdp'), may hold values from -0.109375 to 0.109375
- contract_bias: bfloat16 [768], P('fsdp'), may hold values from -3 to 3
- out_cotangent: bfloat16 [256, 16, 768], P('tp', 'fsdp'), may hold values from -6 to 6
Outputs:
- output: bfloat16 [256, 16, 768], P('tp', 'fsdp')
- inputs_grad: float32 [256, 16, 768], P('tp', 'fsdp')
- cond_grad: float32 [16, 768], P('fsdp')
- ada_weight_grad: float32 [768, 4608], P('fsdp')
- ada_bias_grad: float32 [4608], P('fsdp')
- qkv_weight_grad: float32 [768, 3, 768], P('fsdp', None, 'tp')
- qv_bias_grad: float32 [2, 768], P(None, 'fsdp')
- proj_weight_grad: float32 [768, 768], P('tp', 'fsdp')
- proj_bias_grad: float32 [768], P('fsdp')
- fc1_weight_grad: float32 [768, 3072], P('fsdp', 'tp')
- fc1_bias_grad: float32 [3072], P('fsdp')
- fc2_weight_grad: float32 [3072, 768], P('tp', 'fsdp')
- fc2_bias_grad: float32 [768], P('fsdp')
The draws below stay inside these ranges and needn't reach their ends.
All inputs are finite; a program needn't handle non-finite values.
Results may differ from the reference program's by a relative error of at most 0.019.
The reference program's roundings to bfloat16 on the way count: a program that leaves them out, or rounds other values in their place, can miss the bound.
Values may be sent and summed in bfloat16 or wider, within the bound.
No kernel may reach another device: no remote copies, remote signals or barrier semaphores. Data moves between devices by JAX's collectives and lax.ppermute only.
A program may use at most 64 MiB of HBM per device.

```python
import math
import jax
import jax.numpy as jnp
from jax import lax

D = 768
HEADS = 12
HEAD = 64
FF = 3072
SEQ = 256
LAT_DEV = 2
LATENTS = 16


def raised(drawn, stream_key, source, target, parts, factor):
    owner, partner = [(jnp.arange(drawn.shape[dim]) // (drawn.shape[dim] // parts)).reshape([-1 if axis == dim else 1 for axis in range(drawn.ndim)]) for dim in (source, target)]
    chosen = jax.random.permutation(stream_key, parts)[partner]
    strong = (owner == chosen) | (owner == (partner + parts // 2) % parts)
    return jnp.where(strong, factor * drawn, drawn)


def shard_levels(rng, dims, split, low, high):
    factor_of = 1.0
    for dim, shards_of in split:
        steps = jax.random.uniform(jax.random.fold_in(jax.random.fold_in(rng, 6), dim), (shards_of,), jnp.float32, low / len(split), high / len(split))
        factor_of = factor_of * jnp.repeat(jnp.exp(steps), dims[dim] // shards_of).reshape((-1,) + (1,) * (len(dims) - 1 - dim))
    return factor_of


def bell_draw(key, shape, deviation, reach, cuts=(), held_as=jnp.bfloat16):
    array = deviation * jax.random.normal(key, shape, jnp.float32)
    if cuts:
        array = array * shard_levels(key, shape, cuts, -0.22, 0.18)
    return jnp.clip(array, -reach, reach).astype(held_as)


def bell_draw_with(rng, shape, deviation, bound, cuts, heavy, dtype=jnp.bfloat16):
    array = deviation * jax.random.normal(rng, shape, jnp.float32)
    if cuts:
        array = array * shard_levels(rng, shape, cuts, -0.22, 0.18)
    return jnp.clip(raised(array, jax.random.fold_in(rng, 3), *heavy), -bound, bound).astype(dtype)


def setup_inputs(seed: int = 0) -> dict:
    streams_of = jax.random.split(jax.random.key(seed), 14)
    inputs = bell_draw_with(streams_of[0], (SEQ, LATENTS, D), 1.0, 6.0, ((0, 4), (1, 8)), (1, 2, 8, 2.0))
    conditioning = bell_draw(streams_of[1], (LATENTS, D), 1.0, 6.0, ((0, 8),))
    ada_weight = bell_draw(streams_of[2], (D, 6 * D), D ** -0.5, 0.21875, ((0, 8),))
    ada_bias = bell_draw(streams_of[3], (6 * D,), 0.5, 3.0, ((0, 8),))
    query_key_value_weight = bell_draw(streams_of[4], (D, 3, D), D ** -0.5, 0.21875, ((0, 8), (2, 4)))
    qv_bias = bell_draw(streams_of[5], (2, D), 0.5, 3.0, ((1, 8),))
    attention_output_weight = bell_draw(streams_of[6], (D, D), (D // 16) ** -0.5, 0.875, ((0, 4), (1, 8)))
    attention_output_bias = bell_draw(streams_of[7], (D,), 0.5, 3.0, ((0, 8),))
    expand_weight = bell_draw(streams_of[8], (D, FF), D ** -0.5, 0.21875, ((0, 8), (1, 4)))
    hidden_layer_bias = bell_draw(streams_of[9], (FF,), 0.5, 3.0, ((0, 8),))
    contract_weight = bell_draw(streams_of[10], (FF, D), FF ** -0.5, 0.109375, ((0, 4), (1, 8)))
    contract_bias = bell_draw(streams_of[11], (D,), 0.5, 3.0, ((0, 8),))
    out_cotangent = bell_draw_with(streams_of[12], (SEQ, LATENTS, D), 1.0, 6.0, ((0, 4), (1, 8)), (1, 2, 8, 2.0))
    return dict(inputs=inputs, conditioning=conditioning, ada_weight=ada_weight, ada_bias=ada_bias, query_key_value_weight=query_key_value_weight, qv_bias=qv_bias, attention_output_weight=attention_output_weight, attention_output_bias=attention_output_bias, expand_weight=expand_weight, hidden_layer_bias=hidden_layer_bias, contract_weight=contract_weight, contract_bias=contract_bias, out_cotangent=out_cotangent)


EPS = 1e-06
PRECISE_MODE = lax.Precision.HIGHEST

@jax.custom_vjp
def low(v):
    return lax.optimization_barrier(v.astype(jnp.bfloat16)).astype(jnp.float32)

@jax.custom_vjp
def reduced_backward(v):
    return v

def low_keep(v):
    return (low(v), None)

def low_pass(kept, grad):
    return (grad,)

def back_keep(v):
    return (v, None)

def back_low(kept, grad):
    return (low(grad),)
low.defvjp(low_keep, low_pass)
reduced_backward.defvjp(back_keep, back_low)

def layer_norm(values_in):
    average = lax.optimization_barrier(jnp.mean(values_in, axis=-1, keepdims=True))
    centered = values_in - average
    variance = lax.optimization_barrier(jnp.mean(centered * centered, axis=-1, keepdims=True))
    return centered * lax.rsqrt(variance + EPS)

def group_block(params, group_in, group_mod):
    query_key_value_weight, qv_bias, attention_output_weight, attention_output_bias, expand_weight, hidden_layer_bias, contract_weight, contract_bias = params
    shift_attn, scale_attn, gate_attn = (group_mod[:, 0], group_mod[:, 1], group_mod[:, 2])
    shift_mlp, scale_mlp, gate_mlp = (group_mod[:, 3], group_mod[:, 4], group_mod[:, 5])
    positions = group_in.shape[0]
    latents = group_in.shape[1]
    attention_normed_input = low(layer_norm(group_in) * (1.0 + scale_attn) + shift_attn)
    attention_projected = jnp.einsum('fqt,tbj->bfqj', attention_normed_input, query_key_value_weight, precision=PRECISE_MODE)
    queries = reduced_backward(low(attention_projected[0] + qv_bias[0])).reshape(positions, latents, HEADS, HEAD)
    key_rows = reduced_backward(low(attention_projected[1])).reshape(positions, latents, HEADS, HEAD)
    value_rows = reduced_backward(low(attention_projected[2] + qv_bias[1])).reshape(positions, latents, HEADS, HEAD)
    scores = reduced_backward(jnp.einsum('slhe,tlhe->lhst', queries, key_rows, precision=PRECISE_MODE) * (1.0 / math.sqrt(HEAD)))
    probabilities = jax.nn.softmax(scores, axis=-1)
    attention_mixed = jnp.einsum('lhst,tlhe->slhe', low(probabilities), value_rows, precision=PRECISE_MODE)
    attention_mixed = reduced_backward(low(attention_mixed.reshape(positions, latents, D)))
    attention_residual_path = reduced_backward(jnp.einsum('nbv,vr->nbr', attention_mixed, attention_output_weight, precision=PRECISE_MODE) + attention_output_bias)
    middle = group_in + gate_attn * attention_residual_path
    perceptron_normed_input = low(layer_norm(middle) * (1.0 + scale_mlp) + shift_mlp)
    hidden_preactivation = reduced_backward(jnp.einsum('wqg,gi->wqi', perceptron_normed_input, expand_weight, precision=PRECISE_MODE) + hidden_layer_bias)
    hidden_activated = low(jax.nn.gelu(hidden_preactivation, approximate=True))
    perceptron_residual_path = reduced_backward(jnp.einsum('zra,au->zru', hidden_activated, contract_weight, precision=PRECISE_MODE) + contract_bias)
    return middle + gate_mlp * perceptron_residual_path

def forward(inputs, conditioning, ada_weight, ada_bias, query_key_value_weight, qv_bias, attention_output_weight, attention_output_bias, expand_weight, hidden_layer_bias, contract_weight, contract_bias):
    cond_act = low(jax.nn.silu(conditioning))
    modulation = reduced_backward(jnp.dot(cond_act, ada_weight, precision=PRECISE_MODE)) + ada_bias
    groups = LATENTS // LAT_DEV
    group_mods = modulation.reshape(groups, LAT_DEV, 6, D)
    group_inputs = inputs.reshape(SEQ, groups, LAT_DEV, D).transpose(1, 0, 2, 3)
    params = (query_key_value_weight, qv_bias, attention_output_weight, attention_output_bias, expand_weight, hidden_layer_bias, contract_weight, contract_bias)

    def run_group(paired):
        return group_block(params, paired[0], paired[1])
    results = lax.map(jax.checkpoint(run_group), (group_inputs, group_mods))
    return results.transpose(1, 0, 2, 3).reshape(SEQ, LATENTS, D)

def reference(inputs, conditioning, ada_weight, ada_bias, query_key_value_weight, qv_bias, attention_output_weight, attention_output_bias, expand_weight, hidden_layer_bias, contract_weight, contract_bias, out_cotangent):
    output, pullback = jax.vjp(forward, inputs.astype(jnp.float32), conditioning.astype(jnp.float32), ada_weight.astype(jnp.float32), ada_bias.astype(jnp.float32), query_key_value_weight.astype(jnp.float32), qv_bias.astype(jnp.float32), attention_output_weight.astype(jnp.float32), attention_output_bias.astype(jnp.float32), expand_weight.astype(jnp.float32), hidden_layer_bias.astype(jnp.float32), contract_weight.astype(jnp.float32), contract_bias.astype(jnp.float32))
    grads = pullback(out_cotangent.astype(jnp.float32))
    return (output.astype(jnp.bfloat16), grads[0], grads[1], grads[2], grads[3], grads[4], grads[5], grads[6], grads[7], grads[8], grads[9], grads[10], grads[11])
```

```python
import functools
import math

import jax
import jax.numpy as jnp
from jax import lax
from jax.experimental import pallas as pl
from jax.experimental.pallas import tpu as pltpu
from jax.sharding import PartitionSpec as P

HEAD = 64
EPS = 1e-06
BF = jnp.bfloat16
F32 = jnp.float32
VMEM_LIMIT = 48 * 1024 * 1024


def layer_norm(values_in):
    average = jnp.mean(values_in, axis=-1, keepdims=True)
    centered = values_in - average
    variance = jnp.mean(centered * centered, axis=-1, keepdims=True)
    return centered * lax.rsqrt(variance + EPS)


def modulate(values_in, shifts, scales):
    return layer_norm(values_in) * (1.0 + scales) + shifts


def gelu_tanh(values_in):
    return jax.nn.gelu(values_in, approximate=True)


def swap(block, axis, offset):
    count = lax.axis_size(axis)
    return lax.ppermute(block, axis, [(i, i ^ offset) for i in range(count)])


def digits(count):
    bits = count.bit_length() - 1
    found, stride = [], 1
    if bits % 2:
        found.append((1, 2))
        stride = 2
    while stride < count:
        found.append((stride, 4))
        stride *= 4
    return found


def gather_blocks(own):
    count = lax.axis_size("fsdp")
    blocks = {0: own}
    for stride, radix in reversed(digits(count)):
        known = sorted(blocks)
        if len(known) > 4:
            stacked = jnp.stack([blocks[k] for k in known])
            for d in range(1, radix):
                moved = swap(stacked, "fsdp", d * stride)
                for place, k in enumerate(known):
                    blocks[k ^ (d * stride)] = moved[place]
        else:
            for d in range(1, radix):
                for k in known:
                    blocks[k ^ (d * stride)] = swap(blocks[k], "fsdp", d * stride)
    return [blocks[k] for k in range(count)]


def assemble_kernel(rank_ref, *refs):
    out_ref = refs[-1]
    rank = rank_ref[0]
    for k, block in enumerate(refs[:-1]):
        rows = block.shape[0]
        place = jnp.bitwise_xor(rank, k) * rows
        out_ref[pl.ds(pl.multiple_of(place, rows), rows), :] = block[...]


def assemble(blocks, rank):
    rows, cols = blocks[0].shape
    count = len(blocks)
    if rows % 16:
        order = jnp.bitwise_xor(jnp.arange(count), rank)
        return jnp.take(jnp.stack(blocks), order, axis=0).reshape(count * rows, cols)
    return pl.pallas_call(
        assemble_kernel,
        out_shape=jax.ShapeDtypeStruct((count * rows, cols), blocks[0].dtype),
        in_specs=[pl.BlockSpec(memory_space=pltpu.SMEM)]
        + [pl.BlockSpec(memory_space=pltpu.VMEM)] * count,
        out_specs=pl.BlockSpec(memory_space=pltpu.VMEM),
        compiler_params=pltpu.CompilerParams(vmem_limit_bytes=VMEM_LIMIT),
        name="assemble",
    )(rank.reshape(1).astype(jnp.int32), *blocks)


def weight_grad_kernel(rank_ref, left_ref, right_ref, out_ref):
    rank = rank_ref[0]
    count, rows, cols = out_ref.shape
    for at in range(0, cols, 256):
        product = lax.dot_general(
            left_ref[...],
            right_ref[:, at : at + 256],
            (((0,), (0,)), ((), ())),
            preferred_element_type=F32,
        ).astype(BF)
        for k in range(count):
            out_ref[jnp.bitwise_xor(rank, k), :, at : at + 256] = product[
                k * rows : (k + 1) * rows
            ]


def weight_grad(left, right, rank, count):
    rows = left.shape[1] // count
    cols = right.shape[1]
    if rows % 16:
        whole = jnp.dot(left.T, right, preferred_element_type=F32).astype(BF)
        order = jnp.bitwise_xor(jnp.arange(count), rank)
        return jnp.take(whole.reshape(count, rows, cols), order, axis=0)
    return pl.pallas_call(
        weight_grad_kernel,
        out_shape=jax.ShapeDtypeStruct((count, rows, cols), BF),
        in_specs=[
            pl.BlockSpec(memory_space=pltpu.SMEM),
            pl.BlockSpec(memory_space=pltpu.VMEM),
            pl.BlockSpec(memory_space=pltpu.VMEM),
        ],
        out_specs=pl.BlockSpec(memory_space=pltpu.VMEM),
        compiler_params=pltpu.CompilerParams(vmem_limit_bytes=VMEM_LIMIT),
        name="weight_grad",
    )(rank.reshape(1).astype(jnp.int32), left, right)


def scatter_blocks(parts):
    count = lax.axis_size("fsdp")
    blocks = {k: parts[k] for k in range(count)}
    stages = digits(count)
    for at, (stride, radix) in enumerate(stages):
        kept = [k for k in sorted(blocks) if (k // stride) % radix == 0]
        arrived = {k: [] for k in kept}
        if len(kept) > 4:
            for d in range(1, radix):
                sent = jnp.stack([blocks[k ^ (d * stride)] for k in kept])
                got = swap(sent, "fsdp", d * stride)
                for place, k in enumerate(kept):
                    arrived[k].append(got[place])
        else:
            for k in reversed(kept):
                for d in range(1, radix):
                    arrived[k].append(swap(blocks[k ^ (d * stride)], "fsdp", d * stride))
        last = at == len(stages) - 1
        summed = {}
        for k in kept:
            total = blocks[k].astype(F32)
            for part in arrived[k]:
                total = total + part.astype(F32)
            summed[k] = total if last else total.astype(BF)
        blocks = summed
    return blocks[0]


def tp_gather(rows):
    count = lax.axis_size("tp")
    return jnp.concatenate([rows] + [swap(rows, "tp", d) for d in range(1, count)], axis=1)


def tp_scatter(partial, positions):
    count = lax.axis_size("tp")
    total = partial[:, :positions].astype(F32)
    for d in range(1, count):
        total = total + swap(
            partial[:, d * positions : (d + 1) * positions], "tp", d
        ).astype(F32)
    return total


def shards(
    inputs,
    conditioning,
    ada_weight,
    ada_bias,
    query_key_value_weight,
    qv_bias,
    attention_output_weight,
    attention_output_bias,
    expand_weight,
    hidden_layer_bias,
    contract_weight,
    contract_bias,
    out_cotangent,
):
    tp_rank = lax.axis_index("tp")
    tp_count = lax.axis_size("tp")
    rank = lax.axis_index("fsdp")
    count = lax.axis_size("fsdp")
    positions, latents, width = inputs.shape
    feat = ada_weight.shape[0]
    head_cols = query_key_value_weight.shape[2]
    heads = head_cols // HEAD
    hidden_cols = expand_weight.shape[1]
    hidden_part = hidden_layer_bias.shape[0]
    mod_part = ada_bias.shape[0]

    attn_own = jnp.concatenate(
        [query_key_value_weight.reshape(feat, 3 * head_cols), attention_output_weight.T], axis=1
    )
    contract_own = contract_weight.T

    cond_float = conditioning.astype(F32)
    cond_low = jax.nn.silu(cond_float).astype(BF)
    bias_own = jnp.concatenate(
        [qv_bias.reshape(-1), attention_output_bias, hidden_layer_bias, contract_bias]
    )
    cond_sent = cond_low.reshape(latents, count, feat).transpose(1, 0, 2)
    sent = jnp.concatenate(
        [
            cond_sent.reshape(count, latents * feat),
            jnp.broadcast_to(bias_own[None], (count, bias_own.shape[0])),
        ],
        axis=1,
    )
    got = lax.all_to_all(sent, "fsdp", split_axis=0, concat_axis=0, tiled=True)
    cond_cols = got[:, : latents * feat].reshape(count * latents, feat)
    bias_all = got[:, latents * feat :].astype(F32)
    at = 2 * feat
    qv_all = bias_all[:, :at].reshape(count, 2, feat).transpose(1, 0, 2).reshape(2, width)
    proj_shift = bias_all[:, at : at + feat].reshape(width)
    fc1_shift = bias_all[:, at + feat : at + feat + hidden_part].reshape(-1)
    fc2_shift = bias_all[:, at + feat + hidden_part :].reshape(width)
    query_bias = lax.dynamic_slice_in_dim(qv_all[0], tp_rank * head_cols, head_cols, 0)
    value_bias = lax.dynamic_slice_in_dim(qv_all[1], tp_rank * head_cols, head_cols, 0)
    hidden_bias = lax.dynamic_slice_in_dim(fc1_shift, tp_rank * hidden_cols, hidden_cols, 0)

    mod_partial = jnp.dot(cond_cols, ada_weight, preferred_element_type=F32)
    bias_row = lax.dynamic_update_slice(
        jnp.zeros((mod_part * count,), F32), ada_bias.astype(F32), (rank * mod_part,)
    )
    mod_partial = mod_partial + bias_row
    mod_got = lax.all_to_all(mod_partial, "fsdp", split_axis=0, concat_axis=0, tiled=True)
    modulation = jnp.sum(mod_got.reshape(count, latents, 6, 1, width), axis=0)
    shift_attn, scale_attn, gate_attn = (modulation[:, 0], modulation[:, 1], modulation[:, 2])
    shift_mlp, scale_mlp, gate_mlp = (modulation[:, 3], modulation[:, 4], modulation[:, 5])

    attn_blocks = gather_blocks(attn_own)
    first_blocks = gather_blocks(expand_weight)
    second_blocks = gather_blocks(contract_own)

    residual_in = inputs.transpose(1, 0, 2).astype(F32)
    cotangent = out_cotangent.transpose(1, 0, 2).astype(F32)
    tokens = latents * positions * tp_count

    attn_in = modulate(residual_in, shift_attn, scale_attn).astype(BF)
    grad_mlp = (cotangent * gate_mlp).astype(BF)
    attn_rows = tp_gather(attn_in)
    grad_mlp_rows = tp_gather(grad_mlp)
    attn_full = assemble(attn_blocks, rank)
    qkv_full = attn_full[:, : 3 * head_cols]
    proj_full = attn_full[:, 3 * head_cols :]
    projected = jnp.dot(
        attn_rows.reshape(tokens, width), qkv_full, preferred_element_type=F32
    )
    split = (latents, positions * tp_count, heads, HEAD)
    queries = (projected[:, :head_cols] + query_bias).astype(BF).reshape(split)
    keys = projected[:, head_cols : 2 * head_cols].astype(BF).reshape(split)
    values = (projected[:, 2 * head_cols :] + value_bias).astype(BF).reshape(split)
    factor = 1.0 / math.sqrt(HEAD)
    scores = jnp.einsum("lshe,lthe->lhst", queries, keys, preferred_element_type=F32) * factor
    top = jnp.max(scores, axis=-1, keepdims=True)
    weights = jnp.exp(scores - top)
    probs = weights / jnp.sum(weights, axis=-1, keepdims=True)
    probs_low = probs.astype(BF)
    attended = (
        jnp.einsum("lhst,lthe->lshe", probs_low, values, preferred_element_type=F32)
        .astype(BF)
        .reshape(tokens, head_cols)
    )
    attn_partial = lax.dot_general(
        attended, proj_full, (((1,), (1,)), ((), ())), preferred_element_type=F32
    ).astype(BF)
    attn_branch = (
        tp_scatter(attn_partial.reshape(latents, -1, width), positions) + proj_shift
    )
    middle = residual_in + gate_attn * attn_branch
    mlp_in = modulate(middle, shift_mlp, scale_mlp).astype(BF)
    mlp_rows = tp_gather(mlp_in).reshape(tokens, width)
    grad_rows = grad_mlp_rows.reshape(tokens, width)
    first_full = assemble(first_blocks, rank)
    second_full = assemble(second_blocks, rank)
    hidden_pre = jnp.dot(mlp_rows, first_full, preferred_element_type=F32) + hidden_bias
    hidden_act = gelu_tanh(hidden_pre).astype(BF)
    act_grad = jnp.dot(grad_rows, second_full, preferred_element_type=F32)
    grad_pre = jax.vjp(gelu_tanh, hidden_pre)[1](act_grad)[0].astype(BF)
    grad_in_partial = lax.dot_general(
        grad_pre, first_full, (((1,), (1,)), ((), ())), preferred_element_type=F32
    ).astype(BF)
    grad_mlp_input = tp_scatter(grad_in_partial.reshape(latents, -1, width), positions)
    mlp_partial = lax.dot_general(
        hidden_act, second_full, (((1,), (1,)), ((), ())), preferred_element_type=F32
    ).astype(BF)
    mlp_branch = tp_scatter(mlp_partial.reshape(latents, -1, width), positions) + fc2_shift
    output = (middle + gate_mlp * mlp_branch).astype(BF)

    second_grad = weight_grad(grad_rows, hidden_act, rank, count)
    first_grad = weight_grad(mlp_rows, grad_pre, rank, count)

    grad_gate_mlp = jnp.sum(cotangent * mlp_branch, axis=1)
    grad_fc2_bias = jnp.sum(grad_mlp.astype(F32), axis=(0, 1))
    grad_fc1_bias = jnp.sum(grad_pre.astype(F32), axis=0)

    grad_middle_norm, grad_shift_mlp, grad_scale_mlp = jax.vjp(
        modulate, middle, shift_mlp, scale_mlp
    )[1](grad_mlp_input)
    grad_middle = cotangent + grad_middle_norm
    grad_gate_attn = jnp.sum(grad_middle * attn_branch, axis=1)
    grad_attn = (grad_middle * gate_attn).astype(BF)
    grad_proj_bias = jnp.sum(grad_attn.astype(F32), axis=(0, 1))
    grad_attn_rows = tp_gather(grad_attn).reshape(tokens, width)
    grad_attended = (
        jnp.dot(grad_attn_rows, proj_full, preferred_element_type=F32).astype(BF).reshape(split)
    )
    grad_values = jnp.einsum(
        "lhst,lshe->lthe", probs_low, grad_attended, preferred_element_type=F32
    )
    grad_probs = jnp.einsum("lshe,lthe->lhst", grad_attended, values, preferred_element_type=F32)
    grad_scores = (
        probs * (grad_probs - jnp.sum(probs * grad_probs, axis=-1, keepdims=True))
    ).astype(BF)
    grad_queries = (
        jnp.einsum("lhst,lthe->lshe", grad_scores, keys, preferred_element_type=F32) * factor
    )
    grad_keys = (
        jnp.einsum("lhst,lshe->lthe", grad_scores, queries, preferred_element_type=F32) * factor
    )
    grad_qkv = jnp.concatenate(
        [
            part.astype(BF).reshape(tokens, head_cols)
            for part in (grad_queries, grad_keys, grad_values)
        ],
        axis=1,
    )
    grad_in_partial = lax.dot_general(
        grad_qkv, qkv_full, (((1,), (1,)), ((), ())), preferred_element_type=F32
    ).astype(BF)
    grad_attn_input = tp_scatter(grad_in_partial.reshape(latents, -1, width), positions)
    qkv_grad = weight_grad(attn_rows.reshape(tokens, width), grad_qkv, rank, count)
    proj_grad = weight_grad(grad_attn_rows, attended, rank, count)
    grad_qv = jnp.sum(grad_qkv.astype(F32), axis=0)

    grad_input_norm, grad_shift_attn, grad_scale_attn = jax.vjp(
        modulate, residual_in, shift_attn, scale_attn
    )[1](grad_attn_input)
    inputs_grad = grad_middle + grad_input_norm

    grad_mod_own = jnp.stack(
        [
            grad_shift_attn.reshape(latents, width),
            grad_scale_attn.reshape(latents, width),
            grad_gate_attn,
            grad_shift_mlp.reshape(latents, width),
            grad_scale_mlp.reshape(latents, width),
            grad_gate_mlp,
        ],
        axis=1,
    ).reshape(latents, 6 * width)
    zero = jnp.zeros((), jnp.int32)
    grad_qv_own = lax.dynamic_update_slice(
        jnp.zeros((2, width), F32),
        jnp.stack([grad_qv[:head_cols], grad_qv[2 * head_cols :]]),
        (zero, tp_rank * head_cols),
    )
    grad_fc1_own = lax.dynamic_update_slice(
        jnp.zeros((hidden_cols * tp_count,), F32), grad_fc1_bias, (tp_rank * hidden_cols,)
    )
    packed = jnp.concatenate(
        [
            grad_mod_own.reshape(-1),
            grad_qv_own.reshape(-1),
            grad_proj_bias,
            grad_fc1_own,
            grad_fc2_bias,
        ]
    ).astype(BF)
    packed_total = packed.astype(F32)
    for d in range(1, tp_count):
        packed_total = packed_total + swap(packed, "tp", d).astype(F32)
    mods = latents * 6 * width
    grad_mod_low = packed_total[:mods].astype(BF)
    rest = packed_total[mods:]
    qv_sum = rest[: 2 * width].reshape(2, count, feat).transpose(1, 0, 2).reshape(count, -1)
    proj_sum = rest[2 * width : 3 * width].reshape(count, feat)
    fc1_sum = rest[3 * width : 3 * width + hidden_cols * tp_count].reshape(count, hidden_part)
    fc2_sum = rest[3 * width + hidden_cols * tp_count :].reshape(count, feat)
    sent = jnp.concatenate(
        [
            jnp.broadcast_to(grad_mod_low[None], (count, mods)),
            jnp.concatenate([qv_sum, proj_sum, fc1_sum, fc2_sum], axis=1).astype(BF),
        ],
        axis=1,
    )
    got = lax.all_to_all(sent, "fsdp", split_axis=0, concat_axis=0, tiled=True)
    grad_mod_all = got[:, :mods].reshape(count * latents, 6 * width)
    bias_grads = jnp.sum(got[:, mods:].astype(F32), axis=0)
    qv_bias_grad = bias_grads[: 2 * feat].reshape(2, feat)
    proj_bias_grad = bias_grads[2 * feat : 3 * feat]
    fc1_bias_grad = bias_grads[3 * feat : 3 * feat + hidden_part]
    fc2_bias_grad = bias_grads[3 * feat + hidden_part :]
    ada_bias_grad = jnp.sum(
        lax.dynamic_slice_in_dim(grad_mod_all, rank * mod_part, mod_part, 1).astype(F32), axis=0
    )
    ada_weight_grad = lax.dot_general(
        cond_cols, grad_mod_all, (((0,), (0,)), ((), ())), preferred_element_type=F32
    )
    silu_cols = lax.dot_general(
        grad_mod_all, ada_weight, (((1,), (1,)), ((), ())), preferred_element_type=F32
    )
    silu_got = lax.all_to_all(
        silu_cols.reshape(count, latents, feat), "fsdp", split_axis=0, concat_axis=0, tiled=True
    )
    silu_grad = silu_got.transpose(1, 0, 2).reshape(latents, width)
    cond_grad = jax.vjp(jax.nn.silu, cond_float)[1](silu_grad)[0]

    second_sum = scatter_blocks(second_grad)
    first_sum = scatter_blocks(first_grad)
    attn_sum = scatter_blocks(jnp.concatenate([qkv_grad, proj_grad], axis=2))
    return (
        output.transpose(1, 0, 2),
        inputs_grad.transpose(1, 0, 2),
        cond_grad,
        ada_weight_grad,
        ada_bias_grad,
        attn_sum[:, : 3 * head_cols].reshape(feat, 3, head_cols),
        qv_bias_grad,
        attn_sum[:, 3 * head_cols :].T,
        proj_bias_grad,
        first_sum,
        fc1_bias_grad,
        second_sum.T,
        fc2_bias_grad,
    )


def solution(mesh):
    return jax.shard_map(
        shards,
        mesh=mesh,
        in_specs=(
            P("tp", "fsdp", None),
            P("fsdp", None),
            P("fsdp", None),
            P("fsdp"),
            P("fsdp", None, "tp"),
            P(None, "fsdp"),
            P("tp", "fsdp"),
            P("fsdp"),
            P("fsdp", "tp"),
            P("fsdp"),
            P("tp", "fsdp"),
            P("fsdp"),
            P("tp", "fsdp", None),
        ),
        out_specs=(
            P("tp", "fsdp", None),
            P("tp", "fsdp", None),
            P("fsdp", None),
            P("fsdp", None),
            P("fsdp"),
            P("fsdp", None, "tp"),
            P(None, "fsdp"),
            P("tp", "fsdp"),
            P("fsdp"),
            P("fsdp", "tp"),
            P("fsdp"),
            P("tp", "fsdp"),
            P("fsdp"),
        ),
        check_vma=False,
    )
```

```python
import functools
import math

import jax
import jax.numpy as jnp
from jax import lax
from jax.experimental import pallas as pl
from jax.experimental.pallas import tpu as pltpu
from jax.sharding import PartitionSpec as P

HEAD = 64
EPS = 1e-06
BF = jnp.bfloat16
F32 = jnp.float32
FACTOR = 1.0 / math.sqrt(HEAD)
CURVE = math.sqrt(2.0 / math.pi)
CUBIC = 0.044715


def call(kernel, name, outs, args, scalars=(), scratch=(), flops=0, ordered=()):
    in_specs = (
        [pl.BlockSpec(memory_space=pltpu.SMEM)] * len(scalars)
        + [pl.BlockSpec(memory_space=pl.ANY)] * len(ordered)
        + [pl.BlockSpec(memory_space=pltpu.VMEM)] * len(args)
    )
    skip = len(scalars)

    def body(*refs):
        kernel(*refs[:skip], *refs[skip + len(ordered) :])

    shapes = [jax.ShapeDtypeStruct(shape, dtype) for shape, dtype in outs]
    moved = sum(math.prod(a.shape) * a.dtype.itemsize for a in args)
    moved += sum(math.prod(s.shape) * s.dtype.itemsize for s in shapes)
    return pl.pallas_call(
        body,
        out_shape=shapes,
        in_specs=in_specs,
        out_specs=[pl.BlockSpec(memory_space=pltpu.VMEM)] * len(outs),
        scratch_shapes=list(scratch),
        compiler_params=pltpu.CompilerParams(vmem_limit_bytes=24 * 1024 * 1024),
        cost_estimate=pl.CostEstimate(
            flops=int(flops), bytes_accessed=int(moved), transcendentals=0
        ),
        name=name,
    )(*[s.reshape(1).astype(jnp.int32) for s in scalars], *ordered, *args)


def dot(a, b, over=(1, 0)):
    return lax.dot_general(
        a, b, (((over[0],), (over[1],)), ((), ())), preferred_element_type=F32
    )


def normed(v):
    centered = v - jnp.mean(v, axis=-1, keepdims=True)
    scale = lax.rsqrt(jnp.mean(centered * centered, axis=-1, keepdims=True) + EPS)
    return centered * scale, scale


def norm_back(n, scale, grad):
    mean = jnp.mean(grad, axis=-1, keepdims=True)
    along = jnp.mean(grad * n, axis=-1, keepdims=True)
    return (grad - mean - n * along) * scale


def swap(block, axis, offset):
    count = lax.axis_size(axis)
    return lax.ppermute(block, axis, [(i, i ^ offset) for i in range(count)])


def tp_gather(rows):
    far = swap(rows, "tp", 2)
    near = swap(rows, "tp", 1)
    return [rows, near, far, swap(far, "tp", 1)]


def tp_scatter(parts):
    return [parts[0], swap(parts[2], "tp", 2), swap(parts[3], "tp", 3), swap(parts[1], "tp", 1)]


def pack_kernel(cond, qv, proj, second, hidden, out):
    count = out.shape[0]
    feat = qv.shape[1]
    latents = cond.shape[0]
    out[...] = jnp.zeros_like(out)
    value = cond[...].astype(F32)
    act = (value / (1.0 + jnp.exp(-value))).astype(BF).astype(F32)
    rows = [qv[...], proj[...], second[...], hidden[...]]
    for k in range(count):
        out[k, 0:latents, 0:feat] = act[:, k * feat : (k + 1) * feat]
        at = latents
        for row in rows:
            out[k, at : at + row.shape[0], 0:feat] = row.astype(F32)
            at += row.shape[0]


def mod_kernel(got, ada, bias, out, cols_out, scr):
    count, latents, _ = out.shape
    feat = ada.shape[0]
    for f in range(count):
        scr[f * latents : (f + 1) * latents, :] = got[f, 0:latents, :]
    cols = scr[:, 0:feat].astype(BF)
    cols_out[...] = cols
    width = ada.shape[1] // 6
    for j in range(6):
        at = slice(j * width, (j + 1) * width)
        part = dot(cols, ada[:, at]) + bias[:, at]
        for f in range(count):
            out[f, :, at] = part[f * latents : (f + 1) * latents]


def bias_kernel(tp_rank, got, qkv_out, proj_out, second_out, hidden_out, *, latents, feat, tp):
    count = got.shape[0]
    per = count // tp
    first = tp_rank[0] * per
    cols = per * feat
    qkv_out[...] = jnp.zeros_like(qkv_out)
    at = latents
    for i in range(per):
        f = first + i
        here = slice(i * feat, (i + 1) * feat)
        qkv_out[0:1, here] = got[f, at : at + 1, 0:feat]
        qkv_out[0:1, 2 * cols + i * feat : 2 * cols + (i + 1) * feat] = got[
            f, at + 1 : at + 2, 0:feat
        ]
        for r in range(tp):
            lane = (i * tp + r) * feat
            hidden_out[0:1, lane : lane + feat] = got[f, at + 4 + r : at + 5 + r, 0:feat]
    for f in range(count):
        here = slice(f * feat, (f + 1) * feat)
        proj_out[0:1, here] = got[f, at + 2 : at + 3, 0:feat]
        second_out[0:1, here] = got[f, at + 3 : at + 4, 0:feat]


def assemble_kernel(rank, *refs):
    *blocks, qkv_out, proj_out = refs
    cut = qkv_out.shape[1]
    for k, block in enumerate(blocks):
        rows = block.shape[0]
        at = pl.ds(pl.multiple_of(jnp.bitwise_xor(rank[0], k) * rows, rows), rows)
        qkv_out[at, :] = block[:, :cut]
        proj_out[at, :] = block[:, cut:]


def first_norm_kernel(got, x, mod_out, out):
    mod = got[0]
    for f in range(1, got.shape[0]):
        mod = mod + got[f]
    mod_out[...] = mod
    latents = mod.shape[0]
    width = x.shape[1]
    rows = x.shape[0] // latents
    for l in range(latents):
        here = slice(l * rows, (l + 1) * rows)
        n, _ = normed(x[here, :].astype(F32))
        shift, scale = mod[l : l + 1, :width], mod[l : l + 1, width : 2 * width]
        out[here, :] = (n * (1.0 + scale) + shift).astype(BF)


def gate_grad_kernel(cot, mod, out, bias_out):
    latents = mod.shape[0]
    width = cot.shape[1]
    rows = cot.shape[0] // latents
    total = jnp.zeros((1, width), F32)
    for l in range(latents):
        here = slice(l * rows, (l + 1) * rows)
        value = (cot[here, :].astype(F32) * mod[l : l + 1, 5 * width :]).astype(BF)
        out[here, :] = value
        total = total + jnp.sum(value.astype(F32), axis=0, keepdims=True)
    bias_out[...] = total


def unpack_rows(blocks, rows, latents):
    part = blocks[0].shape[0] // latents
    whole = part * len(blocks)
    for b, block in enumerate(blocks):
        for l in range(latents):
            rows[l * whole + b * part : l * whole + (b + 1) * part, :] = block[
                l * part : (l + 1) * part, :
            ]


def put_parts(value, parts, latent):
    part = value.shape[0] // len(parts)
    for b, out in enumerate(parts):
        out[latent * part : (latent + 1) * part, :] = value[b * part : (b + 1) * part]


def softmax(q, k):
    scores = dot(q, k, (1, 1)) * FACTOR
    weights = jnp.exp(scores - jnp.max(scores, axis=-1, keepdims=True))
    return weights * (1.0 / jnp.sum(weights, axis=-1, keepdims=True))


def attn_kernel(x0, x1, x2, x3, qkv_w, proj_w, bias, rows, qkv, att, p0, p1, p2, p3, *, latents):
    unpack_rows([x0, x1, x2, x3], rows, latents)
    cols = proj_w.shape[1]
    size = rows.shape[0] // latents
    for l in range(latents):
        here = slice(l * size, (l + 1) * size)
        projected = (dot(rows[here, :], qkv_w[...]) + bias[...]).astype(BF)
        qkv[here, :] = projected
        mixed = []
        for h in range(cols // HEAD):
            q, k, v = [
                projected[:, j * cols + h * HEAD : j * cols + (h + 1) * HEAD] for j in range(3)
            ]
            mixed.append(dot(softmax(q, k).astype(BF), v))
        attended = jnp.concatenate(mixed, axis=1).astype(BF)
        att[here, :] = attended
        put_parts(dot(attended, proj_w[...], (1, 1)).astype(BF), [p0, p1, p2, p3], l)


def middle_kernel(x, p0, p1, p2, p3, bias, mod, branch_out, middle_out, out):
    latents = mod.shape[0]
    width = x.shape[1]
    rows = x.shape[0] // latents
    for l in range(latents):
        here = slice(l * rows, (l + 1) * rows)
        branch = bias[...]
        for part in (p0, p1, p2, p3):
            branch = branch + part[here, :].astype(F32)
        branch_out[here, :] = branch
        gate = mod[l : l + 1, 2 * width : 3 * width]
        middle = x[here, :].astype(F32) + gate * branch
        middle_out[here, :] = middle
        n, _ = normed(middle)
        shift = mod[l : l + 1, 3 * width : 4 * width]
        scale = mod[l : l + 1, 4 * width : 5 * width]
        out[here, :] = (n * (1.0 + scale) + shift).astype(BF)


def mlp_kernel(
    x0, x1, x2, x3, g0, g1, g2, g3, both, bias, act_out, pre_out, p0, p1, p2, p3, *, hidden
):
    rows = x0.shape[0]
    for b, (x, g, part) in enumerate(zip((x0, x1, x2, x3), (g0, g1, g2, g3), (p0, p1, p2, p3))):
        here = slice(b * rows, (b + 1) * rows)
        v = dot(x[...], both[:, :hidden]) + bias[...]
        square = v * v
        t = jnp.tanh(CURVE * v * (1.0 + CUBIC * square))
        act_out[here, :] = (0.5 * v * (1.0 + t)).astype(BF)
        slope = 0.5 * (1.0 + t) + 0.5 * v * (1.0 - t * t) * CURVE * (1.0 + 3.0 * CUBIC * square)
        pre = (dot(g[...], both[:, hidden:]) * slope).astype(BF)
        pre_out[here, :] = pre
        part[...] = dot(pre, both[:, :hidden], (1, 1)).astype(BF)


def store_grad(rank, product, keep, send, cols):
    rows = keep.shape[1]
    place = rank[0] // 2
    for mine in range(2):

        @pl.when(rank[0] % 2 == mine)
        def _():
            for z in range(keep.shape[0]):
                to = jnp.bitwise_xor(place, z)
                keep[to, :, cols] = product[(2 * z + mine) * rows : (2 * z + mine + 1) * rows]
                send[to, :, cols] = product[
                    (2 * z + 1 - mine) * rows : (2 * z + 2 - mine) * rows
                ]


def mlp_grad_kernel(
    rank, x0, x1, x2, x3, g0, g1, g2, g3, act, pre, keep, send, bias_out, rows
):
    size = x0.shape[0]
    hidden = act.shape[1]
    for which, blocks in enumerate(((x0, x1, x2, x3), (g0, g1, g2, g3))):
        for b, block in enumerate(blocks):
            rows[b * size : (b + 1) * size, :] = block[...]
        for at in range(0, hidden, 256):
            right = (pre if which == 0 else act)[:, at : at + 256]
            product = dot(rows[...], right, (0, 0)).astype(BF)
            lane = which * hidden + at
            store_grad(rank, product, keep, send, slice(lane, lane + 256))
    bias_out[...] = jnp.sum(pre[...].astype(F32), axis=0, keepdims=True)


def mlp_out_kernel(act, both, p0, p1, p2, p3, *, hidden):
    rows = p0.shape[0]
    for b, part in enumerate((p0, p1, p2, p3)):
        part[...] = dot(act[b * rows : (b + 1) * rows, :], both[:, hidden:], (1, 1)).astype(BF)


def output_kernel(middle, cot, p0, p1, p2, p3, bias, mod, out, sums):
    latents = mod.shape[0]
    width = middle.shape[1]
    rows = middle.shape[0] // latents
    for l in range(latents):
        here = slice(l * rows, (l + 1) * rows)
        branch = bias[...]
        for part in (p0, p1, p2, p3):
            branch = branch + part[here, :].astype(F32)
        out[here, :] = (middle[here, :] + mod[l : l + 1, 5 * width :] * branch).astype(BF)
        sums[l : l + 1, :] = jnp.sum(cot[here, :].astype(F32) * branch, axis=0, keepdims=True)


def middle_back_kernel(cot, middle, branch, p0, p1, p2, p3, mod, grad_out, out, sums):
    latents = mod.shape[0]
    width = middle.shape[1]
    rows = middle.shape[0] // latents
    total = jnp.zeros((1, width), F32)
    for l in range(latents):
        here = slice(l * rows, (l + 1) * rows)
        grad = p0[here, :].astype(F32)
        for part in (p1, p2, p3):
            grad = grad + part[here, :].astype(F32)
        n, scale = normed(middle[here, :])
        sums[3 * l + 1 : 3 * l + 2, :] = jnp.sum(grad, axis=0, keepdims=True)
        sums[3 * l + 2 : 3 * l + 3, :] = jnp.sum(grad * n, axis=0, keepdims=True)
        factor = 1.0 + mod[l : l + 1, 4 * width : 5 * width]
        whole = cot[here, :].astype(F32) + norm_back(n, scale, grad * factor)
        grad_out[here, :] = whole
        sums[3 * l : 3 * l + 1, :] = jnp.sum(whole * branch[here, :], axis=0, keepdims=True)
        low = (whole * mod[l : l + 1, 2 * width : 3 * width]).astype(BF)
        out[here, :] = low
        total = total + jnp.sum(low.astype(F32), axis=0, keepdims=True)
    sums[3 * latents : 3 * latents + 1, :] = total


def attn_back_kernel(
    g0, g1, g2, g3, qkv_w, proj_w, qkv, rows, grads, p0, p1, p2, p3, *, latents
):
    unpack_rows([g0, g1, g2, g3], rows, latents)
    cols = proj_w.shape[1]
    size = rows.shape[0] // latents
    for l in range(latents):
        here = slice(l * size, (l + 1) * size)
        back = dot(rows[here, :], proj_w[...]).astype(BF)
        projected = qkv[here, :]
        found = [[], [], []]
        for h in range(cols // HEAD):
            q, k, v = [
                projected[:, j * cols + h * HEAD : j * cols + (h + 1) * HEAD] for j in range(3)
            ]
            up = back[:, h * HEAD : (h + 1) * HEAD]
            probs = softmax(q, k)
            grad_probs = dot(up, v, (1, 1))
            inner = jnp.sum(probs * grad_probs, axis=-1, keepdims=True)
            scores = (probs * (grad_probs - inner)).astype(BF)
            found[0].append(dot(scores, k) * FACTOR)
            found[1].append(dot(scores, q, (0, 0)) * FACTOR)
            found[2].append(dot(probs.astype(BF), up, (0, 0)))
        grad = jnp.concatenate(found[0] + found[1] + found[2], axis=1).astype(BF)
        grads[here, :] = grad
        put_parts(dot(grad, qkv_w[...], (1, 1)).astype(BF), [p0, p1, p2, p3], l)


def attn_grad_kernel(rank, rows, grads, back, att, keep, send, bias_out):
    cols = att.shape[1]
    for at in range(0, 3 * cols, cols):
        product = dot(rows[...], grads[:, at : at + cols], (0, 0)).astype(BF)
        store_grad(rank, product, keep, send, slice(at, at + cols))
    product = dot(back[...], att[...], (0, 0)).astype(BF)
    store_grad(rank, product, keep, send, slice(3 * cols, 4 * cols))
    bias_out[...] = jnp.sum(grads[...].astype(F32), axis=0, keepdims=True)


def input_back_kernel(
    x, grad_middle, p0, p1, p2, p3, mod, sums, gates, fc2, fc1, qkv, out, pack, scr
):
    latents = mod.shape[0]
    width = x.shape[1]
    rows = x.shape[0] // latents
    cols = qkv.shape[1] // 3
    scr[...] = jnp.zeros_like(scr)
    for l in range(latents):
        here = slice(l * rows, (l + 1) * rows)
        grad = p0[here, :].astype(F32)
        for part in (p1, p2, p3):
            grad = grad + part[here, :].astype(F32)
        n, scale = normed(x[here, :].astype(F32))
        scr[6 * l : 6 * l + 1, :] = jnp.sum(grad, axis=0, keepdims=True)
        scr[6 * l + 1 : 6 * l + 2, :] = jnp.sum(grad * n, axis=0, keepdims=True)
        scr[6 * l + 2 : 6 * l + 5, :] = sums[3 * l : 3 * l + 3, :]
        scr[6 * l + 5 : 6 * l + 6, :] = gates[l : l + 1, :]
        factor = 1.0 + mod[l : l + 1, width : 2 * width]
        out[here, :] = grad_middle[here, :] + norm_back(n, scale, grad * factor)
    at = 6 * latents
    scr[at : at + 1, :] = sums[3 * latents : 3 * latents + 1, :]
    scr[at + 1 : at + 2, :] = fc2[...]
    scr[at + 2 : at + 3, :] = fc1[...]
    scr[at + 3 : at + 4, 0:cols] = qkv[:, 0:cols]
    scr[at + 3 : at + 4, cols : 2 * cols] = qkv[:, 2 * cols :]
    pack[...] = scr[...].astype(BF)


def spread_kernel(tp_rank, k0, k1, k2, k3, out, parts, total, *, latents, feat):
    count = out.shape[0]
    packs = (k0, k1, k2, k3)
    per = count // len(packs)
    cols = per * feat
    mods = 6 * latents
    summed = jnp.zeros(k0.shape, F32)
    for d, pack in enumerate(packs):
        value = pack[...].astype(F32)
        parts[jnp.bitwise_xor(tp_rank[0], d)] = value
        summed = summed + value
    total[...] = summed
    for k in range(count):
        t, i = k // per, k % per
        here = slice(k * feat, (k + 1) * feat)
        row = slice(mods, mods + 1)
        total[row, :] = jnp.zeros((1, k0.shape[1]), F32)
        total[row, 0:feat] = parts[t, mods + 3 : mods + 4, i * feat : (i + 1) * feat]
        total[row, feat : 2 * feat] = parts[
            t, mods + 3 : mods + 4, cols + i * feat : cols + (i + 1) * feat
        ]
        total[row, 2 * feat : 3 * feat] = summed[mods : mods + 1, here]
        total[row, 3 * feat : 4 * feat] = summed[mods + 1 : mods + 2, here]
        total[row, 4 * feat : 8 * feat] = parts[
            t, mods + 2 : mods + 3, 4 * i * feat : 4 * (i + 1) * feat
        ]
        out[k] = total[...].astype(BF)


def scatter_two(keep, send):
    got = swap(send, "fsdp", 1)
    moved = [swap((keep[d].astype(F32) + got[d].astype(F32)).astype(BF), "fsdp", 2 * d) for d in range(1, keep.shape[0])]
    total = keep[0].astype(F32) + got[0].astype(F32)
    for part in moved:
        total = total + part.astype(F32)
    return total


def shards(
    inputs,
    conditioning,
    ada_weight,
    ada_bias,
    query_key_value_weight,
    qv_bias,
    attention_output_weight,
    attention_output_bias,
    expand_weight,
    hidden_layer_bias,
    contract_weight,
    contract_bias,
    out_cotangent,
):
    tp_rank = lax.axis_index("tp")
    tp_count = lax.axis_size("tp")
    rank = lax.axis_index("fsdp")
    count = lax.axis_size("fsdp")
    positions, latents, width = inputs.shape
    feat = ada_weight.shape[0]
    cols = query_key_value_weight.shape[2]
    hidden = expand_weight.shape[1]
    hidden_part = hidden_layer_bias.shape[0]
    mod_part = ada_bias.shape[0]
    rows = positions * latents
    tokens = rows * tp_count
    mods = 6 * latents
    direct = count == 8
    block = ((rows, width), BF)
    block_f32 = ((rows, width), F32)

    mlp_own = jnp.concatenate([expand_weight, contract_weight.T], axis=1)
    mlp_full = lax.all_gather(mlp_own, "fsdp", axis=0, tiled=True)
    attn_own = jnp.concatenate(
        [query_key_value_weight.reshape(feat, 3 * cols), attention_output_weight.T], axis=1
    )
    if direct:
        blocks = {0: attn_own}
        for d in (2, 4, 6):
            blocks[d] = swap(attn_own, "fsdp", d)
        for d in (0, 2, 4, 6):
            blocks[d + 1] = swap(blocks[d], "fsdp", 1)
        qkv_full, proj_full = call(
            assemble_kernel,
            "attn_weights",
            [((width, 3 * cols), BF), ((width, cols), BF)],
            [blocks[k] for k in range(count)],
            [rank],
        )
    else:
        attn_full = lax.all_gather(attn_own, "fsdp", axis=0, tiled=True)
        qkv_full, proj_full = attn_full[:, : 3 * cols], attn_full[:, 3 * cols :]

    sent = call(
        pack_kernel,
        "pack_conditioning",
        [((count, 16, 128), F32)],
        [
            conditioning,
            qv_bias,
            attention_output_bias.reshape(1, feat),
            contract_bias.reshape(1, feat),
            hidden_layer_bias.reshape(tp_count, feat),
        ],
    )[0]
    got = lax.all_to_all(sent, "fsdp", split_axis=0, concat_axis=0, tiled=True)
    bias_row = lax.dynamic_update_slice(
        jnp.zeros((1, mod_part * count), F32),
        ada_bias.astype(F32).reshape(1, mod_part),
        (0, rank * mod_part),
    )
    mod_partial, cond_cols = call(
        mod_kernel,
        "modulation",
        [((count, latents, 6 * width), F32), ((count * latents, feat), BF)],
        [got, ada_weight, bias_row],
        scratch=[pltpu.VMEM((count * latents, 128), F32)],
    )
    qkv_bias, proj_bias, second_bias, hidden_bias = call(
        functools.partial(bias_kernel, latents=latents, feat=feat, tp=tp_count),
        "biases",
        [((1, 3 * cols), F32), ((1, width), F32), ((1, width), F32), ((1, hidden), F32)],
        [got],
        [tp_rank],
    )
    mod_got = lax.all_to_all(mod_partial, "fsdp", split_axis=0, concat_axis=0, tiled=True)

    x = inputs.transpose(1, 0, 2).reshape(rows, width)
    cot = out_cotangent.transpose(1, 0, 2).reshape(rows, width)
    mod, attn_in = call(
        first_norm_kernel, "first_norm", [((latents, 6 * width), F32), block], [mod_got, x]
    )
    x_blocks = tp_gather(attn_in)
    grad_mlp, fc2_part = call(
        gate_grad_kernel,
        "gate_grad",
        [block, ((1, width), F32)],
        [cot, mod],
        ordered=[x_blocks[2]],
    )
    attn_rows, qkv, att, *parts = call(
        functools.partial(attn_kernel, latents=latents),
        "attention",
        [((tokens, width), BF), ((tokens, 3 * cols), BF), ((tokens, cols), BF)] + [block] * 4,
        [*x_blocks, qkv_full, proj_full, qkv_bias],
        flops=4.6e9,
    )
    g_blocks = tp_gather(grad_mlp)
    branch, middle, mlp_in = call(
        middle_kernel,
        "middle",
        [block_f32, block_f32, block],
        [x, *tp_scatter(parts), proj_bias, mod],
    )
    m_blocks = tp_gather(mlp_in)
    act, pre, *parts = call(
        functools.partial(mlp_kernel, hidden=hidden),
        "mlp",
        [((tokens, hidden), BF)] * 2 + [block] * 4,
        [*m_blocks, *g_blocks, mlp_full, hidden_bias],
        flops=4.0e9,
    )
    grad_in = tp_scatter(parts)
    if direct:
        mlp_keep, mlp_send, fc1_part = call(
            mlp_grad_kernel,
            "mlp_weight_grad",
            [((count // 2, feat, 2 * hidden), BF)] * 2 + [((1, hidden), F32)],
            [*m_blocks, *g_blocks, act, pre],
            [rank],
            scratch=[pltpu.VMEM((tokens, width), BF)],
            flops=2.4e9,
            ordered=[parts[3]],
        )
        mlp_sum = scatter_two(mlp_keep, mlp_send)
    else:
        mlp_grad = jnp.concatenate(
            [
                dot(jnp.concatenate(m_blocks), pre, (0, 0)),
                dot(jnp.concatenate(g_blocks), act, (0, 0)),
            ],
            axis=1,
        )
        mlp_sum = lax.psum_scatter(mlp_grad, "fsdp", scatter_dimension=0, tiled=True)
        fc1_part = jnp.sum(pre.astype(F32), axis=0, keepdims=True)

    grad_middle, grad_attn, sums = call(
        middle_back_kernel,
        "middle_back",
        [block_f32, block, ((8, width), F32)],
        [cot, middle, branch, *grad_in, mod],
    )
    a_blocks = tp_gather(grad_attn)
    parts = call(
        functools.partial(mlp_out_kernel, hidden=hidden),
        "mlp_out",
        [block] * 4,
        [act, mlp_full],
        flops=1.2e9,
        ordered=[a_blocks[2]],
    )
    mlp_parts = tp_scatter(parts)
    back_rows, grads, *parts = call(
        functools.partial(attn_back_kernel, latents=latents),
        "attention_back",
        [((tokens, width), BF), ((tokens, 3 * cols), BF)] + [block] * 4,
        [*a_blocks, qkv_full, proj_full, qkv],
        flops=6.0e9,
    )
    grad_in = tp_scatter(parts)
    output, gates = call(
        output_kernel,
        "output",
        [block, ((8, width), F32)],
        [middle, cot, *mlp_parts, second_bias, mod],
    )
    if direct:
        attn_keep, attn_send, qkv_part = call(
            attn_grad_kernel,
            "attn_weight_grad",
            [((count // 2, feat, 4 * cols), BF)] * 2 + [((1, 3 * cols), F32)],
            [attn_rows, grads, back_rows, att],
            [rank],
            flops=1.2e9,
            ordered=[parts[3]],
        )
        attn_sum = scatter_two(attn_keep, attn_send)
    else:
        attn_grad = jnp.concatenate(
            [dot(attn_rows, grads, (0, 0)), dot(back_rows, att, (0, 0))], axis=1
        )
        attn_sum = lax.psum_scatter(attn_grad, "fsdp", scatter_dimension=0, tiled=True)
        qkv_part = jnp.sum(grads.astype(F32), axis=0, keepdims=True)

    inputs_grad, pack = call(
        input_back_kernel,
        "input_back",
        [block_f32, ((16, width), BF)],
        [x, grad_middle, *grad_in, mod, sums, gates, fc2_part, fc1_part, qkv_part],
        scratch=[pltpu.VMEM((16, width), F32)],
    )
    packs = [pack] + [swap(pack, "tp", d) for d in range(1, tp_count)]
    sent = call(
        functools.partial(spread_kernel, latents=latents, feat=feat),
        "spread",
        [((count, 16, width), BF)],
        packs,
        [tp_rank],
        scratch=[pltpu.VMEM((tp_count, 16, width), F32), pltpu.VMEM((16, width), F32)],
    )[0]
    got = lax.all_to_all(sent, "fsdp", split_axis=0, concat_axis=0, tiled=True)
    grad_mod_all = got[:, :mods].reshape(count * latents, 6 * width)
    silu_cols = dot(grad_mod_all, ada_weight, (1, 1))
    silu_got = lax.all_to_all(
        silu_cols.reshape(count, latents, feat), "fsdp", split_axis=0, concat_axis=0, tiled=True
    )
    ada_weight_grad = dot(cond_cols, grad_mod_all, (0, 0))
    bias_grads = jnp.sum(got[:, mods].astype(F32), axis=0)
    ada_bias_grad = jnp.sum(
        lax.dynamic_slice_in_dim(grad_mod_all, rank * mod_part, mod_part, 1).astype(F32), axis=0
    )
    silu_grad = silu_got.transpose(1, 0, 2).reshape(latents, width)
    cond_grad = jax.vjp(jax.nn.silu, conditioning.astype(F32))[1](silu_grad)[0]

    return (
        output.reshape(latents, positions, width).transpose(1, 0, 2),
        inputs_grad.reshape(latents, positions, width).transpose(1, 0, 2),
        cond_grad,
        ada_weight_grad,
        ada_bias_grad,
        attn_sum[:, : 3 * cols].reshape(feat, 3, cols),
        bias_grads[: 2 * feat].reshape(2, feat),
        attn_sum[:, 3 * cols :].T,
        bias_grads[2 * feat : 3 * feat],
        mlp_sum[:, :hidden],
        bias_grads[4 * feat : 4 * feat + hidden_part],
        mlp_sum[:, hidden:].T,
        bias_grads[3 * feat : 4 * feat],
    )


def solution(mesh):
    return jax.shard_map(
        shards,
        mesh=mesh,
        in_specs=(
            P("tp", "fsdp", None),
            P("fsdp", None),
            P("fsdp", None),
            P("fsdp"),
            P("fsdp", None, "tp"),
            P(None, "fsdp"),
            P("tp", "fsdp"),
            P("fsdp"),
            P("fsdp", "tp"),
            P("fsdp"),
            P("tp", "fsdp"),
            P("fsdp"),
            P("tp", "fsdp", None),
        ),
        out_specs=(
            P("tp", "fsdp", None),
            P("tp", "fsdp", None),
            P("fsdp", None),
            P("fsdp", None),
            P("fsdp"),
            P("fsdp", None, "tp"),
            P(None, "fsdp"),
            P("tp", "fsdp"),
            P("fsdp"),
            P("fsdp", "tp"),
            P("fsdp"),
            P("tp", "fsdp"),
            P("fsdp"),
        ),
        check_vma=False,
    )
```

```python
import functools
import math

import jax
import jax.numpy as jnp
from jax import lax
from jax.experimental import pallas as pl
from jax.experimental.pallas import tpu as pltpu
from jax.sharding import PartitionSpec as P

HEAD = 64
EPS = 1e-06
BF = jnp.bfloat16
F32 = jnp.float32
FACTOR = 1.0 / math.sqrt(HEAD)
CURVE = math.sqrt(2.0 / math.pi)
CUBIC = 0.044715


def origin(ndim, step):
    return (0,) * ndim


def call(kernel, name, outs, args, scalars=(), scratch=(), ordered=(), flops=1, blocked=False):
    in_specs = (
        [pl.BlockSpec(memory_space=pltpu.SMEM)] * len(scalars)
        + [pl.BlockSpec(memory_space=pl.ANY)] * len(ordered)
        + (
            [pl.BlockSpec(a.shape, functools.partial(origin, a.ndim)) for a in args]
            if blocked
            else [pl.BlockSpec(memory_space=pltpu.VMEM)] * len(args)
        )
    )
    skip = len(scalars)

    def body(*refs):
        kernel(*refs[:skip], *refs[skip + len(ordered) :])

    shapes = [jax.ShapeDtypeStruct(shape, dtype) for shape, dtype in outs]
    return pl.pallas_call(
        body,
        out_shape=shapes,
        grid=(1,) if blocked else (),
        in_specs=in_specs,
        out_specs=[pl.BlockSpec(memory_space=pltpu.VMEM)] * len(outs),
        scratch_shapes=list(scratch),
        compiler_params=pltpu.CompilerParams(vmem_limit_bytes=14 * 1024 * 1024),
        cost_estimate=pl.CostEstimate(flops=int(flops), bytes_accessed=1, transcendentals=0),
        name=name,
    )(*[s.reshape(1).astype(jnp.int32) for s in scalars], *ordered, *args)


def dot(a, b, over=(1, 0)):
    return lax.dot_general(
        a, b, (((over[0],), (over[1],)), ((), ())), preferred_element_type=F32
    )


def normed(v):
    centered = v - jnp.mean(v, axis=-1, keepdims=True)
    scale = lax.rsqrt(jnp.mean(centered * centered, axis=-1, keepdims=True) + EPS)
    return centered * scale, scale


def norm_back(n, scale, grad):
    mean = jnp.mean(grad, axis=-1, keepdims=True)
    along = jnp.mean(grad * n, axis=-1, keepdims=True)
    return (grad - mean - n * along) * scale


def swap(block, axis, offset):
    count = lax.axis_size(axis)
    return lax.ppermute(block, axis, [(i, i ^ offset) for i in range(count)])


def tp_gather(rows):
    far = swap(rows, "tp", 2)
    near = swap(rows, "tp", 1)
    return [rows, near, far, swap(far, "tp", 1)]


def near_rows_kernel(keep, got, own, out):
    rows = own.shape[0]
    own[...] = keep[:rows].astype(F32) + got[:rows].astype(F32)
    out[...] = (keep[rows:].astype(F32) + got[rows:].astype(F32)).astype(BF)


def tp_scatter(keep, send, ordered=()):
    got = swap(send, "tp", 1)
    rows, cols = keep.shape
    own, out = call(
        near_rows_kernel,
        "near_rows",
        [((rows // 2, cols), F32), ((rows // 2, cols), BF)],
        [keep, got],
        ordered=ordered,
    )
    return [own, swap(out, "tp", 2)]


def put_piece(rank, k, value, keep, send):
    to = jnp.bitwise_xor(rank[0], k)

    @pl.when(to % 2 == 0)
    def _():
        keep[to // 2] = value

    @pl.when(to % 2 == 1)
    def _():
        send[to // 2] = value


def pack_kernel(rank, cond, qv, proj, second, hidden, keep, send, scr):
    count = 2 * keep.shape[0]
    feat = qv.shape[1]
    latents = cond.shape[0]
    value = cond[...].astype(F32)
    act = (value / (1.0 + jnp.exp(-value))).astype(BF).astype(F32)
    tail = hidden[...].astype(F32)
    rows = [qv[...].astype(F32), proj[...].astype(F32), second[...].astype(F32)]
    rows += [tail[:, r * feat : (r + 1) * feat] for r in range(tail.shape[1] // feat)]
    scr[...] = jnp.zeros_like(scr)
    at = latents
    for row in rows:
        scr[at : at + row.shape[0], 0:feat] = row
        at += row.shape[0]
    for k in range(count):
        scr[0:latents, 0:feat] = act[:, k * feat : (k + 1) * feat]
        put_piece(rank, k, scr[...], keep, send)


def pair_kernel(keep, got, *outs):
    for z, out in enumerate(outs):
        out[0] = keep[z]
        out[1] = got[z]


def exchange(keep, send, ordered=()):
    size = keep.shape[0]
    piece = keep.shape[1:]
    if size != 4:
        count = 2 * size
        order = jnp.bitwise_xor(jnp.arange(count), lax.axis_index("fsdp"))
        whole = jnp.stack([keep, send], axis=1).reshape(count, *piece)
        got = lax.all_to_all(
            jnp.take(whole, order, axis=0), "fsdp", split_axis=0, concat_axis=0, tiled=True
        )
        return [jnp.take(got, order, axis=0)]
    got = swap(send, "fsdp", 1)
    pairs = call(
        pair_kernel, "pairs", [((2, *piece), keep.dtype)] * size, [keep, got], ordered=ordered
    )
    return [pairs[0]] + [swap(pairs[z], "fsdp", 2 * z) for z in range(1, size)]


def pick(arrays, k):
    per = arrays[0].shape[0]
    return arrays[k // per].at[k % per]


def attn_own_kernel(qkv, proj, out):
    cols = qkv.shape[2]
    for j in range(3):
        out[:, j * cols : (j + 1) * cols] = qkv[j]
    out[:, 3 * cols :] = proj[...].T


def copy_kernel(value, out):
    out[...] = value[...]


def join_kernel(a, b, out):
    half = out.shape[0] // 2
    if len(a.shape) == 2:
        out[0] = a[...]
        out[1] = b[...]
    else:
        out[:half] = a[...]
        out[half:] = b[...]


def join(a, b, ordered=()):
    size = 1 if a.ndim == 2 else a.shape[0]
    shape = (2 * size, *a.shape[-2:])
    return call(join_kernel, "join", [(shape, a.dtype)], [a, b], ordered=ordered)[0]


def gather_steps(own, ordered=((), ())):
    two = join(own, swap(own, "fsdp", 4), ordered[0])
    four = join(two, swap(two, "fsdp", 2), ordered[1])
    return two, four, swap(four, "fsdp", 1)


def mod_kernel(*refs):
    *got, ada, bias, keep, send, cols_out, scr, pieces = refs
    count = pieces.shape[0]
    feat = ada.shape[0]
    latents = scr.shape[0] // count
    for k in range(count):
        scr[k * latents : (k + 1) * latents, :] = pick(got, k)[0:latents, :]
    cols = scr[:, 0:feat].astype(BF)
    cols_out[...] = cols
    width = ada.shape[1] // 6
    pieces[...] = jnp.zeros_like(pieces)
    for j in range(6):
        at = slice(j * width, (j + 1) * width)
        part = dot(cols, ada[:, at]) + bias[:, at]
        for k in range(count):
            for l in range(latents):
                pieces[k, 6 * l + j : 6 * l + j + 1, :] = part[k * latents + l : k * latents + l + 1]
    for z in range(count // 2):
        keep[z] = pieces[2 * z].astype(BF)
        send[z] = pieces[2 * z + 1].astype(BF)


def bias_kernel(rank, tp_rank, *refs, latents, feat, tp):
    *got, qkv_out, proj_out, second_out, hidden_out, scr = refs
    count = scr.shape[0]
    for k in range(count):
        scr[jnp.bitwise_xor(rank[0], k)] = pick(got, k)[...]
    per = count // tp
    first = tp_rank[0] * per
    cols = per * feat
    qkv_out[...] = jnp.zeros_like(qkv_out)
    at = latents
    for i in range(per):
        f = first + i
        here = slice(i * feat, (i + 1) * feat)
        qkv_out[0:1, here] = scr[f, at : at + 1, 0:feat]
        qkv_out[0:1, 2 * cols + i * feat : 2 * cols + (i + 1) * feat] = scr[
            f, at + 1 : at + 2, 0:feat
        ]
        for r in range(tp):
            lane = (i * tp + r) * feat
            hidden_out[0:1, lane : lane + feat] = scr[f, at + 4 + r : at + 5 + r, 0:feat]
    for f in range(count):
        here = slice(f * feat, (f + 1) * feat)
        proj_out[0:1, here] = scr[f, at + 2 : at + 3, 0:feat]
        second_out[0:1, here] = scr[f, at + 3 : at + 4, 0:feat]


def assemble_kernel(rank, mine, other, *outs):
    rows = mine.shape[1]
    for i, z in enumerate((0, 2, 1, 3)):
        for x, blocks in enumerate((mine, other)):
            at = jnp.bitwise_xor(rank[0], 2 * z + x) * rows
            at = pl.ds(pl.multiple_of(at, rows), rows)
            lane = 0
            for out in outs:
                out[at, :] = blocks[i, :, lane : lane + out.shape[1]]
                lane += out.shape[1]


def first_norm_kernel(x0, x1, x2, x3, *refs):
    *got, mod_out, out = refs
    mod = got[0][...].astype(F32)
    for part in got[1:]:
        mod = mod + part[...].astype(F32)
    mod_out[...] = mod[0 : mod_out.shape[0]]
    latents = mod_out.shape[0] // 6
    part = x0.shape[0] // (2 * latents)
    whole = out.shape[0] // latents
    for b, block in enumerate((x0, x1, x2, x3)):
        for l in range(latents):
            n, _ = normed(block[l * part : (l + 1) * part, :].astype(F32))
            shift, scale = mod[6 * l : 6 * l + 1], mod[6 * l + 1 : 6 * l + 2]
            out[l * whole + b * part : l * whole + (b + 1) * part, :] = (
                n * (1.0 + scale) + shift
            ).astype(BF)


def gate_grad_kernel(x0, x1, x2, x3, mod, out, bias_out):
    latents = mod.shape[0] // 6
    rows = x0.shape[0] // 2
    part = rows // latents
    total = jnp.zeros((1, mod.shape[1]), F32)
    for b, block in enumerate((x0, x1, x2, x3)):
        for l in range(latents):
            cot = block[rows + l * part : rows + (l + 1) * part, :].astype(F32)
            value = (cot * mod[6 * l + 5 : 6 * l + 6, :]).astype(BF)
            out[b * rows + l * part : b * rows + (l + 1) * part, :] = value
            if b == 0:
                total = total + jnp.sum(value.astype(F32), axis=0, keepdims=True)
    bias_out[...] = total


def unpack_rows(blocks, rows, latents):
    part = blocks[0].shape[0] // latents
    whole = part * len(blocks)
    for b, block in enumerate(blocks):
        for l in range(latents):
            rows[l * whole + b * part : l * whole + (b + 1) * part, :] = block[
                l * part : (l + 1) * part, :
            ]


def put_parts(value, keep, send, latent):
    part = value.shape[0] // 4
    rows = keep.shape[0] // 2
    for b in range(4):
        out = send if b % 2 else keep
        at = (b // 2) * rows + latent * part
        out[at : at + part, :] = value[b * part : (b + 1) * part]


def softmax(q, k):
    scores = dot(q, k, (1, 1)) * FACTOR
    weights = jnp.exp(scores - jnp.max(scores, axis=-1, keepdims=True))
    return weights * (1.0 / jnp.sum(weights, axis=-1, keepdims=True))


def attn_kernel(rows, qkv_w, proj_w, bias, qkv, att, keep, send, *, latents):
    cols = proj_w.shape[1]
    size = rows.shape[0] // latents
    for l in range(latents):
        here = slice(l * size, (l + 1) * size)
        projected = (dot(rows[here, :], qkv_w[...]) + bias[...]).astype(BF)
        qkv[here, :] = projected
        mixed = []
        for h in range(cols // HEAD):
            q, k, v = [
                projected[:, j * cols + h * HEAD : j * cols + (h + 1) * HEAD] for j in range(3)
            ]
            mixed.append(dot(softmax(q, k).astype(BF), v))
        attended = jnp.concatenate(mixed, axis=1).astype(BF)
        att[here, :] = attended
        put_parts(dot(attended, proj_w[...], (1, 1)).astype(BF), keep, send, l)


def middle_kernel(x, p0, p1, bias, mod, branch_out, middle_out, out):
    latents = mod.shape[0] // 6
    rows = out.shape[0] // latents
    for l in range(latents):
        here = slice(l * rows, (l + 1) * rows)
        branch = bias[...] + p0[here, :] + p1[here, :].astype(F32)
        branch_out[here, :] = branch
        gate = mod[6 * l + 2 : 6 * l + 3, :]
        middle = x[here, :].astype(F32) + gate * branch
        middle_out[here, :] = middle
        n, _ = normed(middle)
        shift = mod[6 * l + 3 : 6 * l + 4, :]
        scale = mod[6 * l + 4 : 6 * l + 5, :]
        out[here, :] = (n * (1.0 + scale) + shift).astype(BF)


def mlp_kernel(
    x0, x1, x2, x3, grads, first, second, bias, act_out, pre_out, x_out, keep, send
):
    rows = x0.shape[0]
    for b, x in enumerate((x0, x1, x2, x3)):
        here = slice(b * rows, (b + 1) * rows)
        x_out[here, :] = x[...]
        v = dot(x[...], first[...]) + bias[...]
        square = v * v
        t = jnp.tanh(CURVE * v * (1.0 + CUBIC * square))
        act_out[here, :] = (0.5 * v * (1.0 + t)).astype(BF)
        slope = 0.5 * (1.0 + t) + 0.5 * v * (1.0 - t * t) * CURVE * (1.0 + 3.0 * CUBIC * square)
        pre = (dot(grads[here, :], second[...]) * slope).astype(BF)
        pre_out[here, :] = pre
        at = (b // 2) * rows
        out = send if b % 2 else keep
        out[at : at + rows, :] = dot(pre, first[...], (1, 1)).astype(BF)


def store_grad(rank, product, keep, send, cols):
    rows = keep.shape[1]
    place = rank[0] // 2
    for mine in range(2):

        @pl.when(rank[0] % 2 == mine)
        def _():
            for z in range(keep.shape[0]):
                to = jnp.bitwise_xor(place, z)
                keep[to, :, cols] = product[(2 * z + mine) * rows : (2 * z + mine + 1) * rows]
                send[to, :, cols] = product[
                    (2 * z + 1 - mine) * rows : (2 * z + 2 - mine) * rows
                ]


def mlp_grad_kernel(rank, x, g, act, pre, keep_b, send_b, keep_c, send_c, bias_out):
    hidden = act.shape[1]
    for left, right, keep, send in ((x, pre, keep_b, send_b), (g, act, keep_c, send_c)):
        for at in range(0, hidden, 256):
            product = dot(left[...], right[:, at : at + 256], (0, 0)).astype(BF)
            store_grad(rank, product, keep, send, slice(at, at + 256))
    bias_out[...] = jnp.sum(pre[...].astype(F32), axis=0, keepdims=True)


def mlp_out_kernel(act, second, keep, send):
    rows = keep.shape[0] // 2
    for b in range(4):
        at = (b // 2) * rows
        out = send if b % 2 else keep
        value = dot(act[b * rows : (b + 1) * rows, :], second[...], (1, 1))
        out[at : at + rows, :] = value.astype(BF)


def output_kernel(middle, x, p0, p1, bias, mod, out, sums):
    latents = mod.shape[0] // 6
    size = middle.shape[0]
    rows = size // latents
    for l in range(latents):
        here = slice(l * rows, (l + 1) * rows)
        branch = bias[...] + p0[here, :] + p1[here, :].astype(F32)
        cot = x[size + l * rows : size + (l + 1) * rows, :].astype(F32)
        out[here, :] = (middle[here, :] + mod[6 * l + 5 : 6 * l + 6, :] * branch).astype(BF)
        sums[l : l + 1, :] = jnp.sum(cot * branch, axis=0, keepdims=True)


def middle_back_kernel(x, middle, branch, p0, p1, mod, grad_out, out, sums):
    latents = mod.shape[0] // 6
    width = middle.shape[1]
    size = middle.shape[0]
    rows = size // latents
    total = jnp.zeros((1, width), F32)
    for l in range(latents):
        here = slice(l * rows, (l + 1) * rows)
        grad = p0[here, :] + p1[here, :].astype(F32)
        cot = x[size + l * rows : size + (l + 1) * rows, :].astype(F32)
        n, scale = normed(middle[here, :])
        sums[3 * l + 1 : 3 * l + 2, :] = jnp.sum(grad, axis=0, keepdims=True)
        sums[3 * l + 2 : 3 * l + 3, :] = jnp.sum(grad * n, axis=0, keepdims=True)
        factor = 1.0 + mod[6 * l + 4 : 6 * l + 5, :]
        whole = cot + norm_back(n, scale, grad * factor)
        grad_out[here, :] = whole
        sums[3 * l : 3 * l + 1, :] = jnp.sum(whole * branch[here, :], axis=0, keepdims=True)
        low = (whole * mod[6 * l + 2 : 6 * l + 3, :]).astype(BF)
        out[here, :] = low
        total = total + jnp.sum(low.astype(F32), axis=0, keepdims=True)
    sums[3 * latents : 3 * latents + 1, :] = total


def attn_back_kernel(
    g0, g1, g2, g3, qkv_w, proj_w, qkv, rows, grads, keep, send, *, latents
):
    unpack_rows([g0, g1, g2, g3], rows, latents)
    cols = proj_w.shape[1]
    size = rows.shape[0] // latents
    for l in range(latents):
        here = slice(l * size, (l + 1) * size)
        back = dot(rows[here, :], proj_w[...]).astype(BF)
        projected = qkv[here, :]
        found = [[], [], []]
        for h in range(cols // HEAD):
            q, k, v = [
                projected[:, j * cols + h * HEAD : j * cols + (h + 1) * HEAD] for j in range(3)
            ]
            up = back[:, h * HEAD : (h + 1) * HEAD]
            probs = softmax(q, k)
            grad_probs = dot(up, v, (1, 1))
            inner = jnp.sum(probs * grad_probs, axis=-1, keepdims=True)
            scores = (probs * (grad_probs - inner)).astype(BF)
            found[0].append(dot(scores, k) * FACTOR)
            found[1].append(dot(scores, q, (0, 0)) * FACTOR)
            found[2].append(dot(probs.astype(BF), up, (0, 0)))
        grad = jnp.concatenate(found[0] + found[1] + found[2], axis=1).astype(BF)
        grads[here, :] = grad
        put_parts(dot(grad, qkv_w[...], (1, 1)).astype(BF), keep, send, l)


def attn_grad_kernel(rank, rows, grads, back, att, keep, send, bias_out):
    cols = att.shape[1]
    for at in range(0, 3 * cols, cols):
        product = dot(rows[...], grads[:, at : at + cols], (0, 0)).astype(BF)
        store_grad(rank, product, keep, send, slice(at, at + cols))
    product = dot(back[...], att[...], (0, 0)).astype(BF)
    store_grad(rank, product, keep, send, slice(3 * cols, 4 * cols))
    bias_out[...] = jnp.sum(grads[...].astype(F32), axis=0, keepdims=True)


def input_back_kernel(
    x, grad_middle, p0, p1, mod, sums, gates, fc2, fc1, qkv, out, pack, scr
):
    latents = mod.shape[0] // 6
    rows = out.shape[0] // latents
    cols = qkv.shape[1] // 3
    scr[...] = jnp.zeros_like(scr)
    for l in range(latents):
        here = slice(l * rows, (l + 1) * rows)
        grad = p0[here, :] + p1[here, :].astype(F32)
        n, scale = normed(x[here, :].astype(F32))
        scr[6 * l : 6 * l + 1, :] = jnp.sum(grad, axis=0, keepdims=True)
        scr[6 * l + 1 : 6 * l + 2, :] = jnp.sum(grad * n, axis=0, keepdims=True)
        scr[6 * l + 2 : 6 * l + 5, :] = sums[3 * l : 3 * l + 3, :]
        scr[6 * l + 5 : 6 * l + 6, :] = gates[l : l + 1, :]
        factor = 1.0 + mod[6 * l + 1 : 6 * l + 2, :]
        out[here, :] = grad_middle[here, :] + norm_back(n, scale, grad * factor)
    at = 6 * latents
    scr[at : at + 1, :] = sums[3 * latents : 3 * latents + 1, :]
    scr[at + 1 : at + 2, :] = fc2[...]
    scr[at + 2 : at + 3, :] = fc1[...]
    scr[at + 3 : at + 4, 0:cols] = qkv[:, 0:cols]
    scr[at + 3 : at + 4, cols : 2 * cols] = qkv[:, 2 * cols :]
    pack[...] = scr[...].astype(BF)


def spread_kernel(
    rank, tp_rank, k0, k1, k2, k3, keep, send, parts, total, *, latents, feat
):
    count = 2 * keep.shape[0]
    packs = (k0, k1, k2, k3)
    per = count // len(packs)
    cols = per * feat
    mods = 6 * latents
    summed = jnp.zeros(k0.shape, F32)
    for d, pack in enumerate(packs):
        value = pack[...].astype(F32)
        parts[jnp.bitwise_xor(tp_rank[0], d)] = value
        summed = summed + value
    total[...] = summed
    row = slice(mods, mods + 1)
    total[row, :] = jnp.zeros((1, k0.shape[1]), F32)
    for k in range(count):
        t, i = k // per, k % per
        here = slice(k * feat, (k + 1) * feat)
        total[row, 0:feat] = parts[t, mods + 3 : mods + 4, i * feat : (i + 1) * feat]
        total[row, feat : 2 * feat] = parts[
            t, mods + 3 : mods + 4, cols + i * feat : cols + (i + 1) * feat
        ]
        total[row, 2 * feat : 3 * feat] = summed[mods : mods + 1, here]
        total[row, 3 * feat : 4 * feat] = summed[mods + 1 : mods + 2, here]
        total[row, 4 * feat : 8 * feat] = parts[
            t, mods + 2 : mods + 3, 4 * i * feat : 4 * (i + 1) * feat
        ]
        put_piece(rank, k, total[...].astype(BF), keep, send)


def silu_kernel(*refs, latents):
    *got, ada, keep, send, grads, bias_out, scr, out_scr = refs
    width = ada.shape[1] // 6
    feat = ada.shape[0]
    count = scr.shape[1] // latents
    mods = 6 * latents
    bias = jnp.zeros((1, width), F32)
    for k in range(count):
        value = pick(got, k)[...].astype(F32)
        bias = bias + value[mods : mods + 1]
        for l in range(latents):
            for j in range(6):
                scr[j, k * latents + l : k * latents + l + 1, :] = value[6 * l + j : 6 * l + j + 1]
    bias_out[...] = bias
    total = jnp.zeros((count * latents, feat), F32)
    for j in range(6):
        at = slice(j * width, (j + 1) * width)
        rows = scr[j].astype(BF)
        grads[:, at] = rows
        total = total + dot(rows, ada[:, at], (1, 1))
    out_scr[...] = jnp.zeros_like(out_scr)
    for k in range(count):
        out_scr[k, 0:latents, 0:feat] = total[k * latents : (k + 1) * latents]
    for z in range(count // 2):
        keep[z] = out_scr[2 * z]
        send[z] = out_scr[2 * z + 1]


def cond_kernel(rank, *refs, latents, feat):
    *got, cond, out, scr = refs
    count = scr.shape[0]
    for k in range(count):
        scr[jnp.bitwise_xor(rank[0], k)] = pick(got, k)[...]
    value = cond[...].astype(F32)
    gate = 1.0 / (1.0 + jnp.exp(-value))
    slope = gate * (1.0 + value * (1.0 - gate))
    for k in range(count):
        here = slice(k * feat, (k + 1) * feat)
        out[:, here] = scr[k, 0:latents, 0:feat] * slope[:, here]


def scatter_pieces(keep, send):
    count = 2 * keep.shape[0]
    order = jnp.bitwise_xor(jnp.arange(count), lax.axis_index("fsdp"))
    whole = jnp.stack([keep, send], axis=1).reshape(count, *keep.shape[1:]).astype(F32)
    whole = jnp.take(whole, order, axis=0)
    return lax.psum_scatter(whole, "fsdp", scatter_dimension=0, tiled=False)


def halve_four_kernel(keep, got, own, out):
    for z in range(2):
        own[z] = keep[2 * z].astype(F32) + got[2 * z].astype(F32)
        out[z] = (keep[2 * z + 1].astype(F32) + got[2 * z + 1].astype(F32)).astype(BF)


def halve_two_kernel(keep, got, own, out):
    own[...] = keep[0] + got[0].astype(F32)
    out[...] = (keep[1] + got[1].astype(F32)).astype(BF)


def halve_four(keep, send):
    shape = (2, *keep.shape[1:])
    got = swap(send, "fsdp", 1)
    return call(halve_four_kernel, "halve_four", [(shape, F32), (shape, BF)], [keep, got])


def halve_two(keep, send, ordered=()):
    shape = keep.shape[1:]
    got = swap(send, "fsdp", 2)
    outs = [(shape, F32), (shape, BF)]
    return call(halve_two_kernel, "halve_two", outs, [keep, got], ordered=ordered)


def add_kernel(own, got, out):
    out[...] = own[...] + got[...].astype(F32)


def halve_one(own, out):
    got = swap(out, "fsdp", 4)
    return call(add_kernel, "last_sum", [(own.shape, F32)], [own, got])[0]


def attn_add_kernel(own, got, qkv, proj):
    cols = qkv.shape[2]
    for j in range(3):
        here = slice(j * cols, (j + 1) * cols)
        qkv[j] = own[:, here] + got[:, here].astype(F32)
    here = slice(3 * cols, 4 * cols)
    proj[...] = (own[:, here] + got[:, here].astype(F32)).T


def shards(
    inputs,
    conditioning,
    ada_weight,
    ada_bias,
    query_key_value_weight,
    qv_bias,
    attention_output_weight,
    attention_output_bias,
    expand_weight,
    hidden_layer_bias,
    contract_weight,
    contract_bias,
    out_cotangent,
):
    tp_rank = lax.axis_index("tp")
    tp_count = lax.axis_size("tp")
    rank = lax.axis_index("fsdp")
    count = lax.axis_size("fsdp")
    positions, latents, width = inputs.shape
    feat = ada_weight.shape[0]
    cols = query_key_value_weight.shape[2]
    hidden = expand_weight.shape[1]
    hidden_part = hidden_layer_bias.shape[0]
    mod_part = ada_bias.shape[0]
    rows = positions * latents
    tokens = rows * tp_count
    mods = 6 * latents
    direct = count == 8
    block = ((rows, width), BF)
    block_f32 = ((rows, width), F32)

    half = count // 2
    cond_keep, cond_send = call(
        pack_kernel,
        "pack_conditioning",
        [((half, 16, 128), F32)] * 2,
        [
            conditioning,
            qv_bias,
            attention_output_bias.reshape(1, feat),
            contract_bias.reshape(1, feat),
            hidden_layer_bias.reshape(1, hidden_part),
        ],
        [rank],
        scratch=[pltpu.VMEM((16, 128), F32)],
        blocked=True,
    )
    cond_got = exchange(cond_keep, cond_send)

    bias_row = lax.dynamic_update_slice(
        jnp.zeros((1, mod_part * count), F32),
        ada_bias.astype(F32).reshape(1, mod_part),
        (0, rank * mod_part),
    )
    mod_keep, mod_send, cond_cols = call(
        mod_kernel,
        "modulation",
        [((half, 16, width), BF)] * 2 + [((count * latents, feat), BF)],
        [*cond_got, ada_weight, bias_row],
        scratch=[
            pltpu.VMEM((count * latents, 128), F32),
            pltpu.VMEM((count, 16, width), F32),
        ],
    )
    x_own = jnp.stack([inputs.transpose(1, 0, 2), out_cotangent.transpose(1, 0, 2)])
    x_own = x_own.reshape(2 * rows, width)
    x_own = call(
        copy_kernel, "tokens", [((2 * rows, width), BF)], [x_own], ordered=cond_got
    )[0]
    x_blocks = tp_gather(x_own)

    qkv_own = query_key_value_weight.transpose(1, 0, 2)
    if direct:
        attn_own = call(
            attn_own_kernel,
            "attn_own",
            [((feat, 4 * cols), BF)],
            [qkv_own, attention_output_weight],
            ordered=[cond_got[0]],
            blocked=True,
        )[0]
        mod_half = halve_four(mod_keep, mod_send)
        mod_own, mod_out = halve_two(*mod_half)
        mod_parts = [mod_own, swap(mod_out, "fsdp", 4)]
        attn_two, attn_four, attn_other = gather_steps(attn_own, ([mod_half[1]], [mod_own]))
        first_own = call(
            copy_kernel,
            "first_own",
            [((feat, hidden), BF)],
            [expand_weight],
            ordered=[attn_four],
            blocked=True,
        )[0]
        first_two, first_four, first_other = gather_steps(first_own)
        second_own = call(
            copy_kernel,
            "second_own",
            [((feat, hidden), BF)],
            [contract_weight.T],
            ordered=[first_two],
            blocked=True,
        )[0]
        second_two, second_four, second_other = gather_steps(second_own)
        qkv_full, proj_full = call(
            assemble_kernel,
            "attn_weights",
            [((width, 3 * cols), BF), ((width, cols), BF)],
            [attn_four, attn_other],
            [rank],
        )
        first_full = call(
            assemble_kernel,
            "first_weights",
            [((width, hidden), BF)],
            [first_four, first_other],
            [rank],
        )[0]
        second_full = call(
            assemble_kernel,
            "second_weights",
            [((width, hidden), BF)],
            [second_four, second_other],
            [rank],
        )[0]
        steps = [[attn_four], [first_two], [first_four, second_two], [second_four]]
    else:
        steps = [[]] * 4
        mod_parts = [scatter_pieces(mod_keep, mod_send)]
        qkv_full = lax.all_gather(
            query_key_value_weight.reshape(feat, 3 * cols), "fsdp", axis=0, tiled=True
        )
        proj_full = lax.all_gather(attention_output_weight.T, "fsdp", axis=0, tiled=True)
        first_full = lax.all_gather(expand_weight, "fsdp", axis=0, tiled=True)
        second_full = lax.all_gather(contract_weight.T, "fsdp", axis=0, tiled=True)

    qkv_bias, proj_bias, second_bias, hidden_bias = call(
        functools.partial(bias_kernel, latents=latents, feat=feat, tp=tp_count),
        "biases",
        [((1, 3 * cols), F32), ((1, width), F32), ((1, width), F32), ((1, hidden), F32)],
        cond_got,
        [rank, tp_rank],
        scratch=[pltpu.VMEM((count, 16, 128), F32)],
        ordered=[mod_send],
        flops=1e9,
    )
    mod, attn_rows = call(
        first_norm_kernel,
        "first_norm",
        [((mods, width), F32), ((tokens, width), BF)],
        [*x_blocks, *mod_parts],
        ordered=[hidden_bias, *steps[0]],
    )
    pair = ((2 * rows, width), BF)
    qkv, att, keep, send = call(
        functools.partial(attn_kernel, latents=latents),
        "attention",
        [((tokens, 3 * cols), BF), ((tokens, cols), BF), pair, pair],
        [attn_rows, qkv_full, proj_full, qkv_bias],
        ordered=steps[1],
    )
    branch_parts = tp_scatter(keep, send)
    grad_rows, fc2_part = call(
        gate_grad_kernel,
        "gate_grad",
        [((tokens, width), BF), ((1, width), F32)],
        [*x_blocks, mod],
        ordered=[branch_parts[0], *steps[2]],
        flops=1e9,
    )
    branch, middle, mlp_in = call(
        middle_kernel,
        "middle",
        [block_f32, block_f32, block],
        [x_own, *branch_parts, proj_bias, mod],
        ordered=[fc2_part, *steps[3]],
    )
    m_blocks = tp_gather(mlp_in)
    act, pre, mlp_rows, keep, send = call(
        mlp_kernel,
        "mlp",
        [((tokens, hidden), BF)] * 2 + [((tokens, width), BF), pair, pair],
        [*m_blocks, grad_rows, first_full, second_full, hidden_bias],
    )
    out_keep, out_send = call(
        mlp_out_kernel, "mlp_out", [pair, pair], [act, second_full], ordered=[send], flops=1.5e9
    )
    grad_in = tp_scatter(keep, send, [out_send])
    if direct:
        first_keep, first_send, second_keep, second_send, fc1_part = call(
            mlp_grad_kernel,
            "mlp_weight_grad",
            [((half, feat, hidden), BF)] * 4 + [((1, hidden), F32)],
            [mlp_rows, grad_rows, act, pre],
            [rank],
            ordered=[grad_in[0]],
            flops=4e9,
        )
        first_half = halve_four(first_keep, first_send)
        first_one = halve_two(*first_half)
        first_sum = halve_one(*first_one)
        second_half = halve_four(second_keep, second_send)
        second_one = halve_two(*second_half)
        second_sum = halve_one(*second_one)
        steps = [[first_half[1]], [second_half[1], first_one[1]], [second_one[1]]]
    else:
        first_sum = lax.psum_scatter(
            dot(mlp_rows, pre, (0, 0)), "fsdp", scatter_dimension=0, tiled=True
        )
        second_sum = lax.psum_scatter(
            dot(grad_rows, act, (0, 0)), "fsdp", scatter_dimension=0, tiled=True
        )
        fc1_part = jnp.sum(pre.astype(F32), axis=0, keepdims=True)
        steps = [[]] * 3

    grad_middle, grad_attn, sums = call(
        middle_back_kernel,
        "middle_back",
        [block_f32, block, ((8, width), F32)],
        [x_own, middle, branch, *grad_in, mod],
        ordered=[fc1_part] if direct else [],
    )
    a_blocks = tp_gather(grad_attn)
    mlp_parts = tp_scatter(out_keep, out_send, [a_blocks[2]])
    back_rows, grads, keep, send = call(
        functools.partial(attn_back_kernel, latents=latents),
        "attention_back",
        [((tokens, width), BF), ((tokens, 3 * cols), BF), pair, pair],
        [*a_blocks, qkv_full, proj_full, qkv],
        ordered=[mlp_parts[0], *steps[0]],
    )
    grad_in = tp_scatter(keep, send)
    output, gates = call(
        output_kernel,
        "output",
        [block, ((8, width), F32)],
        [middle, x_own, *mlp_parts, second_bias, mod],
    )
    if direct:
        attn_keep, attn_send, qkv_part = call(
            attn_grad_kernel,
            "attn_weight_grad",
            [((half, feat, 4 * cols), BF)] * 2 + [((1, 3 * cols), F32)],
            [attn_rows, grads, back_rows, att],
            [rank],
            ordered=[grad_in[0], gates, *steps[1]],
            flops=6e9,
        )
        attn_half = halve_four(attn_keep, attn_send)
        own, out = halve_two(*attn_half)
        tail = [[attn_half[1]], [out]]
        qkv_sum, proj_sum = call(
            attn_add_kernel,
            "attn_sum",
            [((3, feat, cols), F32), ((cols, feat), F32)],
            [own, swap(out, "fsdp", 4)],
        )
        qkv_sum = qkv_sum.transpose(1, 0, 2)
    else:
        tail = [[]] * 2
        qkv_sum = lax.psum_scatter(
            dot(attn_rows, grads, (0, 0)), "fsdp", scatter_dimension=0, tiled=True
        ).reshape(feat, 3, cols)
        proj_sum = lax.psum_scatter(
            dot(back_rows, att, (0, 0)), "fsdp", scatter_dimension=0, tiled=True
        ).T
        qkv_part = jnp.sum(grads.astype(F32), axis=0, keepdims=True)

    inputs_grad, pack = call(
        input_back_kernel,
        "input_back",
        [block_f32, ((16, width), BF)],
        [x_own, grad_middle, *grad_in, mod, sums, gates, fc2_part, fc1_part, qkv_part],
        scratch=[pltpu.VMEM((16, width), F32)],
    )
    packs = [pack] + [swap(pack, "tp", d) for d in range(1, tp_count)]
    spread_keep, spread_send = call(
        functools.partial(spread_kernel, latents=latents, feat=feat),
        "spread",
        [((half, 16, width), BF)] * 2,
        packs,
        [rank, tp_rank],
        scratch=[pltpu.VMEM((tp_count, 16, width), F32), pltpu.VMEM((16, width), F32)],
        ordered=steps[2],
    )
    silu_keep, silu_send, grad_mod_all, bias_grads = call(
        functools.partial(silu_kernel, latents=latents),
        "silu_columns",
        [((half, 8, 128), F32)] * 2
        + [((count * latents, 6 * width), BF), ((1, width), F32)],
        [*exchange(spread_keep, spread_send), ada_weight],
        scratch=[
            pltpu.VMEM((6, count * latents, width), F32),
            pltpu.VMEM((count, 8, 128), F32),
        ],
        ordered=tail[0],
    )
    cond_grad = call(
        functools.partial(cond_kernel, latents=latents, feat=feat),
        "cond_grad",
        [((latents, width), F32)],
        [*exchange(silu_keep, silu_send), conditioning],
        [rank],
        scratch=[pltpu.VMEM((count, 8, 128), F32)],
        ordered=tail[1],
    )[0]
    ada_weight_grad = dot(cond_cols, grad_mod_all, (0, 0))
    bias_grads = bias_grads.reshape(width)
    ada_bias_grad = jnp.sum(
        lax.dynamic_slice_in_dim(grad_mod_all, rank * mod_part, mod_part, 1).astype(F32), axis=0
    )

    return (
        output.reshape(latents, positions, width).transpose(1, 0, 2),
        inputs_grad.reshape(latents, positions, width).transpose(1, 0, 2),
        cond_grad,
        ada_weight_grad,
        ada_bias_grad,
        qkv_sum,
        bias_grads[: 2 * feat].reshape(2, feat),
        proj_sum,
        bias_grads[2 * feat : 3 * feat],
        first_sum,
        bias_grads[4 * feat : 4 * feat + hidden_part],
        second_sum.T,
        bias_grads[3 * feat : 4 * feat],
    )


def solution(mesh):
    return jax.shard_map(
        shards,
        mesh=mesh,
        in_specs=(
            P("tp", "fsdp", None),
            P("fsdp", None),
            P("fsdp", None),
            P("fsdp"),
            P("fsdp", None, "tp"),
            P(None, "fsdp"),
            P("tp", "fsdp"),
            P("fsdp"),
            P("fsdp", "tp"),
            P("fsdp"),
            P("tp", "fsdp"),
            P("fsdp"),
            P("tp", "fsdp", None),
        ),
        out_specs=(
            P("tp", "fsdp", None),
            P("tp", "fsdp", None),
            P("fsdp", None),
            P("fsdp", None),
            P("fsdp"),
            P("fsdp", None, "tp"),
            P(None, "fsdp"),
            P("tp", "fsdp"),
            P("fsdp"),
            P("fsdp", "tp"),
            P("fsdp"),
            P("tp", "fsdp"),
            P("fsdp"),
        ),
        check_vma=False,
    )
```

```python
import functools
import math

import jax
import jax.numpy as jnp
from jax import lax
from jax.experimental import pallas as pl
from jax.experimental.pallas import tpu as pltpu
from jax.sharding import PartitionSpec as P

HEAD = 64
EPS = 1e-06
BF = jnp.bfloat16
F32 = jnp.float32
FACTOR = 1.0 / math.sqrt(HEAD)
CURVE = math.sqrt(2.0 / math.pi)
CUBIC = 0.044715


def call(kernel, name, outs, args, scalars=(), scratch=(), ordered=(), flops=1, fetch=False):
    space = pltpu.HBM if fetch else pltpu.VMEM
    in_specs = (
        [pl.BlockSpec(memory_space=pltpu.SMEM)] * len(scalars)
        + [pl.BlockSpec(memory_space=pl.ANY)] * len(ordered)
        + [pl.BlockSpec(memory_space=space)] * len(args)
    )
    skip = len(scalars)
    first = skip + len(ordered)

    def body(*refs):
        if not fetch:
            kernel(*refs[:skip], *refs[first:])
            return
        *refs, sems = refs
        held = refs[len(refs) - len(args) :]
        copies = [
            pltpu.make_async_copy(source, target, sems.at[i])
            for i, (source, target) in enumerate(zip(refs[first : first + len(args)], held))
        ]
        for copy in copies:
            copy.start()
        for copy in copies:
            copy.wait()
        kernel(*refs[:skip], *held, *refs[first + len(args) : len(refs) - len(args)])

    extra = []
    if fetch:
        extra = [pltpu.VMEM(a.shape, a.dtype) for a in args]
        extra.append(pltpu.SemaphoreType.DMA((len(args),)))
    return pl.pallas_call(
        body,
        out_shape=[jax.ShapeDtypeStruct(shape, dtype) for shape, dtype in outs],
        in_specs=in_specs,
        out_specs=[pl.BlockSpec(memory_space=pltpu.VMEM)] * len(outs),
        scratch_shapes=[*scratch, *extra],
        compiler_params=pltpu.CompilerParams(vmem_limit_bytes=14 * 1024 * 1024),
        cost_estimate=pl.CostEstimate(flops=int(flops), bytes_accessed=1, transcendentals=0),
        name=name,
    )(*[s.reshape(1).astype(jnp.int32) for s in scalars], *ordered, *args)


def dot(a, b, over=(1, 0)):
    return lax.dot_general(
        a, b, (((over[0],), (over[1],)), ((), ())), preferred_element_type=F32
    )


def normed(v):
    centered = v - jnp.mean(v, axis=-1, keepdims=True)
    scale = lax.rsqrt(jnp.mean(centered * centered, axis=-1, keepdims=True) + EPS)
    return centered * scale, scale


def norm_back(n, scale, grad):
    mean = jnp.mean(grad, axis=-1, keepdims=True)
    along = jnp.mean(grad * n, axis=-1, keepdims=True)
    return (grad - mean - n * along) * scale


def swap(block, axis, offset):
    count = lax.axis_size(axis)
    return lax.ppermute(block, axis, [(i, i ^ offset) for i in range(count)])


def tp_gather(rows):
    far = swap(rows, "tp", 2)
    near = swap(rows, "tp", 1)
    return [rows, near, far, swap(far, "tp", 1)]


def near_rows_kernel(keep, got, own, out):
    rows = own.shape[0]
    own[...] = keep[:rows].astype(F32) + got[:rows].astype(F32)
    out[...] = (keep[rows:].astype(F32) + got[rows:].astype(F32)).astype(BF)


def tp_scatter(keep, send, ordered=()):
    got = swap(send, "tp", 1)
    rows, cols = keep.shape
    own, out = call(
        near_rows_kernel,
        "near_rows",
        [((rows // 2, cols), F32), ((rows // 2, cols), BF)],
        [keep, got],
        ordered=ordered,
    )
    return [own, swap(out, "tp", 2)]


def put_piece(rank, k, value, keep, send):
    to = jnp.bitwise_xor(rank[0], k)

    @pl.when(to % 2 == 0)
    def _():
        keep[to // 2] = value

    @pl.when(to % 2 == 1)
    def _():
        send[to // 2] = value


def pack_kernel(rank, cond, bias, keep, send, scr):
    count = 2 * keep.shape[0]
    latents = cond.shape[0]
    feat = cond.shape[1] // count
    value = cond[...].astype(F32)
    act = (value / (1.0 + jnp.exp(-value))).astype(BF).astype(F32)
    row = bias[...].astype(F32).reshape(1, bias.shape[0])
    scr[...] = jnp.zeros_like(scr)
    for r in range(bias.shape[0] // feat):
        scr[latents + r : latents + r + 1, 0:feat] = row[:, r * feat : (r + 1) * feat]
    for k in range(count):
        scr[0:latents, 0:feat] = act[:, k * feat : (k + 1) * feat]
        put_piece(rank, k, scr[...], keep, send)


def pair_kernel(keep, got, *outs):
    for z, out in enumerate(outs):
        out[0] = keep[z]
        out[1] = got[z]


def exchange(keep, send, ordered=()):
    size = keep.shape[0]
    piece = keep.shape[1:]
    if size != 4:
        count = 2 * size
        order = jnp.bitwise_xor(jnp.arange(count), lax.axis_index("fsdp"))
        whole = jnp.stack([keep, send], axis=1).reshape(count, *piece)
        got = lax.all_to_all(
            jnp.take(whole, order, axis=0), "fsdp", split_axis=0, concat_axis=0, tiled=True
        )
        return [jnp.take(got, order, axis=0)]
    got = swap(send, "fsdp", 1)
    pairs = call(
        pair_kernel, "pairs", [((2, *piece), keep.dtype)] * size, [keep, got], ordered=ordered
    )
    return [pairs[0]] + [swap(pairs[z], "fsdp", 2 * z) for z in range(1, size)]


def pick(arrays, k):
    per = arrays[0].shape[0]
    return arrays[k // per].at[k % per]


def attn_own_kernel(qkv, proj, out):
    cols = qkv.shape[2]
    for j in range(3):
        out[:, j * cols : (j + 1) * cols] = qkv[j]
    out[:, 3 * cols :] = proj[...].T


def copy_kernel(value, out):
    out[...] = value[...]


def join_kernel(a, b, out):
    half = out.shape[0] // 2
    if len(a.shape) == 2:
        out[0] = a[...]
        out[1] = b[...]
    else:
        out[:half] = a[...]
        out[half:] = b[...]


def join(a, b, ordered=()):
    size = 1 if a.ndim == 2 else a.shape[0]
    shape = (2 * size, *a.shape[-2:])
    return call(join_kernel, "join", [(shape, a.dtype)], [a, b], ordered=ordered)[0]


def gather_steps(own):
    two = join(own, swap(own, "fsdp", 4))
    four = join(two, swap(two, "fsdp", 2))
    return two, four, swap(four, "fsdp", 1)


def mod_kernel(*refs):
    *got, ada, bias, keep, send, cols_out, scr, pieces = refs
    count = pieces.shape[0]
    feat = ada.shape[0]
    latents = scr.shape[0] // count
    for k in range(count):
        scr[k * latents : (k + 1) * latents, :] = pick(got, k)[0:latents, :]
    cols = scr[:, 0:feat].astype(BF)
    cols_out[...] = cols
    width = ada.shape[1] // 6
    pieces[...] = jnp.zeros_like(pieces)
    for j in range(6):
        at = slice(j * width, (j + 1) * width)
        part = dot(cols, ada[:, at]) + bias[:, at]
        for k in range(count):
            for l in range(latents):
                pieces[k, 6 * l + j : 6 * l + j + 1, :] = part[k * latents + l : k * latents + l + 1]
    for place, z in enumerate((0, 2, 1, 3) if count == 8 else range(count // 2)):
        keep[place] = pieces[2 * z].astype(BF)
        send[place] = pieces[2 * z + 1].astype(BF)


def bias_kernel(rank, tp_rank, *refs, latents, feat, tp):
    *got, qkv_out, proj_out, second_out, hidden_out, scr = refs
    count = scr.shape[0]
    for k in range(count):
        scr[jnp.bitwise_xor(rank[0], k)] = pick(got, k)[...]
    per = count // tp
    first = tp_rank[0] * per
    cols = per * feat
    qkv_out[...] = jnp.zeros_like(qkv_out)
    at = latents
    for i in range(per):
        f = first + i
        here = slice(i * feat, (i + 1) * feat)
        qkv_out[0:1, here] = scr[f, at : at + 1, 0:feat]
        qkv_out[0:1, 2 * cols + i * feat : 2 * cols + (i + 1) * feat] = scr[
            f, at + 1 : at + 2, 0:feat
        ]
        for r in range(tp):
            lane = (i * tp + r) * feat
            hidden_out[0:1, lane : lane + feat] = scr[f, at + 4 + r : at + 5 + r, 0:feat]
    for f in range(count):
        here = slice(f * feat, (f + 1) * feat)
        proj_out[0:1, here] = scr[f, at + 2 : at + 3, 0:feat]
        second_out[0:1, here] = scr[f, at + 3 : at + 4, 0:feat]


def assemble_kernel(rank, mine, other, *outs):
    rows = mine.shape[1]
    for i, z in enumerate((0, 2, 1, 3)):
        for x, blocks in enumerate((mine, other)):
            at = jnp.bitwise_xor(rank[0], 2 * z + x) * rows
            at = pl.ds(pl.multiple_of(at, rows), rows)
            lane = 0
            for out in outs:
                out[at, :] = blocks[i, :, lane : lane + out.shape[1]]
                lane += out.shape[1]


def first_norm_kernel(x0, x1, x2, x3, *refs):
    *got, mod_out, out = refs
    mod = got[0][...].astype(F32)
    for part in got[1:]:
        mod = mod + part[...].astype(F32)
    mod = mod.reshape(mod.shape[-2:])
    mod_out[...] = mod[0 : mod_out.shape[0]]
    latents = mod_out.shape[0] // 6
    part = x0.shape[0] // (2 * latents)
    whole = out.shape[0] // latents
    for b, block in enumerate((x0, x1, x2, x3)):
        for l in range(latents):
            n, _ = normed(block[l * part : (l + 1) * part, :].astype(F32))
            shift, scale = mod[6 * l : 6 * l + 1], mod[6 * l + 1 : 6 * l + 2]
            out[l * whole + b * part : l * whole + (b + 1) * part, :] = (
                n * (1.0 + scale) + shift
            ).astype(BF)


def gate_grad_kernel(x0, x1, x2, x3, mod, out, bias_out):
    latents = mod.shape[0] // 6
    rows = x0.shape[0] // 2
    part = rows // latents
    total = jnp.zeros((1, mod.shape[1]), F32)
    for b, block in enumerate((x0, x1, x2, x3)):
        for l in range(latents):
            cot = block[rows + l * part : rows + (l + 1) * part, :].astype(F32)
            value = (cot * mod[6 * l + 5 : 6 * l + 6, :]).astype(BF)
            out[b * rows + l * part : b * rows + (l + 1) * part, :] = value
            if b == 0:
                total = total + jnp.sum(value.astype(F32), axis=0, keepdims=True)
    bias_out[...] = total


def unpack_rows(blocks, rows, latents):
    part = blocks[0].shape[0] // latents
    whole = part * len(blocks)
    for b, block in enumerate(blocks):
        for l in range(latents):
            rows[l * whole + b * part : l * whole + (b + 1) * part, :] = block[
                l * part : (l + 1) * part, :
            ]


def put_parts(value, keep, send, latent):
    part = value.shape[0] // 4
    rows = keep.shape[0] // 2
    for b in range(4):
        out = send if b % 2 else keep
        at = (b // 2) * rows + latent * part
        out[at : at + part, :] = value[b * part : (b + 1) * part]


def softmax(q, k):
    scores = dot(q, k, (1, 1)) * FACTOR
    weights = jnp.exp(scores - jnp.max(scores, axis=-1, keepdims=True))
    return weights * (1.0 / jnp.sum(weights, axis=-1, keepdims=True))


def attn_kernel(rows, qkv_w, proj_w, bias, qkv, att, keep, send, *, latents):
    cols = proj_w.shape[1]
    size = rows.shape[0] // latents
    for l in range(latents):
        here = slice(l * size, (l + 1) * size)
        projected = (dot(rows[here, :], qkv_w[...]) + bias[...]).astype(BF)
        qkv[here, :] = projected
        mixed = []
        for h in range(cols // HEAD):
            q, k, v = [
                projected[:, j * cols + h * HEAD : j * cols + (h + 1) * HEAD] for j in range(3)
            ]
            mixed.append(dot(softmax(q, k).astype(BF), v))
        attended = jnp.concatenate(mixed, axis=1).astype(BF)
        att[here, :] = attended
        put_parts(dot(attended, proj_w[...], (1, 1)).astype(BF), keep, send, l)


def middle_kernel(x, p0, p1, bias, mod, branch_out, middle_out, out):
    latents = mod.shape[0] // 6
    rows = out.shape[0] // latents
    for l in range(latents):
        here = slice(l * rows, (l + 1) * rows)
        branch = bias[...] + p0[here, :] + p1[here, :].astype(F32)
        branch_out[here, :] = branch
        gate = mod[6 * l + 2 : 6 * l + 3, :]
        middle = x[here, :].astype(F32) + gate * branch
        middle_out[here, :] = middle
        n, _ = normed(middle)
        shift = mod[6 * l + 3 : 6 * l + 4, :]
        scale = mod[6 * l + 4 : 6 * l + 5, :]
        out[here, :] = (n * (1.0 + scale) + shift).astype(BF)


def mlp_kernel(
    x0, x1, x2, x3, grads, first, second, bias, act_out, pre_out, x_out, keep, send
):
    rows = x0.shape[0]
    for b, x in enumerate((x0, x1, x2, x3)):
        here = slice(b * rows, (b + 1) * rows)
        x_out[here, :] = x[...]
        v = dot(x[...], first[...]) + bias[...]
        square = v * v
        t = jnp.tanh(CURVE * v * (1.0 + CUBIC * square))
        act_out[here, :] = (0.5 * v * (1.0 + t)).astype(BF)
        slope = 0.5 * (1.0 + t) + 0.5 * v * (1.0 - t * t) * CURVE * (1.0 + 3.0 * CUBIC * square)
        pre = (dot(grads[here, :], second[...]) * slope).astype(BF)
        pre_out[here, :] = pre
        at = (b // 2) * rows
        out = send if b % 2 else keep
        out[at : at + rows, :] = dot(pre, first[...], (1, 1)).astype(BF)


def store_grad(rank, product, keep, send, cols, step):
    rows = keep.shape[1]
    for half in range(2):

        @pl.when((rank[0] // step) % 2 == half)
        def _(half=half):
            for k in range(2 * keep.shape[0]):
                to = jnp.bitwise_xor(rank[0], k)
                if step == 1:
                    place = (to // 2 % 2) * 2 + to // 4
                else:
                    place = (to // 4) * 2 + to % 2
                target = keep if (k // step) % 2 == half else send
                target[place, :, cols] = product[k * rows : (k + 1) * rows]


def mlp_grad_kernel(rank, left, right, keep, send, *bias_out, step):
    product = dot(left[...], right[...], (0, 0)).astype(BF)
    store_grad(rank, product, keep, send, slice(0, right.shape[1]), step)
    if bias_out:
        bias_out[0][...] = jnp.sum(right[...].astype(F32), axis=0, keepdims=True)


def mlp_out_kernel(act, second, keep, send):
    rows = keep.shape[0] // 2
    for b in range(4):
        at = (b // 2) * rows
        out = send if b % 2 else keep
        value = dot(act[b * rows : (b + 1) * rows, :], second[...], (1, 1))
        out[at : at + rows, :] = value.astype(BF)


def output_kernel(middle, x, p0, p1, bias, mod, out, sums):
    latents = mod.shape[0] // 6
    size = middle.shape[0]
    rows = size // latents
    for l in range(latents):
        here = slice(l * rows, (l + 1) * rows)
        branch = bias[...] + p0[here, :] + p1[here, :].astype(F32)
        cot = x[size + l * rows : size + (l + 1) * rows, :].astype(F32)
        out[here, :] = (middle[here, :] + mod[6 * l + 5 : 6 * l + 6, :] * branch).astype(BF)
        sums[l : l + 1, :] = jnp.sum(cot * branch, axis=0, keepdims=True)


def middle_back_kernel(x, middle, branch, p0, p1, mod, grad_out, out, sums):
    latents = mod.shape[0] // 6
    width = middle.shape[1]
    size = middle.shape[0]
    rows = size // latents
    total = jnp.zeros((1, width), F32)
    for l in range(latents):
        here = slice(l * rows, (l + 1) * rows)
        grad = p0[here, :] + p1[here, :].astype(F32)
        cot = x[size + l * rows : size + (l + 1) * rows, :].astype(F32)
        n, scale = normed(middle[here, :])
        sums[3 * l + 1 : 3 * l + 2, :] = jnp.sum(grad, axis=0, keepdims=True)
        sums[3 * l + 2 : 3 * l + 3, :] = jnp.sum(grad * n, axis=0, keepdims=True)
        factor = 1.0 + mod[6 * l + 4 : 6 * l + 5, :]
        whole = cot + norm_back(n, scale, grad * factor)
        grad_out[here, :] = whole
        sums[3 * l : 3 * l + 1, :] = jnp.sum(whole * branch[here, :], axis=0, keepdims=True)
        low = (whole * mod[6 * l + 2 : 6 * l + 3, :]).astype(BF)
        out[here, :] = low
        total = total + jnp.sum(low.astype(F32), axis=0, keepdims=True)
    sums[3 * latents : 3 * latents + 1, :] = total


def attn_back_kernel(
    g0, g1, g2, g3, qkv_w, proj_w, qkv, rows, grads, keep, send, bias_out, *, latents
):
    unpack_rows([g0, g1, g2, g3], rows, latents)
    cols = proj_w.shape[1]
    size = rows.shape[0] // latents
    for l in range(latents):
        here = slice(l * size, (l + 1) * size)
        back = dot(rows[here, :], proj_w[...]).astype(BF)
        projected = qkv[here, :]
        found = [[], [], []]
        for h in range(cols // HEAD):
            q, k, v = [
                projected[:, j * cols + h * HEAD : j * cols + (h + 1) * HEAD] for j in range(3)
            ]
            up = back[:, h * HEAD : (h + 1) * HEAD]
            probs = softmax(q, k)
            grad_probs = dot(up, v, (1, 1))
            inner = jnp.sum(probs * grad_probs, axis=-1, keepdims=True)
            scores = (probs * (grad_probs - inner)).astype(BF)
            found[0].append(dot(scores, k) * FACTOR)
            found[1].append(dot(scores, q, (0, 0)) * FACTOR)
            found[2].append(dot(probs.astype(BF), up, (0, 0)))
        grad = jnp.concatenate(found[0] + found[1] + found[2], axis=1).astype(BF)
        grads[here, :] = grad
        part = jnp.sum(grad.astype(F32), axis=0, keepdims=True)
        total = part if l == 0 else total + part
        put_parts(dot(grad, qkv_w[...], (1, 1)).astype(BF), keep, send, l)
    bias_out[...] = total


def attn_grad_kernel(rank, rows, grads, back, att, keep, send):
    cut = grads.shape[1]
    product = dot(rows[...], grads[...], (0, 0)).astype(BF)
    store_grad(rank, product, keep, send, slice(0, cut), 1)
    product = dot(back[...], att[...], (0, 0)).astype(BF)
    store_grad(rank, product, keep, send, slice(cut, keep.shape[2]), 1)


def input_back_kernel(
    x, grad_middle, p0, p1, mod, sums, gates, fc2, fc1, qkv, out, pack, scr
):
    latents = mod.shape[0] // 6
    rows = out.shape[0] // latents
    cols = qkv.shape[1] // 3
    scr[...] = jnp.zeros_like(scr)
    for l in range(latents):
        here = slice(l * rows, (l + 1) * rows)
        grad = p0[here, :] + p1[here, :].astype(F32)
        n, scale = normed(x[here, :].astype(F32))
        scr[6 * l : 6 * l + 1, :] = jnp.sum(grad, axis=0, keepdims=True)
        scr[6 * l + 1 : 6 * l + 2, :] = jnp.sum(grad * n, axis=0, keepdims=True)
        scr[6 * l + 2 : 6 * l + 5, :] = sums[3 * l : 3 * l + 3, :]
        scr[6 * l + 5 : 6 * l + 6, :] = gates[l : l + 1, :]
        factor = 1.0 + mod[6 * l + 1 : 6 * l + 2, :]
        out[here, :] = grad_middle[here, :] + norm_back(n, scale, grad * factor)
    at = 6 * latents
    scr[at : at + 1, :] = sums[3 * latents : 3 * latents + 1, :]
    scr[at + 1 : at + 2, :] = fc2[...]
    scr[at + 2 : at + 3, :] = fc1[...]
    scr[at + 3 : at + 4, 0:cols] = qkv[:, 0:cols]
    scr[at + 3 : at + 4, cols : 2 * cols] = qkv[:, 2 * cols :]
    pack[...] = scr[...].astype(BF)


def spread_kernel(
    rank, tp_rank, k0, k1, k2, k3, keep, send, parts, total, *, latents, feat
):
    count = 2 * keep.shape[0]
    packs = (k0, k1, k2, k3)
    per = count // len(packs)
    cols = per * feat
    mods = 6 * latents
    summed = jnp.zeros(k0.shape, F32)
    for d, pack in enumerate(packs):
        value = pack[...].astype(F32)
        parts[jnp.bitwise_xor(tp_rank[0], d)] = value
        summed = summed + value
    total[...] = summed
    row = slice(mods, mods + 1)
    total[row, :] = jnp.zeros((1, k0.shape[1]), F32)
    for k in range(count):
        t, i = k // per, k % per
        here = slice(k * feat, (k + 1) * feat)
        total[row, 0:feat] = parts[t, mods + 3 : mods + 4, i * feat : (i + 1) * feat]
        total[row, feat : 2 * feat] = parts[
            t, mods + 3 : mods + 4, cols + i * feat : cols + (i + 1) * feat
        ]
        total[row, 2 * feat : 3 * feat] = summed[mods : mods + 1, here]
        total[row, 3 * feat : 4 * feat] = summed[mods + 1 : mods + 2, here]
        total[row, 4 * feat : 8 * feat] = parts[
            t, mods + 2 : mods + 3, 4 * i * feat : 4 * (i + 1) * feat
        ]
        put_piece(rank, k, total[...].astype(BF), keep, send)


def silu_kernel(*refs, latents):
    *got, ada, keep, send, grads, bias_out, scr, out_scr = refs
    width = ada.shape[1] // 6
    feat = ada.shape[0]
    count = scr.shape[1] // latents
    mods = 6 * latents
    bias = jnp.zeros((1, width), F32)
    for k in range(count):
        value = pick(got, k)[...].astype(F32)
        bias = bias + value[mods : mods + 1]
        for l in range(latents):
            for j in range(6):
                scr[j, k * latents + l : k * latents + l + 1, :] = value[6 * l + j : 6 * l + j + 1]
    bias_out[...] = bias
    total = jnp.zeros((count * latents, feat), F32)
    for j in range(6):
        at = slice(j * width, (j + 1) * width)
        rows = scr[j].astype(BF)
        grads[:, at] = rows
        total = total + dot(rows, ada[:, at], (1, 1))
    out_scr[...] = jnp.zeros_like(out_scr)
    for k in range(count):
        out_scr[k, 0:latents, 0:feat] = total[k * latents : (k + 1) * latents]
    for z in range(count // 2):
        keep[z] = out_scr[2 * z]
        send[z] = out_scr[2 * z + 1]


def cond_kernel(rank, *refs, latents, feat):
    *got, cond, out, scr = refs
    count = scr.shape[0]
    for k in range(count):
        scr[jnp.bitwise_xor(rank[0], k)] = pick(got, k)[...]
    value = cond[...].astype(F32)
    gate = 1.0 / (1.0 + jnp.exp(-value))
    slope = gate * (1.0 + value * (1.0 - gate))
    for k in range(count):
        here = slice(k * feat, (k + 1) * feat)
        out[:, here] = scr[k, 0:latents, 0:feat] * slope[:, here]


def scatter_pieces(keep, send):
    count = 2 * keep.shape[0]
    order = jnp.bitwise_xor(jnp.arange(count), lax.axis_index("fsdp"))
    whole = jnp.stack([keep, send], axis=1).reshape(count, *keep.shape[1:]).astype(F32)
    whole = jnp.take(whole, order, axis=0)
    return lax.psum_scatter(whole, "fsdp", scatter_dimension=0, tiled=False)


def halve_kernel(keep, got, own, out):
    half = own.shape[0]
    for i in range(half):
        own[i] = keep[i].astype(F32) + got[i].astype(F32)
        out[i] = (keep[half + i].astype(F32) + got[half + i].astype(F32)).astype(BF)


def halve(keep, send, offset, ordered=()):
    got = swap(send, "fsdp", offset)
    shape = (keep.shape[0] // 2, *keep.shape[1:])
    outs = [(shape, F32), (shape, BF)]
    return call(halve_kernel, "halve", outs, [keep, got], ordered=ordered)


def add_kernel(own, got, out):
    out[...] = own[...] + got[...].astype(F32)


def last_sum(own, out, offset):
    got = swap(out, "fsdp", offset)
    total = call(add_kernel, "last_sum", [(own.shape, F32)], [own, got])[0]
    return total.reshape(own.shape[1:])


def attn_add_kernel(own, got, qkv, proj):
    cols = qkv.shape[2]
    for j in range(3):
        here = slice(j * cols, (j + 1) * cols)
        qkv[j] = own[0, :, here] + got[0, :, here].astype(F32)
    here = slice(3 * cols, 4 * cols)
    proj[...] = (own[0, :, here] + got[0, :, here].astype(F32)).T


def shards(
    inputs,
    conditioning,
    ada_weight,
    ada_bias,
    query_key_value_weight,
    qv_bias,
    attention_output_weight,
    attention_output_bias,
    expand_weight,
    hidden_layer_bias,
    contract_weight,
    contract_bias,
    out_cotangent,
):
    tp_rank = lax.axis_index("tp")
    tp_count = lax.axis_size("tp")
    rank = lax.axis_index("fsdp")
    count = lax.axis_size("fsdp")
    positions, latents, width = inputs.shape
    feat = ada_weight.shape[0]
    cols = query_key_value_weight.shape[2]
    hidden = expand_weight.shape[1]
    hidden_part = hidden_layer_bias.shape[0]
    mod_part = ada_bias.shape[0]
    rows = positions * latents
    tokens = rows * tp_count
    mods = 6 * latents
    direct = count == 8
    block = ((rows, width), BF)
    block_f32 = ((rows, width), F32)

    qkv_own = query_key_value_weight.transpose(1, 0, 2)
    first_ops = []
    if direct:
        attn_own = call(
            attn_own_kernel,
            "attn_own",
            [((feat, 4 * cols), BF)],
            [qkv_own, attention_output_weight],
            fetch=True,
        )[0]
        first_ops = [attn_own]
        attn_two = join(attn_own, swap(attn_own, "fsdp", 4))

    half = count // 2
    bias_own = jnp.concatenate(
        [qv_bias.reshape(-1), attention_output_bias, contract_bias, hidden_layer_bias]
    )
    cond_keep, cond_send = call(
        pack_kernel,
        "pack_conditioning",
        [((half, 16, 128), F32)] * 2,
        [conditioning, bias_own],
        [rank],
        scratch=[pltpu.VMEM((16, 128), F32)],
        ordered=first_ops,
    )
    cond_got = exchange(cond_keep, cond_send, [attn_two] if direct else ())

    bias_row = lax.dynamic_update_slice(
        jnp.zeros((1, mod_part * count), F32),
        ada_bias.astype(F32).reshape(1, mod_part),
        (0, rank * mod_part),
    )
    mod_keep, mod_send, cond_cols = call(
        mod_kernel,
        "modulation",
        [((half, 16, width), BF)] * 2 + [((count * latents, feat), BF)],
        [*cond_got, ada_weight, bias_row],
        scratch=[
            pltpu.VMEM((count * latents, 128), F32),
            pltpu.VMEM((count, 16, width), F32),
        ],
    )
    x_own = jnp.stack([inputs.transpose(1, 0, 2), out_cotangent.transpose(1, 0, 2)])
    x_own = x_own.reshape(2 * rows, width)
    x_own = call(
        copy_kernel, "tokens", [((2 * rows, width), BF)], [x_own], ordered=cond_got
    )[0]
    x_blocks = tp_gather(x_own)

    if direct:
        attn_four = join(attn_two, swap(attn_two, "fsdp", 2), [mod_send])
        attn_other = swap(attn_four, "fsdp", 1)
        first_own = call(
            copy_kernel,
            "first_own",
            [((feat, hidden), BF)],
            [expand_weight],
            ordered=[attn_four],
            fetch=True,
        )[0]
        first_two, first_four, first_other = gather_steps(first_own)
        second_own = call(
            copy_kernel,
            "second_own",
            [((feat, hidden), BF)],
            [contract_weight.T],
            ordered=[first_four],
            fetch=True,
        )[0]
        second_two, second_four, second_other = gather_steps(second_own)
        qkv_full, proj_full = call(
            assemble_kernel,
            "attn_weights",
            [((width, 3 * cols), BF), ((width, cols), BF)],
            [attn_four, attn_other],
            [rank],
        )
        first_full = call(
            assemble_kernel,
            "first_weights",
            [((width, hidden), BF)],
            [first_four, first_other],
            [rank],
        )[0]
        second_full = call(
            assemble_kernel,
            "second_weights",
            [((width, hidden), BF)],
            [second_four, second_other],
            [rank],
        )[0]
        steps = [[first_four], [], [second_two, first_full], [second_four]]
        half_one = halve(mod_keep, mod_send, 1)
        half_two = halve(*half_one, 2, [first_two])
        mod_parts = [half_two[0], swap(half_two[1], "fsdp", 4)]
    else:
        steps = [[]] * 4
        mod_parts = [scatter_pieces(mod_keep, mod_send)]
        qkv_full = lax.all_gather(
            query_key_value_weight.reshape(feat, 3 * cols), "fsdp", axis=0, tiled=True
        )
        proj_full = lax.all_gather(attention_output_weight.T, "fsdp", axis=0, tiled=True)
        first_full = lax.all_gather(expand_weight, "fsdp", axis=0, tiled=True)
        second_full = lax.all_gather(contract_weight.T, "fsdp", axis=0, tiled=True)

    qkv_bias, proj_bias, second_bias, hidden_bias = call(
        functools.partial(bias_kernel, latents=latents, feat=feat, tp=tp_count),
        "biases",
        [((1, 3 * cols), F32), ((1, width), F32), ((1, width), F32), ((1, hidden), F32)],
        cond_got,
        [rank, tp_rank],
        scratch=[pltpu.VMEM((count, 16, 128), F32)],
        ordered=[mod_send],
        flops=1e9,
    )
    mod, attn_rows = call(
        first_norm_kernel,
        "first_norm",
        [((mods, width), F32), ((tokens, width), BF)],
        [*x_blocks, *mod_parts],
        ordered=[hidden_bias, *steps[0]],
    )
    pair = ((2 * rows, width), BF)
    qkv, att, keep, send = call(
        functools.partial(attn_kernel, latents=latents),
        "attention",
        [((tokens, 3 * cols), BF), ((tokens, cols), BF), pair, pair],
        [attn_rows, qkv_full, proj_full, qkv_bias],
        ordered=steps[1],
    )
    branch_parts = tp_scatter(keep, send, steps[2])
    grad_rows, fc2_part = call(
        gate_grad_kernel,
        "gate_grad",
        [((tokens, width), BF), ((1, width), F32)],
        [*x_blocks, mod],
        ordered=[branch_parts[0]],
        flops=1e9,
    )
    branch, middle, mlp_in = call(
        middle_kernel,
        "middle",
        [block_f32, block_f32, block],
        [x_own, *branch_parts, proj_bias, mod],
        ordered=[fc2_part, *steps[3]],
    )
    m_blocks = tp_gather(mlp_in)
    act, pre, mlp_rows, keep, send = call(
        mlp_kernel,
        "mlp",
        [((tokens, hidden), BF)] * 2 + [((tokens, width), BF), pair, pair],
        [*m_blocks, grad_rows, first_full, second_full, hidden_bias],
    )
    first_done = []
    if direct:
        blocks = [((half, feat, hidden), BF)] * 2
        first_keep, first_send, fc1_part = call(
            functools.partial(mlp_grad_kernel, step=1),
            "first_grad",
            blocks + [((1, hidden), F32)],
            [mlp_rows, pre],
            [rank],
            ordered=[send],
            flops=2e9,
        )
        first_done = [fc1_part]
    grad_in = tp_scatter(keep, send, first_done)
    out_keep, out_send = call(
        mlp_out_kernel,
        "mlp_out",
        [pair, pair],
        [act, second_full],
        ordered=[grad_in[0]],
        flops=1.5e9,
    )
    if direct:
        second_keep, second_send = call(
            functools.partial(mlp_grad_kernel, step=2),
            "second_grad",
            blocks,
            [grad_rows, act],
            [rank],
            ordered=[out_send],
            flops=2e9,
        )
        first_half = halve(first_keep, first_send, 1)
        first_one = halve(*first_half, 2)
        first_sum = last_sum(*first_one, 4)
        second_half = halve(second_keep, second_send, 2)
        second_one = halve(*second_half, 4)
        second_sum = last_sum(*second_one, 1)
        steps = [[first_half[1]], [second_half[1]], [first_one[1]], [second_one[1]]]
    else:
        first_sum = lax.psum_scatter(
            dot(mlp_rows, pre, (0, 0)), "fsdp", scatter_dimension=0, tiled=True
        )
        second_sum = lax.psum_scatter(
            dot(grad_rows, act, (0, 0)), "fsdp", scatter_dimension=0, tiled=True
        )
        fc1_part = jnp.sum(pre.astype(F32), axis=0, keepdims=True)
        steps = [[]] * 4
        second_keep = fc1_part

    grad_middle, grad_attn, sums = call(
        middle_back_kernel,
        "middle_back",
        [block_f32, block, ((8, width), F32)],
        [x_own, middle, branch, *grad_in, mod],
        ordered=[second_keep],
    )
    a_blocks = tp_gather(grad_attn)
    mlp_parts = tp_scatter(out_keep, out_send, [a_blocks[2]])
    back_rows, grads, keep, send, qkv_part = call(
        functools.partial(attn_back_kernel, latents=latents),
        "attention_back",
        [((tokens, width), BF), ((tokens, 3 * cols), BF), pair, pair, ((1, 3 * cols), F32)],
        [*a_blocks, qkv_full, proj_full, qkv],
        ordered=[mlp_parts[0], *steps[0]],
    )
    output, gates = call(
        output_kernel,
        "output",
        [block, ((8, width), F32)],
        [middle, x_own, *mlp_parts, second_bias, mod],
    )
    grad_in = tp_scatter(keep, send, [*steps[1], gates])
    if direct:
        attn_keep, attn_send = call(
            attn_grad_kernel,
            "attn_weight_grad",
            [((half, feat, 4 * cols), BF)] * 2,
            [attn_rows, grads, back_rows, att],
            [rank],
            ordered=[grad_in[0]],
            flops=6e9,
        )
        attn_half = halve(attn_keep, attn_send, 1)
        own, out = halve(*attn_half, 2)
        tail = [[attn_half[1]], [out]]
        qkv_sum, proj_sum = call(
            attn_add_kernel,
            "attn_sum",
            [((3, feat, cols), F32), ((cols, feat), F32)],
            [own, swap(out, "fsdp", 4)],
        )
        qkv_sum = qkv_sum.transpose(1, 0, 2)
    else:
        tail = [[]] * 2
        qkv_sum = lax.psum_scatter(
            dot(attn_rows, grads, (0, 0)), "fsdp", scatter_dimension=0, tiled=True
        ).reshape(feat, 3, cols)
        proj_sum = lax.psum_scatter(
            dot(back_rows, att, (0, 0)), "fsdp", scatter_dimension=0, tiled=True
        ).T

    inputs_grad, pack = call(
        input_back_kernel,
        "input_back",
        [block_f32, ((16, width), BF)],
        [x_own, grad_middle, *grad_in, mod, sums, gates, fc2_part, fc1_part, qkv_part],
        scratch=[pltpu.VMEM((16, width), F32)],
        ordered=steps[2],
    )
    packs = [pack] + [swap(pack, "tp", d) for d in range(1, tp_count)]
    spread_keep, spread_send = call(
        functools.partial(spread_kernel, latents=latents, feat=feat),
        "spread",
        [((half, 16, width), BF)] * 2,
        packs,
        [rank, tp_rank],
        scratch=[pltpu.VMEM((tp_count, 16, width), F32), pltpu.VMEM((16, width), F32)],
    )
    silu_keep, silu_send, grad_mod_all, bias_grads = call(
        functools.partial(silu_kernel, latents=latents),
        "silu_columns",
        [((half, 8, 128), F32)] * 2
        + [((count * latents, 6 * width), BF), ((1, width), F32)],
        [*exchange(spread_keep, spread_send, [*steps[3], *tail[0]]), ada_weight],
        scratch=[
            pltpu.VMEM((6, count * latents, width), F32),
            pltpu.VMEM((count, 8, 128), F32),
        ],
    )
    cond_grad = call(
        functools.partial(cond_kernel, latents=latents, feat=feat),
        "cond_grad",
        [((latents, width), F32)],
        [*exchange(silu_keep, silu_send), conditioning],
        [rank],
        scratch=[pltpu.VMEM((count, 8, 128), F32)],
        ordered=tail[1],
    )[0]
    ada_weight_grad = dot(cond_cols, grad_mod_all, (0, 0))
    bias_grads = bias_grads.reshape(width)
    ada_bias_grad = jnp.sum(
        lax.dynamic_slice_in_dim(grad_mod_all, rank * mod_part, mod_part, 1).astype(F32), axis=0
    )

    return (
        output.reshape(latents, positions, width).transpose(1, 0, 2),
        inputs_grad.reshape(latents, positions, width).transpose(1, 0, 2),
        cond_grad,
        ada_weight_grad,
        ada_bias_grad,
        qkv_sum,
        bias_grads[: 2 * feat].reshape(2, feat),
        proj_sum,
        bias_grads[2 * feat : 3 * feat],
        first_sum,
        bias_grads[4 * feat : 4 * feat + hidden_part],
        second_sum.T,
        bias_grads[3 * feat : 4 * feat],
    )


def solution(mesh):
    return jax.shard_map(
        shards,
        mesh=mesh,
        in_specs=(
            P("tp", "fsdp", None),
            P("fsdp", None),
            P("fsdp", None),
            P("fsdp"),
            P("fsdp", None, "tp"),
            P(None, "fsdp"),
            P("tp", "fsdp"),
            P("fsdp"),
            P("fsdp", "tp"),
            P("fsdp"),
            P("tp", "fsdp"),
            P("fsdp"),
            P("tp", "fsdp", None),
        ),
        out_specs=(
            P("tp", "fsdp", None),
            P("tp", "fsdp", None),
            P("fsdp", None),
            P("fsdp", None),
            P("fsdp"),
            P("fsdp", None, "tp"),
            P(None, "fsdp"),
            P("tp", "fsdp"),
            P("fsdp"),
            P("fsdp", "tp"),
            P("fsdp"),
            P("tp", "fsdp"),
            P("fsdp"),
        ),
        check_vma=False,
    )
```

```python
import functools
import math

import jax
import jax.numpy as jnp
from jax import lax
from jax.experimental import pallas as pl
from jax.experimental.pallas import tpu as pltpu
from jax.sharding import PartitionSpec as P

HEAD = 64
EPS = 1e-06
BF = jnp.bfloat16
F32 = jnp.float32
FACTOR = 1.0 / math.sqrt(HEAD)
CURVE = math.sqrt(2.0 / math.pi)
CUBIC = 0.044715


def call(kernel, name, outs, args, scalars=(), scratch=(), ordered=(), flops=1, fetch=False):
    space = pltpu.HBM if fetch else pltpu.VMEM
    in_specs = (
        [pl.BlockSpec(memory_space=pltpu.SMEM)] * len(scalars)
        + [pl.BlockSpec(memory_space=pl.ANY)] * len(ordered)
        + [pl.BlockSpec(memory_space=space)] * len(args)
    )
    skip = len(scalars)
    first = skip + len(ordered)

    def body(*refs):
        if not fetch:
            kernel(*refs[:skip], *refs[first:])
            return
        *refs, sems = refs
        held = refs[len(refs) - len(args) :]
        copies = [
            pltpu.make_async_copy(source, target, sems.at[i])
            for i, (source, target) in enumerate(zip(refs[first : first + len(args)], held))
        ]
        for copy in copies:
            copy.start()
        for copy in copies:
            copy.wait()
        kernel(*refs[:skip], *held, *refs[first + len(args) : len(refs) - len(args)])

    extra = []
    if fetch:
        extra = [pltpu.VMEM(a.shape, a.dtype) for a in args]
        extra.append(pltpu.SemaphoreType.DMA((len(args),)))
    return pl.pallas_call(
        body,
        out_shape=[jax.ShapeDtypeStruct(shape, dtype) for shape, dtype in outs],
        in_specs=in_specs,
        out_specs=[pl.BlockSpec(memory_space=pltpu.VMEM)] * len(outs),
        scratch_shapes=[*scratch, *extra],
        compiler_params=pltpu.CompilerParams(vmem_limit_bytes=14 * 1024 * 1024),
        cost_estimate=pl.CostEstimate(flops=int(flops), bytes_accessed=1, transcendentals=0),
        name=name,
    )(*[s.reshape(1).astype(jnp.int32) for s in scalars], *ordered, *args)


def dot(a, b, over=(1, 0)):
    return lax.dot_general(
        a, b, (((over[0],), (over[1],)), ((), ())), preferred_element_type=F32
    )


def normed(v):
    centered = v - jnp.mean(v, axis=-1, keepdims=True)
    scale = lax.rsqrt(jnp.mean(centered * centered, axis=-1, keepdims=True) + EPS)
    return centered * scale, scale


def norm_back(n, scale, grad):
    mean = jnp.mean(grad, axis=-1, keepdims=True)
    along = jnp.mean(grad * n, axis=-1, keepdims=True)
    return (grad - mean - n * along) * scale


def swap(block, axis, offset):
    count = lax.axis_size(axis)
    return lax.ppermute(block, axis, [(i, i ^ offset) for i in range(count)])


def tp_gather(rows):
    far = swap(rows, "tp", 2)
    near = swap(rows, "tp", 1)
    return [rows, near, far, swap(far, "tp", 1)]


def near_rows_kernel(keep, got, own, out):
    rows = own.shape[0]
    own[...] = keep[:rows].astype(F32) + got[:rows].astype(F32)
    out[...] = (keep[rows:].astype(F32) + got[rows:].astype(F32)).astype(BF)


def tp_scatter(keep, send, ordered=()):
    got = swap(send, "tp", 1)
    rows, cols = keep.shape
    own, out = call(
        near_rows_kernel,
        "near_rows",
        [((rows // 2, cols), F32), ((rows // 2, cols), BF)],
        [keep, got],
        ordered=ordered,
    )
    return [own, swap(out, "tp", 2)]


def put_piece(rank, k, value, keep, send):
    to = jnp.bitwise_xor(rank[0], k)

    @pl.when(to % 2 == 0)
    def _():
        keep[to // 2] = value

    @pl.when(to % 2 == 1)
    def _():
        send[to // 2] = value


def pack_kernel(rank, cond, bias, keep, send, scr):
    count = 2 * keep.shape[0]
    latents = cond.shape[0]
    feat = cond.shape[1] // count
    value = cond[...].astype(F32)
    act = (value / (1.0 + jnp.exp(-value))).astype(BF).astype(F32)
    row = bias[...].astype(F32).reshape(1, bias.shape[0])
    scr[...] = jnp.zeros_like(scr)
    for r in range(bias.shape[0] // feat):
        scr[latents + r : latents + r + 1, 0:feat] = row[:, r * feat : (r + 1) * feat]
    for k in range(count):
        scr[0:latents, 0:feat] = act[:, k * feat : (k + 1) * feat]
        put_piece(rank, k, scr[...], keep, send)


def pair_kernel(keep, got, *outs):
    for z, out in enumerate(outs):
        out[0] = keep[z]
        out[1] = got[z]


def exchange(keep, send, ordered=()):
    size = keep.shape[0]
    piece = keep.shape[1:]
    if size != 4:
        count = 2 * size
        order = jnp.bitwise_xor(jnp.arange(count), lax.axis_index("fsdp"))
        whole = jnp.stack([keep, send], axis=1).reshape(count, *piece)
        got = lax.all_to_all(
            jnp.take(whole, order, axis=0), "fsdp", split_axis=0, concat_axis=0, tiled=True
        )
        return [jnp.take(got, order, axis=0)]
    got = swap(send, "fsdp", 1)
    pairs = call(
        pair_kernel, "pairs", [((2, *piece), keep.dtype)] * size, [keep, got], ordered=ordered
    )
    return [pairs[0]] + [swap(pairs[z], "fsdp", 2 * z) for z in range(1, size)]


def pick(arrays, k):
    per = arrays[0].shape[0]
    return arrays[k // per].at[k % per]


def attn_own_kernel(qkv, proj, out):
    cols = qkv.shape[2]
    for j in range(3):
        out[:, j * cols : (j + 1) * cols] = qkv[j]
    out[:, 3 * cols :] = proj[...].T


def copy_kernel(value, out):
    out[...] = value[...]


def join_kernel(a, b, out):
    half = out.shape[0] // 2
    if len(a.shape) == 2:
        out[0] = a[...]
        out[1] = b[...]
    else:
        out[:half] = a[...]
        out[half:] = b[...]


def join(a, b, ordered=()):
    size = 1 if a.ndim == 2 else a.shape[0]
    shape = (2 * size, *a.shape[-2:])
    return call(join_kernel, "join", [(shape, a.dtype)], [a, b], ordered=ordered)[0]


def gather_steps(own):
    two = join(own, swap(own, "fsdp", 4))
    four = join(two, swap(two, "fsdp", 2))
    return two, four, swap(four, "fsdp", 1)


def mod_kernel(*refs):
    *got, ada, bias, keep, send, cols_out, scr, pieces = refs
    count = pieces.shape[0]
    feat = ada.shape[0]
    latents = scr.shape[0] // count
    for k in range(count):
        scr[k * latents : (k + 1) * latents, :] = pick(got, k)[0:latents, :]
    cols = scr[:, 0:feat].astype(BF)
    cols_out[...] = cols
    width = ada.shape[1] // 6
    pieces[...] = jnp.zeros_like(pieces)
    for j in range(6):
        at = slice(j * width, (j + 1) * width)
        part = dot(cols, ada[:, at]) + bias[:, at]
        for k in range(count):
            for l in range(latents):
                pieces[k, 6 * l + j : 6 * l + j + 1, :] = part[k * latents + l : k * latents + l + 1]
    for place, z in enumerate((0, 2, 1, 3) if count == 8 else range(count // 2)):
        keep[place] = pieces[2 * z].astype(BF)
        send[place] = pieces[2 * z + 1].astype(BF)


def bias_kernel(rank, tp_rank, *refs, latents, feat, tp):
    *got, qkv_out, proj_out, second_out, hidden_out, scr = refs
    count = scr.shape[0]
    for k in range(count):
        scr[jnp.bitwise_xor(rank[0], k)] = pick(got, k)[...]
    per = count // tp
    first = tp_rank[0] * per
    cols = per * feat
    qkv_out[...] = jnp.zeros_like(qkv_out)
    at = latents
    for i in range(per):
        f = first + i
        here = slice(i * feat, (i + 1) * feat)
        qkv_out[0:1, here] = scr[f, at : at + 1, 0:feat]
        qkv_out[0:1, 2 * cols + i * feat : 2 * cols + (i + 1) * feat] = scr[
            f, at + 1 : at + 2, 0:feat
        ]
        for r in range(tp):
            lane = (i * tp + r) * feat
            hidden_out[0:1, lane : lane + feat] = scr[f, at + 4 + r : at + 5 + r, 0:feat]
    for f in range(count):
        here = slice(f * feat, (f + 1) * feat)
        proj_out[0:1, here] = scr[f, at + 2 : at + 3, 0:feat]
        second_out[0:1, here] = scr[f, at + 3 : at + 4, 0:feat]


def assemble_kernel(rank, mine, other, *outs):
    rows = mine.shape[1]
    for i, z in enumerate((0, 2, 1, 3)):
        for x, blocks in enumerate((mine, other)):
            at = jnp.bitwise_xor(rank[0], 2 * z + x) * rows
            at = pl.ds(pl.multiple_of(at, rows), rows)
            lane = 0
            for out in outs:
                out[at, :] = blocks[i, :, lane : lane + out.shape[1]]
                lane += out.shape[1]


def first_norm_kernel(x0, x1, x2, x3, *refs):
    *got, mod_out, out = refs
    mod = got[0][...].astype(F32)
    for part in got[1:]:
        mod = mod + part[...].astype(F32)
    mod = mod.reshape(mod.shape[-2:])
    mod_out[...] = mod[0 : mod_out.shape[0]]
    latents = mod_out.shape[0] // 6
    part = x0.shape[0] // (2 * latents)
    whole = out.shape[0] // latents
    for b, block in enumerate((x0, x1, x2, x3)):
        for l in range(latents):
            n, _ = normed(block[l * part : (l + 1) * part, :].astype(F32))
            shift, scale = mod[6 * l : 6 * l + 1], mod[6 * l + 1 : 6 * l + 2]
            out[l * whole + b * part : l * whole + (b + 1) * part, :] = (
                n * (1.0 + scale) + shift
            ).astype(BF)


def gate_grad_kernel(x0, x1, x2, x3, mod, out, bias_out):
    latents = mod.shape[0] // 6
    rows = x0.shape[0] // 2
    part = rows // latents
    total = jnp.zeros((1, mod.shape[1]), F32)
    for b, block in enumerate((x0, x1, x2, x3)):
        for l in range(latents):
            cot = block[rows + l * part : rows + (l + 1) * part, :].astype(F32)
            value = (cot * mod[6 * l + 5 : 6 * l + 6, :]).astype(BF)
            out[b * rows + l * part : b * rows + (l + 1) * part, :] = value
            if b == 0:
                total = total + jnp.sum(value.astype(F32), axis=0, keepdims=True)
    bias_out[...] = total


def unpack_rows(blocks, rows, latents):
    part = blocks[0].shape[0] // latents
    whole = part * len(blocks)
    for b, block in enumerate(blocks):
        for l in range(latents):
            rows[l * whole + b * part : l * whole + (b + 1) * part, :] = block[
                l * part : (l + 1) * part, :
            ]


def put_parts(value, keep, send, latent):
    part = value.shape[0] // 4
    rows = keep.shape[0] // 2
    for b in range(4):
        out = send if b % 2 else keep
        at = (b // 2) * rows + latent * part
        out[at : at + part, :] = value[b * part : (b + 1) * part]


def softmax(q, k):
    scores = dot(q, k, (1, 1)) * FACTOR
    weights = jnp.exp(scores - jnp.max(scores, axis=-1, keepdims=True))
    return weights * (1.0 / jnp.sum(weights, axis=-1, keepdims=True))


def attn_kernel(rows, qkv_w, proj_w, bias, qkv, att, keep, send, *, latents):
    cols = proj_w.shape[1]
    size = rows.shape[0] // latents
    for l in range(latents):
        here = slice(l * size, (l + 1) * size)
        projected = (dot(rows[here, :], qkv_w[...]) + bias[...]).astype(BF)
        qkv[here, :] = projected
        mixed = []
        for h in range(cols // HEAD):
            q, k, v = [
                projected[:, j * cols + h * HEAD : j * cols + (h + 1) * HEAD] for j in range(3)
            ]
            mixed.append(dot(softmax(q, k).astype(BF), v))
        attended = jnp.concatenate(mixed, axis=1).astype(BF)
        att[here, :] = attended
        put_parts(dot(attended, proj_w[...], (1, 1)).astype(BF), keep, send, l)


def middle_kernel(x, p0, p1, bias, mod, branch_out, middle_out, out):
    latents = mod.shape[0] // 6
    rows = out.shape[0] // latents
    for l in range(latents):
        here = slice(l * rows, (l + 1) * rows)
        branch = bias[...] + p0[here, :] + p1[here, :].astype(F32)
        branch_out[here, :] = branch
        gate = mod[6 * l + 2 : 6 * l + 3, :]
        middle = x[here, :].astype(F32) + gate * branch
        middle_out[here, :] = middle
        n, _ = normed(middle)
        shift = mod[6 * l + 3 : 6 * l + 4, :]
        scale = mod[6 * l + 4 : 6 * l + 5, :]
        out[here, :] = (n * (1.0 + scale) + shift).astype(BF)


def mlp_kernel(
    x0, x1, x2, x3, grads, first, second, bias, act_out, pre_out, x_out, keep, send
):
    rows = x0.shape[0]
    for b, x in enumerate((x0, x1, x2, x3)):
        here = slice(b * rows, (b + 1) * rows)
        x_out[here, :] = x[...]
        v = dot(x[...], first[...]) + bias[...]
        square = v * v
        t = jnp.tanh(CURVE * v * (1.0 + CUBIC * square))
        act_out[here, :] = (0.5 * v * (1.0 + t)).astype(BF)
        slope = 0.5 * (1.0 + t) + 0.5 * v * (1.0 - t * t) * CURVE * (1.0 + 3.0 * CUBIC * square)
        pre = (dot(grads[here, :], second[...]) * slope).astype(BF)
        pre_out[here, :] = pre
        at = (b // 2) * rows
        out = send if b % 2 else keep
        out[at : at + rows, :] = dot(pre, first[...], (1, 1)).astype(BF)


def store_grad(rank, product, keep, send, cols, step):
    rows = keep.shape[1]
    for half in range(2):

        @pl.when((rank[0] // step) % 2 == half)
        def _(half=half):
            for k in range(2 * keep.shape[0]):
                to = jnp.bitwise_xor(rank[0], k)
                if step == 1:
                    place = (to // 2 % 2) * 2 + to // 4
                else:
                    place = (to // 4) * 2 + to % 2
                target = keep if (k // step) % 2 == half else send
                target[place, :, cols] = product[k * rows : (k + 1) * rows]


def mlp_grad_kernel(rank, left, right, keep, send, *bias_out, step):
    product = dot(left[...], right[...], (0, 0)).astype(BF)
    store_grad(rank, product, keep, send, slice(0, right.shape[1]), step)
    if bias_out:
        bias_out[0][...] = jnp.sum(right[...].astype(F32), axis=0, keepdims=True)


def mlp_out_kernel(act, second, keep, send):
    rows = keep.shape[0] // 2
    for b in range(4):
        at = (b // 2) * rows
        out = send if b % 2 else keep
        value = dot(act[b * rows : (b + 1) * rows, :], second[...], (1, 1))
        out[at : at + rows, :] = value.astype(BF)


def output_kernel(middle, x, p0, p1, bias, mod, out, sums):
    latents = mod.shape[0] // 6
    size = middle.shape[0]
    rows = size // latents
    for l in range(latents):
        here = slice(l * rows, (l + 1) * rows)
        branch = bias[...] + p0[here, :] + p1[here, :].astype(F32)
        cot = x[size + l * rows : size + (l + 1) * rows, :].astype(F32)
        out[here, :] = (middle[here, :] + mod[6 * l + 5 : 6 * l + 6, :] * branch).astype(BF)
        sums[l : l + 1, :] = jnp.sum(cot * branch, axis=0, keepdims=True)


def middle_back_kernel(x, middle, branch, p0, p1, mod, grad_out, out, sums):
    latents = mod.shape[0] // 6
    width = middle.shape[1]
    size = middle.shape[0]
    rows = size // latents
    total = jnp.zeros((1, width), F32)
    for l in range(latents):
        here = slice(l * rows, (l + 1) * rows)
        grad = p0[here, :] + p1[here, :].astype(F32)
        cot = x[size + l * rows : size + (l + 1) * rows, :].astype(F32)
        n, scale = normed(middle[here, :])
        sums[3 * l + 1 : 3 * l + 2, :] = jnp.sum(grad, axis=0, keepdims=True)
        sums[3 * l + 2 : 3 * l + 3, :] = jnp.sum(grad * n, axis=0, keepdims=True)
        factor = 1.0 + mod[6 * l + 4 : 6 * l + 5, :]
        whole = cot + norm_back(n, scale, grad * factor)
        grad_out[here, :] = whole
        sums[3 * l : 3 * l + 1, :] = jnp.sum(whole * branch[here, :], axis=0, keepdims=True)
        low = (whole * mod[6 * l + 2 : 6 * l + 3, :]).astype(BF)
        out[here, :] = low
        total = total + jnp.sum(low.astype(F32), axis=0, keepdims=True)
    sums[3 * latents : 3 * latents + 1, :] = total


def attn_back_kernel(
    g0, g1, g2, g3, qkv_w, proj_w, qkv, rows, grads, keep, send, bias_out, *, latents
):
    unpack_rows([g0, g1, g2, g3], rows, latents)
    cols = proj_w.shape[1]
    size = rows.shape[0] // latents
    for l in range(latents):
        here = slice(l * size, (l + 1) * size)
        back = dot(rows[here, :], proj_w[...]).astype(BF)
        projected = qkv[here, :]
        found = [[], [], []]
        for h in range(cols // HEAD):
            q, k, v = [
                projected[:, j * cols + h * HEAD : j * cols + (h + 1) * HEAD] for j in range(3)
            ]
            up = back[:, h * HEAD : (h + 1) * HEAD]
            probs = softmax(q, k)
            grad_probs = dot(up, v, (1, 1))
            inner = jnp.sum(probs * grad_probs, axis=-1, keepdims=True)
            scores = (probs * (grad_probs - inner)).astype(BF)
            found[0].append(dot(scores, k) * FACTOR)
            found[1].append(dot(scores, q, (0, 0)) * FACTOR)
            found[2].append(dot(probs.astype(BF), up, (0, 0)))
        grad = jnp.concatenate(found[0] + found[1] + found[2], axis=1).astype(BF)
        grads[here, :] = grad
        part = jnp.sum(grad.astype(F32), axis=0, keepdims=True)
        total = part if l == 0 else total + part
        put_parts(dot(grad, qkv_w[...], (1, 1)).astype(BF), keep, send, l)
    bias_out[...] = total


def attn_grad_kernel(rank, rows, grads, back, att, keep, send):
    cut = grads.shape[1]
    product = dot(rows[...], grads[...], (0, 0)).astype(BF)
    store_grad(rank, product, keep, send, slice(0, cut), 1)
    product = dot(back[...], att[...], (0, 0)).astype(BF)
    store_grad(rank, product, keep, send, slice(cut, keep.shape[2]), 1)


def input_back_kernel(
    x, grad_middle, p0, p1, mod, sums, gates, fc2, fc1, qkv, out, pack, scr
):
    latents = mod.shape[0] // 6
    rows = out.shape[0] // latents
    cols = qkv.shape[1] // 3
    scr[...] = jnp.zeros_like(scr)
    for l in range(latents):
        here = slice(l * rows, (l + 1) * rows)
        grad = p0[here, :] + p1[here, :].astype(F32)
        n, scale = normed(x[here, :].astype(F32))
        scr[6 * l : 6 * l + 1, :] = jnp.sum(grad, axis=0, keepdims=True)
        scr[6 * l + 1 : 6 * l + 2, :] = jnp.sum(grad * n, axis=0, keepdims=True)
        scr[6 * l + 2 : 6 * l + 5, :] = sums[3 * l : 3 * l + 3, :]
        scr[6 * l + 5 : 6 * l + 6, :] = gates[l : l + 1, :]
        factor = 1.0 + mod[6 * l + 1 : 6 * l + 2, :]
        out[here, :] = grad_middle[here, :] + norm_back(n, scale, grad * factor)
    at = 6 * latents
    scr[at : at + 1, :] = sums[3 * latents : 3 * latents + 1, :]
    scr[at + 1 : at + 2, :] = fc2[...]
    scr[at + 2 : at + 3, :] = fc1[...]
    scr[at + 3 : at + 4, 0:cols] = qkv[:, 0:cols]
    scr[at + 3 : at + 4, cols : 2 * cols] = qkv[:, 2 * cols :]
    pack[...] = scr[...].astype(BF)


def spread_kernel(
    rank, tp_rank, k0, k1, k2, k3, keep, send, parts, total, *, latents, feat
):
    count = 2 * keep.shape[0]
    packs = (k0, k1, k2, k3)
    per = count // len(packs)
    cols = per * feat
    mods = 6 * latents
    summed = jnp.zeros(k0.shape, F32)
    for d, pack in enumerate(packs):
        value = pack[...].astype(F32)
        parts[jnp.bitwise_xor(tp_rank[0], d)] = value
        summed = summed + value
    total[...] = summed
    row = slice(mods, mods + 1)
    total[row, :] = jnp.zeros((1, k0.shape[1]), F32)
    for k in range(count):
        t, i = k // per, k % per
        here = slice(k * feat, (k + 1) * feat)
        total[row, 0:feat] = parts[t, mods + 3 : mods + 4, i * feat : (i + 1) * feat]
        total[row, feat : 2 * feat] = parts[
            t, mods + 3 : mods + 4, cols + i * feat : cols + (i + 1) * feat
        ]
        total[row, 2 * feat : 3 * feat] = summed[mods : mods + 1, here]
        total[row, 3 * feat : 4 * feat] = summed[mods + 1 : mods + 2, here]
        total[row, 4 * feat : 8 * feat] = parts[
            t, mods + 2 : mods + 3, 4 * i * feat : 4 * (i + 1) * feat
        ]
        put_piece(rank, k, total[...].astype(BF), keep, send)


def silu_kernel(*refs, latents):
    *got, ada, keep, send, grads, bias_out, scr, out_scr = refs
    width = ada.shape[1] // 6
    feat = ada.shape[0]
    count = scr.shape[1] // latents
    mods = 6 * latents
    bias = jnp.zeros((1, width), F32)
    for k in range(count):
        value = pick(got, k)[...].astype(F32)
        bias = bias + value[mods : mods + 1]
        for l in range(latents):
            for j in range(6):
                scr[j, k * latents + l : k * latents + l + 1, :] = value[6 * l + j : 6 * l + j + 1]
    bias_out[...] = bias
    total = jnp.zeros((count * latents, feat), F32)
    for j in range(6):
        at = slice(j * width, (j + 1) * width)
        rows = scr[j].astype(BF)
        grads[:, at] = rows
        total = total + dot(rows, ada[:, at], (1, 1))
    out_scr[...] = jnp.zeros_like(out_scr)
    for k in range(count):
        out_scr[k, 0:latents, 0:feat] = total[k * latents : (k + 1) * latents]
    for z in range(count // 2):
        keep[z] = out_scr[2 * z]
        send[z] = out_scr[2 * z + 1]


def cond_kernel(rank, *refs, latents, feat):
    *got, cond, out, scr = refs
    count = scr.shape[0]
    for k in range(count):
        scr[jnp.bitwise_xor(rank[0], k)] = pick(got, k)[...]
    value = cond[...].astype(F32)
    gate = 1.0 / (1.0 + jnp.exp(-value))
    slope = gate * (1.0 + value * (1.0 - gate))
    for k in range(count):
        here = slice(k * feat, (k + 1) * feat)
        out[:, here] = scr[k, 0:latents, 0:feat] * slope[:, here]


def scatter_pieces(keep, send):
    count = 2 * keep.shape[0]
    order = jnp.bitwise_xor(jnp.arange(count), lax.axis_index("fsdp"))
    whole = jnp.stack([keep, send], axis=1).reshape(count, *keep.shape[1:]).astype(F32)
    whole = jnp.take(whole, order, axis=0)
    return lax.psum_scatter(whole, "fsdp", scatter_dimension=0, tiled=False)


def halve_kernel(keep, got, own, out):
    half = own.shape[0]
    for i in range(half):
        own[i] = keep[i].astype(F32) + got[i].astype(F32)
        out[i] = (keep[half + i].astype(F32) + got[half + i].astype(F32)).astype(BF)


def halve(keep, send, offset, ordered=()):
    got = swap(send, "fsdp", offset)
    shape = (keep.shape[0] // 2, *keep.shape[1:])
    outs = [(shape, F32), (shape, BF)]
    return call(halve_kernel, "halve", outs, [keep, got], ordered=ordered)


def add_kernel(own, got, out):
    out[...] = own[...] + got[...].astype(F32)


def last_sum(own, out, offset):
    got = swap(out, "fsdp", offset)
    total = call(add_kernel, "last_sum", [(own.shape, F32)], [own, got])[0]
    return total.reshape(own.shape[1:])


def attn_add_kernel(own, got, qkv, proj):
    cols = qkv.shape[2]
    for j in range(3):
        here = slice(j * cols, (j + 1) * cols)
        qkv[j] = own[0, :, here] + got[0, :, here].astype(F32)
    here = slice(3 * cols, 4 * cols)
    proj[...] = (own[0, :, here] + got[0, :, here].astype(F32)).T


def shards(
    inputs,
    conditioning,
    ada_weight,
    ada_bias,
    query_key_value_weight,
    qv_bias,
    attention_output_weight,
    attention_output_bias,
    expand_weight,
    hidden_layer_bias,
    contract_weight,
    contract_bias,
    out_cotangent,
):
    tp_rank = lax.axis_index("tp")
    tp_count = lax.axis_size("tp")
    rank = lax.axis_index("fsdp")
    count = lax.axis_size("fsdp")
    positions, latents, width = inputs.shape
    feat = ada_weight.shape[0]
    cols = query_key_value_weight.shape[2]
    hidden = expand_weight.shape[1]
    hidden_part = hidden_layer_bias.shape[0]
    mod_part = ada_bias.shape[0]
    rows = positions * latents
    tokens = rows * tp_count
    mods = 6 * latents
    direct = count == 8
    block = ((rows, width), BF)
    block_f32 = ((rows, width), F32)

    qkv_own = query_key_value_weight.transpose(1, 0, 2)
    first_ops = []
    if direct:
        attn_own = call(
            attn_own_kernel,
            "attn_own",
            [((feat, 4 * cols), BF)],
            [qkv_own, attention_output_weight],
            fetch=True,
        )[0]
        first_ops = [attn_own]
        attn_two = join(attn_own, swap(attn_own, "fsdp", 4))

    half = count // 2
    bias_own = jnp.concatenate(
        [qv_bias.reshape(-1), attention_output_bias, contract_bias, hidden_layer_bias]
    )
    cond_keep, cond_send = call(
        pack_kernel,
        "pack_conditioning",
        [((half, 16, 128), F32)] * 2,
        [conditioning, bias_own],
        [rank],
        scratch=[pltpu.VMEM((16, 128), F32)],
        ordered=first_ops,
    )
    cond_got = exchange(cond_keep, cond_send, [attn_two] if direct else ())

    bias_row = lax.dynamic_update_slice(
        jnp.zeros((1, mod_part * count), F32),
        ada_bias.astype(F32).reshape(1, mod_part),
        (0, rank * mod_part),
    )
    mod_keep, mod_send, cond_cols = call(
        mod_kernel,
        "modulation",
        [((half, 16, width), BF)] * 2 + [((count * latents, feat), BF)],
        [*cond_got, ada_weight, bias_row],
        scratch=[
            pltpu.VMEM((count * latents, 128), F32),
            pltpu.VMEM((count, 16, width), F32),
        ],
    )
    x_own = jnp.stack([inputs.transpose(1, 0, 2), out_cotangent.transpose(1, 0, 2)])
    x_own = x_own.reshape(2 * rows, width)
    x_own = call(
        copy_kernel, "tokens", [((2 * rows, width), BF)], [x_own], ordered=cond_got
    )[0]
    x_blocks = tp_gather(x_own)

    if direct:
        half_one = halve(mod_keep, mod_send, 1)
        half_two = halve(*half_one, 2)
        mod_parts = [half_two[0], swap(half_two[1], "fsdp", 4)]
        attn_four = join(attn_two, swap(attn_two, "fsdp", 2), [mod_send])
        attn_other = swap(attn_four, "fsdp", 1)
        first_own = call(
            copy_kernel,
            "first_own",
            [((feat, hidden), BF)],
            [expand_weight],
            ordered=[half_two[1]],
            fetch=True,
        )[0]
        first_two, first_four, first_other = gather_steps(first_own)
        second_own = call(
            copy_kernel,
            "second_own",
            [((feat, hidden), BF)],
            [contract_weight.T],
            ordered=[first_four],
            fetch=True,
        )[0]
        second_two, second_four, second_other = gather_steps(second_own)
        qkv_full, proj_full = call(
            assemble_kernel,
            "attn_weights",
            [((width, 3 * cols), BF), ((width, cols), BF)],
            [attn_four, attn_other],
            [rank],
        )
        first_full = call(
            assemble_kernel,
            "first_weights",
            [((width, hidden), BF)],
            [first_four, first_other],
            [rank],
        )[0]
        second_full = call(
            assemble_kernel,
            "second_weights",
            [((width, hidden), BF)],
            [second_four, second_other],
            [rank],
        )[0]
        steps = [[attn_four], [first_two], [first_four], [second_two], [second_four, first_full]]
    else:
        steps = [[]] * 5
        mod_parts = [scatter_pieces(mod_keep, mod_send)]
        qkv_full = lax.all_gather(
            query_key_value_weight.reshape(feat, 3 * cols), "fsdp", axis=0, tiled=True
        )
        proj_full = lax.all_gather(attention_output_weight.T, "fsdp", axis=0, tiled=True)
        first_full = lax.all_gather(expand_weight, "fsdp", axis=0, tiled=True)
        second_full = lax.all_gather(contract_weight.T, "fsdp", axis=0, tiled=True)

    qkv_bias, proj_bias, second_bias, hidden_bias = call(
        functools.partial(bias_kernel, latents=latents, feat=feat, tp=tp_count),
        "biases",
        [((1, 3 * cols), F32), ((1, width), F32), ((1, width), F32), ((1, hidden), F32)],
        cond_got,
        [rank, tp_rank],
        scratch=[pltpu.VMEM((count, 16, 128), F32)],
        ordered=[mod_send],
        flops=1e9,
    )
    mod, attn_rows = call(
        first_norm_kernel,
        "first_norm",
        [((mods, width), F32), ((tokens, width), BF)],
        [*x_blocks, *mod_parts],
        ordered=[hidden_bias, *steps[0]],
    )
    pair = ((2 * rows, width), BF)
    qkv, att, keep, send = call(
        functools.partial(attn_kernel, latents=latents),
        "attention",
        [((tokens, 3 * cols), BF), ((tokens, cols), BF), pair, pair],
        [attn_rows, qkv_full, proj_full, qkv_bias],
        ordered=steps[1],
    )
    branch_parts = tp_scatter(keep, send, steps[2])
    grad_rows, fc2_part = call(
        gate_grad_kernel,
        "gate_grad",
        [((tokens, width), BF), ((1, width), F32)],
        [*x_blocks, mod],
        ordered=[branch_parts[0], *steps[3]],
        flops=1e9,
    )
    branch, middle, mlp_in = call(
        middle_kernel,
        "middle",
        [block_f32, block_f32, block],
        [x_own, *branch_parts, proj_bias, mod],
        ordered=[fc2_part, *steps[4]],
    )
    m_blocks = tp_gather(mlp_in)
    act, pre, mlp_rows, keep, send = call(
        mlp_kernel,
        "mlp",
        [((tokens, hidden), BF)] * 2 + [((tokens, width), BF), pair, pair],
        [*m_blocks, grad_rows, first_full, second_full, hidden_bias],
    )
    first_done = []
    if direct:
        blocks = [((half, feat, hidden), BF)] * 2
        first_keep, first_send, fc1_part = call(
            functools.partial(mlp_grad_kernel, step=1),
            "first_grad",
            blocks + [((1, hidden), F32)],
            [mlp_rows, pre],
            [rank],
            ordered=[send],
            flops=2e9,
        )
        first_done = [fc1_part]
    grad_in = tp_scatter(keep, send, first_done)
    out_keep, out_send = call(
        mlp_out_kernel,
        "mlp_out",
        [pair, pair],
        [act, second_full],
        ordered=[grad_in[0]],
        flops=1.5e9,
    )
    if direct:
        second_keep, second_send = call(
            functools.partial(mlp_grad_kernel, step=1),
            "second_grad",
            blocks,
            [grad_rows, act],
            [rank],
            ordered=[out_send],
            flops=2e9,
        )
        first_half = halve(first_keep, first_send, 1)
        second_sent = call(
            copy_kernel, "second_sent", blocks[:1], [second_send], ordered=[first_half[1]]
        )[0]
        steps = [[first_half[1], second_sent]]
    else:
        first_sum = lax.psum_scatter(
            dot(mlp_rows, pre, (0, 0)), "fsdp", scatter_dimension=0, tiled=True
        )
        second_sum = lax.psum_scatter(
            dot(grad_rows, act, (0, 0)), "fsdp", scatter_dimension=0, tiled=True
        )
        fc1_part = jnp.sum(pre.astype(F32), axis=0, keepdims=True)
        steps = [[]]
        second_keep = fc1_part

    grad_middle, grad_attn, sums = call(
        middle_back_kernel,
        "middle_back",
        [block_f32, block, ((8, width), F32)],
        [x_own, middle, branch, *grad_in, mod],
        ordered=[second_keep],
    )
    a_blocks = tp_gather(grad_attn)
    mlp_parts = tp_scatter(out_keep, out_send, [a_blocks[2]])
    back_rows, grads, keep, send, qkv_part = call(
        functools.partial(attn_back_kernel, latents=latents),
        "attention_back",
        [((tokens, width), BF), ((tokens, 3 * cols), BF), pair, pair, ((1, 3 * cols), F32)],
        [*a_blocks, qkv_full, proj_full, qkv],
        ordered=[mlp_parts[0], *steps[0]],
    )
    output, gates = call(
        output_kernel,
        "output",
        [block, ((8, width), F32)],
        [middle, x_own, *mlp_parts, second_bias, mod],
    )
    grad_in = tp_scatter(keep, send, [gates])
    if direct:
        attn_keep, attn_send = call(
            attn_grad_kernel,
            "attn_weight_grad",
            [((half, feat, 4 * cols), BF)] * 2,
            [attn_rows, grads, back_rows, att],
            [rank],
            ordered=[grad_in[0]],
            flops=6e9,
        )
    else:
        qkv_sum = lax.psum_scatter(
            dot(attn_rows, grads, (0, 0)), "fsdp", scatter_dimension=0, tiled=True
        ).reshape(feat, 3, cols)
        proj_sum = lax.psum_scatter(
            dot(back_rows, att, (0, 0)), "fsdp", scatter_dimension=0, tiled=True
        ).T

    inputs_grad, pack = call(
        input_back_kernel,
        "input_back",
        [block_f32, ((16, width), BF)],
        [x_own, grad_middle, *grad_in, mod, sums, gates, fc2_part, fc1_part, qkv_part],
        scratch=[pltpu.VMEM((16, width), F32)],
    )
    tail = [[]] * 3
    if direct:
        first_one = halve(*first_half, 2, [pack])
        first_sum = last_sum(*first_one, 4)
        second_half = halve(second_keep, second_sent, 1, [pack])
        tail[0] = [first_one[1], second_half[1]]
    packs = [pack] + [swap(pack, "tp", d) for d in range(1, tp_count)]
    spread_keep, spread_send = call(
        functools.partial(spread_kernel, latents=latents, feat=feat),
        "spread",
        [((half, 16, width), BF)] * 2,
        packs,
        [rank, tp_rank],
        scratch=[pltpu.VMEM((tp_count, 16, width), F32), pltpu.VMEM((16, width), F32)],
        ordered=tail[0],
    )
    if direct:
        attn_half = halve(attn_keep, attn_send, 1, [spread_send])
        attn_own_sum, attn_out = halve(*attn_half, 2)
        qkv_sum, proj_sum = call(
            attn_add_kernel,
            "attn_sum",
            [((3, feat, cols), F32), ((cols, feat), F32)],
            [attn_own_sum, swap(attn_out, "fsdp", 4)],
        )
        qkv_sum = qkv_sum.transpose(1, 0, 2)
        second_one = halve(*second_half, 2, [spread_send])
        second_sum = last_sum(*second_one, 4)
        tail[1] = [attn_half[1], second_one[1]]
        tail[2] = [attn_out]
    silu_keep, silu_send, grad_mod_all, bias_grads = call(
        functools.partial(silu_kernel, latents=latents),
        "silu_columns",
        [((half, 8, 128), F32)] * 2
        + [((count * latents, 6 * width), BF), ((1, width), F32)],
        [*exchange(spread_keep, spread_send, tail[1]), ada_weight],
        scratch=[
            pltpu.VMEM((6, count * latents, width), F32),
            pltpu.VMEM((count, 8, 128), F32),
        ],
    )
    cond_grad = call(
        functools.partial(cond_kernel, latents=latents, feat=feat),
        "cond_grad",
        [((latents, width), F32)],
        [*exchange(silu_keep, silu_send, tail[2]), conditioning],
        [rank],
        scratch=[pltpu.VMEM((count, 8, 128), F32)],
    )[0]
    ada_weight_grad = dot(cond_cols, grad_mod_all, (0, 0))
    bias_grads = bias_grads.reshape(width)
    ada_bias_grad = jnp.sum(
        lax.dynamic_slice_in_dim(grad_mod_all, rank * mod_part, mod_part, 1).astype(F32), axis=0
    )

    return (
        output.reshape(latents, positions, width).transpose(1, 0, 2),
        inputs_grad.reshape(latents, positions, width).transpose(1, 0, 2),
        cond_grad,
        ada_weight_grad,
        ada_bias_grad,
        qkv_sum,
        bias_grads[: 2 * feat].reshape(2, feat),
        proj_sum,
        bias_grads[2 * feat : 3 * feat],
        first_sum,
        bias_grads[4 * feat : 4 * feat + hidden_part],
        second_sum.T,
        bias_grads[3 * feat : 4 * feat],
    )


def solution(mesh):
    return jax.shard_map(
        shards,
        mesh=mesh,
        in_specs=(
            P("tp", "fsdp", None),
            P("fsdp", None),
            P("fsdp", None),
            P("fsdp"),
            P("fsdp", None, "tp"),
            P(None, "fsdp"),
            P("tp", "fsdp"),
            P("fsdp"),
            P("fsdp", "tp"),
            P("fsdp"),
            P("tp", "fsdp"),
            P("fsdp"),
            P("tp", "fsdp", None),
        ),
        out_specs=(
            P("tp", "fsdp", None),
            P("tp", "fsdp", None),
            P("fsdp", None),
            P("fsdp", None),
            P("fsdp"),
            P("fsdp", None, "tp"),
            P(None, "fsdp"),
            P("tp", "fsdp"),
            P("fsdp"),
            P("fsdp", "tp"),
            P("fsdp"),
            P("tp", "fsdp"),
            P("fsdp"),
        ),
        check_vma=False,
    )
```

```python
import functools
import math

import jax
import jax.numpy as jnp
from jax import lax
from jax.experimental import pallas as pl
from jax.experimental.pallas import tpu as pltpu
from jax.sharding import PartitionSpec as P

HEAD = 64
EPS = 1e-06
BF = jnp.bfloat16
F32 = jnp.float32
FACTOR = 1.0 / math.sqrt(HEAD)
CURVE = math.sqrt(2.0 / math.pi)
CUBIC = 0.044715


def call(kernel, name, outs, args, scalars=(), scratch=(), ordered=(), flops=1, fetch=False):
    space = pltpu.HBM if fetch else pltpu.VMEM
    in_specs = (
        [pl.BlockSpec(memory_space=pltpu.SMEM)] * len(scalars)
        + [pl.BlockSpec(memory_space=pl.ANY)] * len(ordered)
        + [pl.BlockSpec(memory_space=space)] * len(args)
    )
    skip = len(scalars)
    first = skip + len(ordered)

    def body(*refs):
        if not fetch:
            kernel(*refs[:skip], *refs[first:])
            return
        *refs, sems = refs
        held = refs[len(refs) - len(args) :]
        copies = [
            pltpu.make_async_copy(source, target, sems.at[i])
            for i, (source, target) in enumerate(zip(refs[first : first + len(args)], held))
        ]
        for copy in copies:
            copy.start()
        for copy in copies:
            copy.wait()
        kernel(*refs[:skip], *held, *refs[first + len(args) : len(refs) - len(args)])

    extra = []
    if fetch:
        extra = [pltpu.VMEM(a.shape, a.dtype) for a in args]
        extra.append(pltpu.SemaphoreType.DMA((len(args),)))
    return pl.pallas_call(
        body,
        out_shape=[jax.ShapeDtypeStruct(shape, dtype) for shape, dtype in outs],
        in_specs=in_specs,
        out_specs=[pl.BlockSpec(memory_space=pltpu.VMEM)] * len(outs),
        scratch_shapes=[*scratch, *extra],
        compiler_params=pltpu.CompilerParams(vmem_limit_bytes=14 * 1024 * 1024),
        cost_estimate=pl.CostEstimate(flops=int(flops), bytes_accessed=1, transcendentals=0),
        name=name,
    )(*[s.reshape(1).astype(jnp.int32) for s in scalars], *ordered, *args)


def dot(a, b, over=(1, 0)):
    return lax.dot_general(
        a, b, (((over[0],), (over[1],)), ((), ())), preferred_element_type=F32
    )


def normed(v):
    centered = v - jnp.mean(v, axis=-1, keepdims=True)
    scale = lax.rsqrt(jnp.mean(centered * centered, axis=-1, keepdims=True) + EPS)
    return centered * scale, scale


def norm_back(n, scale, grad):
    mean = jnp.mean(grad, axis=-1, keepdims=True)
    along = jnp.mean(grad * n, axis=-1, keepdims=True)
    return (grad - mean - n * along) * scale


def swap(block, axis, offset):
    count = lax.axis_size(axis)
    return lax.ppermute(block, axis, [(i, i ^ offset) for i in range(count)])


def tp_gather(rows):
    far = swap(rows, "tp", 2)
    near = swap(rows, "tp", 1)
    return [rows, near, far, swap(far, "tp", 1)]


def near_rows_kernel(keep, got, own, out):
    rows = own.shape[0]
    own[...] = keep[:rows].astype(F32) + got[:rows].astype(F32)
    out[...] = (keep[rows:].astype(F32) + got[rows:].astype(F32)).astype(BF)


def tp_scatter(keep, send, ordered=()):
    got = swap(send, "tp", 1)
    rows, cols = keep.shape
    own, out = call(
        near_rows_kernel,
        "near_rows",
        [((rows // 2, cols), F32), ((rows // 2, cols), BF)],
        [keep, got],
        ordered=ordered,
    )
    return [own, swap(out, "tp", 2)]


def put_piece(rank, k, value, keep, send):
    to = jnp.bitwise_xor(rank[0], k)

    @pl.when(to % 2 == 0)
    def _():
        keep[to // 2] = value

    @pl.when(to % 2 == 1)
    def _():
        send[to // 2] = value


def pack_kernel(rank, cond, bias, keep, send, scr):
    count = 2 * keep.shape[0]
    latents = cond.shape[0]
    feat = cond.shape[1] // count
    value = cond[...].astype(F32)
    act = (value / (1.0 + jnp.exp(-value))).astype(BF).astype(F32)
    row = bias[...].astype(F32).reshape(1, bias.shape[0])
    scr[...] = jnp.zeros_like(scr)
    for r in range(bias.shape[0] // feat):
        scr[latents + r : latents + r + 1, 0:feat] = row[:, r * feat : (r + 1) * feat]
    for k in range(count):
        scr[0:latents, 0:feat] = act[:, k * feat : (k + 1) * feat]
        put_piece(rank, k, scr[...], keep, send)


def pair_kernel(keep, got, *outs):
    for z, out in enumerate(outs):
        out[0] = keep[z]
        out[1] = got[z]


def exchange(keep, send, ordered=(), got=None):
    size = keep.shape[0]
    piece = keep.shape[1:]
    if size != 4:
        count = 2 * size
        order = jnp.bitwise_xor(jnp.arange(count), lax.axis_index("fsdp"))
        whole = jnp.stack([keep, send], axis=1).reshape(count, *piece)
        got = lax.all_to_all(
            jnp.take(whole, order, axis=0), "fsdp", split_axis=0, concat_axis=0, tiled=True
        )
        return [jnp.take(got, order, axis=0)]
    got = swap(send, "fsdp", 1) if got is None else got
    pairs = call(
        pair_kernel, "pairs", [((2, *piece), keep.dtype)] * size, [keep, got], ordered=ordered
    )
    return [pairs[0]] + [swap(pairs[z], "fsdp", 2 * z) for z in range(1, size)]


def pick(arrays, k):
    per = arrays[0].shape[0]
    return arrays[k // per].at[k % per]


def both_own_kernel(qkv, proj, first, out):
    cols = qkv.shape[2]
    for j in range(3):
        out[:, j * cols : (j + 1) * cols] = qkv[j]
    out[:, 3 * cols : 4 * cols] = proj[...].T
    out[:, 4 * cols :] = first[...]


def join_split_kernel(a, b, *outs):
    half = a.shape[0]
    lane = 0
    for out in outs:
        here = slice(lane, lane + out.shape[2])
        out[:half] = a[:, :, here]
        out[half:] = b[:, :, here]
        lane += out.shape[2]


def copy_kernel(value, out):
    out[...] = value[...]


def join_kernel(a, b, out):
    half = out.shape[0] // 2
    if len(a.shape) == 2:
        out[0] = a[...]
        out[1] = b[...]
    else:
        out[:half] = a[...]
        out[half:] = b[...]


def join(a, b, ordered=()):
    size = 1 if a.ndim == 2 else a.shape[0]
    shape = (2 * size, *a.shape[-2:])
    return call(join_kernel, "join", [(shape, a.dtype)], [a, b], ordered=ordered)[0]


def gather_steps(own):
    two = join(own, swap(own, "fsdp", 4))
    four = join(two, swap(two, "fsdp", 2))
    return two, four, swap(four, "fsdp", 1)


def mod_kernel(*refs):
    *got, ada, bias, keep, send, cols_out, scr, pieces = refs
    count = pieces.shape[0]
    feat = ada.shape[0]
    latents = scr.shape[0] // count
    for k in range(count):
        scr[k * latents : (k + 1) * latents, :] = pick(got, k)[0:latents, :]
    cols = scr[:, 0:feat].astype(BF)
    cols_out[...] = cols
    width = ada.shape[1] // 6
    pieces[...] = jnp.zeros_like(pieces)
    for j in range(6):
        at = slice(j * width, (j + 1) * width)
        part = dot(cols, ada[:, at]) + bias[:, at]
        for k in range(count):
            for l in range(latents):
                pieces[k, 6 * l + j : 6 * l + j + 1, :] = part[k * latents + l : k * latents + l + 1]
    for place, z in enumerate((0, 2, 1, 3) if count == 8 else range(count // 2)):
        keep[place] = pieces[2 * z].astype(BF)
        send[place] = pieces[2 * z + 1].astype(BF)


def bias_kernel(rank, tp_rank, *refs, latents, feat, tp):
    *got, qkv_out, proj_out, second_out, hidden_out, scr = refs
    count = scr.shape[0]
    for k in range(count):
        scr[jnp.bitwise_xor(rank[0], k)] = pick(got, k)[...]
    per = count // tp
    first = tp_rank[0] * per
    cols = per * feat
    qkv_out[...] = jnp.zeros_like(qkv_out)
    at = latents
    for i in range(per):
        f = first + i
        here = slice(i * feat, (i + 1) * feat)
        qkv_out[0:1, here] = scr[f, at : at + 1, 0:feat]
        qkv_out[0:1, 2 * cols + i * feat : 2 * cols + (i + 1) * feat] = scr[
            f, at + 1 : at + 2, 0:feat
        ]
        for r in range(tp):
            lane = (i * tp + r) * feat
            hidden_out[0:1, lane : lane + feat] = scr[f, at + 4 + r : at + 5 + r, 0:feat]
    for f in range(count):
        here = slice(f * feat, (f + 1) * feat)
        proj_out[0:1, here] = scr[f, at + 2 : at + 3, 0:feat]
        second_out[0:1, here] = scr[f, at + 3 : at + 4, 0:feat]


def assemble_kernel(rank, mine, other, *outs):
    rows = mine.shape[1]
    for i, z in enumerate((0, 2, 1, 3)):
        for x, blocks in enumerate((mine, other)):
            at = jnp.bitwise_xor(rank[0], 2 * z + x) * rows
            at = pl.ds(pl.multiple_of(at, rows), rows)
            lane = 0
            for out in outs:
                out[at, :] = blocks[i, :, lane : lane + out.shape[1]]
                lane += out.shape[1]


def first_norm_kernel(x0, x1, x2, x3, *refs):
    *got, mod_out, out = refs
    mod = got[0][...].astype(F32)
    for part in got[1:]:
        mod = mod + part[...].astype(F32)
    mod = mod.reshape(mod.shape[-2:])
    mod_out[...] = mod[0 : mod_out.shape[0]]
    latents = mod_out.shape[0] // 6
    part = x0.shape[0] // (2 * latents)
    whole = out.shape[0] // latents
    for b, block in enumerate((x0, x1, x2, x3)):
        for l in range(latents):
            n, _ = normed(block[l * part : (l + 1) * part, :].astype(F32))
            shift, scale = mod[6 * l : 6 * l + 1], mod[6 * l + 1 : 6 * l + 2]
            out[l * whole + b * part : l * whole + (b + 1) * part, :] = (
                n * (1.0 + scale) + shift
            ).astype(BF)


def gate_grad_kernel(x0, x1, x2, x3, mod, out, bias_out):
    latents = mod.shape[0] // 6
    rows = x0.shape[0] // 2
    part = rows // latents
    total = jnp.zeros((1, mod.shape[1]), F32)
    for b, block in enumerate((x0, x1, x2, x3)):
        for l in range(latents):
            cot = block[rows + l * part : rows + (l + 1) * part, :].astype(F32)
            value = (cot * mod[6 * l + 5 : 6 * l + 6, :]).astype(BF)
            out[b * rows + l * part : b * rows + (l + 1) * part, :] = value
            if b == 0:
                total = total + jnp.sum(value.astype(F32), axis=0, keepdims=True)
    bias_out[...] = total


def unpack_rows(blocks, rows, latents):
    part = blocks[0].shape[0] // latents
    whole = part * len(blocks)
    for b, block in enumerate(blocks):
        for l in range(latents):
            rows[l * whole + b * part : l * whole + (b + 1) * part, :] = block[
                l * part : (l + 1) * part, :
            ]


def put_parts(value, keep, send, latent):
    part = value.shape[0] // 4
    rows = keep.shape[0] // 2
    for b in range(4):
        out = send if b % 2 else keep
        at = (b // 2) * rows + latent * part
        out[at : at + part, :] = value[b * part : (b + 1) * part]


def softmax(q, k):
    scores = dot(q, k, (1, 1)) * FACTOR
    weights = jnp.exp(scores - jnp.max(scores, axis=-1, keepdims=True))
    return weights * (1.0 / jnp.sum(weights, axis=-1, keepdims=True))


def attn_kernel(rows, qkv_w, proj_w, bias, qkv, att, keep, send, *, latents):
    cols = proj_w.shape[1]
    size = rows.shape[0] // latents
    for l in range(latents):
        here = slice(l * size, (l + 1) * size)
        projected = (dot(rows[here, :], qkv_w[...]) + bias[...]).astype(BF)
        qkv[here, :] = projected
        mixed = []
        for h in range(cols // HEAD):
            q, k, v = [
                projected[:, j * cols + h * HEAD : j * cols + (h + 1) * HEAD] for j in range(3)
            ]
            mixed.append(dot(softmax(q, k).astype(BF), v))
        attended = jnp.concatenate(mixed, axis=1).astype(BF)
        att[here, :] = attended
        put_parts(dot(attended, proj_w[...], (1, 1)).astype(BF), keep, send, l)


def middle_kernel(x, p0, p1, bias, mod, branch_out, middle_out, out):
    latents = mod.shape[0] // 6
    rows = out.shape[0] // latents
    for l in range(latents):
        here = slice(l * rows, (l + 1) * rows)
        branch = bias[...] + p0[here, :] + p1[here, :].astype(F32)
        branch_out[here, :] = branch
        gate = mod[6 * l + 2 : 6 * l + 3, :]
        middle = x[here, :].astype(F32) + gate * branch
        middle_out[here, :] = middle
        n, _ = normed(middle)
        shift = mod[6 * l + 3 : 6 * l + 4, :]
        scale = mod[6 * l + 4 : 6 * l + 5, :]
        out[here, :] = (n * (1.0 + scale) + shift).astype(BF)


def mlp_kernel(
    x0, x1, x2, x3, grads, first, second, bias, act_out, pre_out, x_out, keep, send
):
    rows = x0.shape[0]
    for b, x in enumerate((x0, x1, x2, x3)):
        here = slice(b * rows, (b + 1) * rows)
        x_out[here, :] = x[...]
        v = dot(x[...], first[...]) + bias[...]
        square = v * v
        t = jnp.tanh(CURVE * v * (1.0 + CUBIC * square))
        act_out[here, :] = (0.5 * v * (1.0 + t)).astype(BF)
        slope = 0.5 * (1.0 + t) + 0.5 * v * (1.0 - t * t) * CURVE * (1.0 + 3.0 * CUBIC * square)
        pre = (dot(grads[here, :], second[...]) * slope).astype(BF)
        pre_out[here, :] = pre
        at = (b // 2) * rows
        out = send if b % 2 else keep
        out[at : at + rows, :] = dot(pre, first[...], (1, 1)).astype(BF)


def store_grad(rank, product, keep, send, cols, step):
    rows = keep.shape[1]
    for half in range(2):

        @pl.when((rank[0] // step) % 2 == half)
        def _(half=half):
            for k in range(2 * keep.shape[0]):
                to = jnp.bitwise_xor(rank[0], k)
                if step == 1:
                    place = (to // 2 % 2) * 2 + to // 4
                else:
                    place = (to // 4) * 2 + to % 2
                target = keep if (k // step) % 2 == half else send
                target[place, :, cols] = product[k * rows : (k + 1) * rows]


def mlp_grad_kernel(rank, left, right, keep, send, *bias_out, step):
    product = dot(left[...], right[...], (0, 0)).astype(BF)
    store_grad(rank, product, keep, send, slice(0, right.shape[1]), step)
    if bias_out:
        bias_out[0][...] = jnp.sum(right[...].astype(F32), axis=0, keepdims=True)


def mlp_out_kernel(act, second, x0, x1, x2, x3, bias, keep, send, sums, *, latents):
    rows = keep.shape[0] // 2
    part = rows // latents
    sums[...] = jnp.zeros_like(sums)
    for b, x in enumerate((x0, x1, x2, x3)):
        at = (b // 2) * rows
        out = send if b % 2 else keep
        value = dot(act[b * rows : (b + 1) * rows, :], second[...], (1, 1))
        out[at : at + rows, :] = value.astype(BF)
        if b == 0:
            value = value + bias[...]
        grad = value * x[rows:, :].astype(F32)
        for l in range(latents):
            sums[l : l + 1, :] += jnp.sum(
                grad[l * part : (l + 1) * part], axis=0, keepdims=True
            )


def output_kernel(middle, p0, p1, bias, mod, out):
    latents = mod.shape[0] // 6
    rows = middle.shape[0] // latents
    for l in range(latents):
        here = slice(l * rows, (l + 1) * rows)
        branch = bias[...] + p0[here, :] + p1[here, :].astype(F32)
        out[here, :] = (middle[here, :] + mod[6 * l + 5 : 6 * l + 6, :] * branch).astype(BF)


def middle_back_kernel(x, middle, branch, p0, p1, mod, grad_out, out, sums):
    latents = mod.shape[0] // 6
    width = middle.shape[1]
    size = middle.shape[0]
    rows = size // latents
    total = jnp.zeros((1, width), F32)
    for l in range(latents):
        here = slice(l * rows, (l + 1) * rows)
        grad = p0[here, :] + p1[here, :].astype(F32)
        cot = x[size + l * rows : size + (l + 1) * rows, :].astype(F32)
        n, scale = normed(middle[here, :])
        sums[3 * l + 1 : 3 * l + 2, :] = jnp.sum(grad, axis=0, keepdims=True)
        sums[3 * l + 2 : 3 * l + 3, :] = jnp.sum(grad * n, axis=0, keepdims=True)
        factor = 1.0 + mod[6 * l + 4 : 6 * l + 5, :]
        whole = cot + norm_back(n, scale, grad * factor)
        grad_out[here, :] = whole
        sums[3 * l : 3 * l + 1, :] = jnp.sum(whole * branch[here, :], axis=0, keepdims=True)
        low = (whole * mod[6 * l + 2 : 6 * l + 3, :]).astype(BF)
        out[here, :] = low
        total = total + jnp.sum(low.astype(F32), axis=0, keepdims=True)
    sums[3 * latents : 3 * latents + 1, :] = total


def attn_back_kernel(
    g0, g1, g2, g3, qkv_w, proj_w, qkv, rows, grads, keep, send, bias_out, *, latents
):
    unpack_rows([g0, g1, g2, g3], rows, latents)
    cols = proj_w.shape[1]
    size = rows.shape[0] // latents
    for l in range(latents):
        here = slice(l * size, (l + 1) * size)
        back = dot(rows[here, :], proj_w[...]).astype(BF)
        projected = qkv[here, :]
        found = [[], [], []]
        for h in range(cols // HEAD):
            q, k, v = [
                projected[:, j * cols + h * HEAD : j * cols + (h + 1) * HEAD] for j in range(3)
            ]
            up = back[:, h * HEAD : (h + 1) * HEAD]
            probs = softmax(q, k)
            grad_probs = dot(up, v, (1, 1))
            inner = jnp.sum(probs * grad_probs, axis=-1, keepdims=True)
            scores = (probs * (grad_probs - inner)).astype(BF)
            found[0].append(dot(scores, k) * FACTOR)
            found[1].append(dot(scores, q, (0, 0)) * FACTOR)
            found[2].append(dot(probs.astype(BF), up, (0, 0)))
        grad = jnp.concatenate(found[0] + found[1] + found[2], axis=1).astype(BF)
        grads[here, :] = grad
        part = jnp.sum(grad.astype(F32), axis=0, keepdims=True)
        total = part if l == 0 else total + part
        put_parts(dot(grad, qkv_w[...], (1, 1)).astype(BF), keep, send, l)
    bias_out[...] = total


def attn_grad_kernel(rank, rows, grads, back, att, keep, send):
    cut = grads.shape[1]
    product = dot(rows[...], grads[...], (0, 0)).astype(BF)
    store_grad(rank, product, keep, send, slice(0, cut), 1)
    product = dot(back[...], att[...], (0, 0)).astype(BF)
    store_grad(rank, product, keep, send, slice(cut, keep.shape[2]), 1)


def input_back_kernel(
    x, grad_middle, p0, p1, mod, sums, gates, fc2, fc1, qkv, out, pack, scr
):
    latents = mod.shape[0] // 6
    rows = out.shape[0] // latents
    cols = qkv.shape[1] // 3
    scr[...] = jnp.zeros_like(scr)
    for l in range(latents):
        here = slice(l * rows, (l + 1) * rows)
        grad = p0[here, :] + p1[here, :].astype(F32)
        n, scale = normed(x[here, :].astype(F32))
        scr[6 * l : 6 * l + 1, :] = jnp.sum(grad, axis=0, keepdims=True)
        scr[6 * l + 1 : 6 * l + 2, :] = jnp.sum(grad * n, axis=0, keepdims=True)
        scr[6 * l + 2 : 6 * l + 5, :] = sums[3 * l : 3 * l + 3, :]
        scr[6 * l + 5 : 6 * l + 6, :] = gates[l : l + 1, :]
        factor = 1.0 + mod[6 * l + 1 : 6 * l + 2, :]
        out[here, :] = grad_middle[here, :] + norm_back(n, scale, grad * factor)
    at = 6 * latents
    scr[at : at + 1, :] = sums[3 * latents : 3 * latents + 1, :]
    scr[at + 1 : at + 2, :] = fc2[...]
    scr[at + 2 : at + 3, :] = fc1[...]
    scr[at + 3 : at + 4, 0:cols] = qkv[:, 0:cols]
    scr[at + 3 : at + 4, cols : 2 * cols] = qkv[:, 2 * cols :]
    pack[...] = scr[...].astype(BF)


def spread_kernel(
    rank, tp_rank, k0, k1, k2, k3, keep, send, parts, total, *, latents, feat
):
    count = 2 * keep.shape[0]
    packs = (k0, k1, k2, k3)
    per = count // len(packs)
    cols = per * feat
    mods = 6 * latents
    summed = jnp.zeros(k0.shape, F32)
    for d, pack in enumerate(packs):
        value = pack[...].astype(F32)
        parts[jnp.bitwise_xor(tp_rank[0], d)] = value
        summed = summed + value
    total[...] = summed
    row = slice(mods, mods + 1)
    total[row, :] = jnp.zeros((1, k0.shape[1]), F32)
    for k in range(count):
        t, i = k // per, k % per
        here = slice(k * feat, (k + 1) * feat)
        total[row, 0:feat] = parts[t, mods + 3 : mods + 4, i * feat : (i + 1) * feat]
        total[row, feat : 2 * feat] = parts[
            t, mods + 3 : mods + 4, cols + i * feat : cols + (i + 1) * feat
        ]
        total[row, 2 * feat : 3 * feat] = summed[mods : mods + 1, here]
        total[row, 3 * feat : 4 * feat] = summed[mods + 1 : mods + 2, here]
        total[row, 4 * feat : 8 * feat] = parts[
            t, mods + 2 : mods + 3, 4 * i * feat : 4 * (i + 1) * feat
        ]
        put_piece(rank, k, total[...].astype(BF), keep, send)


def silu_kernel(*refs, latents):
    *got, ada, keep, send, grads, bias_out, scr, out_scr = refs
    width = ada.shape[1] // 6
    feat = ada.shape[0]
    count = scr.shape[1] // latents
    mods = 6 * latents
    bias = jnp.zeros((1, width), F32)
    for k in range(count):
        value = pick(got, k)[...].astype(F32)
        bias = bias + value[mods : mods + 1]
        for l in range(latents):
            for j in range(6):
                scr[j, k * latents + l : k * latents + l + 1, :] = value[6 * l + j : 6 * l + j + 1]
    bias_out[...] = bias
    total = jnp.zeros((count * latents, feat), F32)
    for j in range(6):
        at = slice(j * width, (j + 1) * width)
        rows = scr[j].astype(BF)
        grads[:, at] = rows
        total = total + dot(rows, ada[:, at], (1, 1))
    out_scr[...] = jnp.zeros_like(out_scr)
    for k in range(count):
        out_scr[k, 0:latents, 0:feat] = total[k * latents : (k + 1) * latents]
    for z in range(count // 2):
        keep[z] = out_scr[2 * z]
        send[z] = out_scr[2 * z + 1]


def cond_kernel(rank, *refs, latents, feat):
    *got, cond, out, scr = refs
    count = scr.shape[0]
    for k in range(count):
        scr[jnp.bitwise_xor(rank[0], k)] = pick(got, k)[...]
    value = cond[...].astype(F32)
    gate = 1.0 / (1.0 + jnp.exp(-value))
    slope = gate * (1.0 + value * (1.0 - gate))
    for k in range(count):
        here = slice(k * feat, (k + 1) * feat)
        out[:, here] = scr[k, 0:latents, 0:feat] * slope[:, here]


def scatter_pieces(keep, send):
    count = 2 * keep.shape[0]
    order = jnp.bitwise_xor(jnp.arange(count), lax.axis_index("fsdp"))
    whole = jnp.stack([keep, send], axis=1).reshape(count, *keep.shape[1:]).astype(F32)
    whole = jnp.take(whole, order, axis=0)
    return lax.psum_scatter(whole, "fsdp", scatter_dimension=0, tiled=False)


def halve_kernel(keep, got, own, out):
    half = own.shape[0]
    for i in range(half):
        own[i] = keep[i].astype(F32) + got[i].astype(F32)
        out[i] = (keep[half + i].astype(F32) + got[half + i].astype(F32)).astype(BF)


def halve(keep, send, offset, ordered=()):
    got = swap(send, "fsdp", offset)
    shape = (keep.shape[0] // 2, *keep.shape[1:])
    outs = [(shape, F32), (shape, BF)]
    return call(halve_kernel, "halve", outs, [keep, got], ordered=ordered)


def add_kernel(own, got, out):
    out[...] = own[...] + got[...].astype(F32)


def last_sum(own, out, offset):
    got = swap(out, "fsdp", offset)
    total = call(add_kernel, "last_sum", [(own.shape, F32)], [own, got])[0]
    return total.reshape(own.shape[1:])


def attn_add_kernel(own, got, qkv, proj):
    cols = qkv.shape[2]
    for j in range(3):
        here = slice(j * cols, (j + 1) * cols)
        qkv[j] = own[0, :, here] + got[0, :, here].astype(F32)
    here = slice(3 * cols, 4 * cols)
    proj[...] = (own[0, :, here] + got[0, :, here].astype(F32)).T


def shards(
    inputs,
    conditioning,
    ada_weight,
    ada_bias,
    query_key_value_weight,
    qv_bias,
    attention_output_weight,
    attention_output_bias,
    expand_weight,
    hidden_layer_bias,
    contract_weight,
    contract_bias,
    out_cotangent,
):
    tp_rank = lax.axis_index("tp")
    tp_count = lax.axis_size("tp")
    rank = lax.axis_index("fsdp")
    count = lax.axis_size("fsdp")
    positions, latents, width = inputs.shape
    feat = ada_weight.shape[0]
    cols = query_key_value_weight.shape[2]
    hidden = expand_weight.shape[1]
    hidden_part = hidden_layer_bias.shape[0]
    mod_part = ada_bias.shape[0]
    rows = positions * latents
    tokens = rows * tp_count
    mods = 6 * latents
    direct = count == 8
    block = ((rows, width), BF)
    block_f32 = ((rows, width), F32)

    qkv_own = query_key_value_weight.transpose(1, 0, 2)
    first_ops = []
    if direct:
        both_own = call(
            both_own_kernel,
            "both_own",
            [((feat, 4 * cols + hidden), BF)],
            [qkv_own, attention_output_weight, expand_weight],
            fetch=True,
        )[0]
        first_ops = [both_own]
        both_far = swap(both_own, "fsdp", 4)

    half = count // 2
    bias_own = jnp.concatenate(
        [qv_bias.reshape(-1), attention_output_bias, contract_bias, hidden_layer_bias]
    )
    cond_keep, cond_send = call(
        pack_kernel,
        "pack_conditioning",
        [((half, 16, 128), F32)] * 2,
        [conditioning, bias_own],
        [rank],
        scratch=[pltpu.VMEM((16, 128), F32)],
        ordered=first_ops,
    )
    if direct:
        both_two = join(both_own, both_far, [cond_send])
    cond_got = exchange(cond_keep, cond_send, [both_two] if direct else ())

    bias_row = lax.dynamic_update_slice(
        jnp.zeros((1, mod_part * count), F32),
        ada_bias.astype(F32).reshape(1, mod_part),
        (0, rank * mod_part),
    )
    mod_keep, mod_send, cond_cols = call(
        mod_kernel,
        "modulation",
        [((half, 16, width), BF)] * 2 + [((count * latents, feat), BF)],
        [*cond_got, ada_weight, bias_row],
        scratch=[
            pltpu.VMEM((count * latents, 128), F32),
            pltpu.VMEM((count, 16, width), F32),
        ],
    )
    x_own = jnp.stack([inputs.transpose(1, 0, 2), out_cotangent.transpose(1, 0, 2)])
    x_own = x_own.reshape(2 * rows, width)
    x_own = call(
        copy_kernel, "tokens", [((2 * rows, width), BF)], [x_own], ordered=cond_got[:1]
    )[0]
    x_blocks = tp_gather(x_own)

    if direct:
        half_one = halve(mod_keep, mod_send, 1)
        half_two = halve(*half_one, 2)
        mod_parts = [half_two[0], swap(half_two[1], "fsdp", 4)]
        attn_four, first_early = call(
            join_split_kernel,
            "join_split",
            [((4, feat, 4 * cols), BF), ((4, feat, hidden), BF)],
            [both_two, swap(both_two, "fsdp", 2)],
            ordered=[half_one[1]],
        )
        attn_other = swap(attn_four, "fsdp", 1)
        first_four = call(
            copy_kernel,
            "first_sent",
            [((4, feat, hidden), BF)],
            [first_early],
            ordered=[attn_other],
        )[0]
        first_other = swap(first_four, "fsdp", 1)
        second_own = call(
            copy_kernel,
            "second_own",
            [((feat, hidden), BF)],
            [contract_weight.T],
            ordered=[mod_parts[1]],
            fetch=True,
        )[0]
        second_two, second_four, second_other = gather_steps(second_own)
        qkv_full, proj_full = call(
            assemble_kernel,
            "attn_weights",
            [((width, 3 * cols), BF), ((width, cols), BF)],
            [attn_four, attn_other],
            [rank],
        )
        first_full = call(
            assemble_kernel,
            "first_weights",
            [((width, hidden), BF)],
            [first_four, first_other],
            [rank],
        )[0]
        second_full = call(
            assemble_kernel,
            "second_weights",
            [((width, hidden), BF)],
            [second_four, second_other],
            [rank],
        )[0]
        steps = [[attn_four], [first_four], [second_two], [], [second_four, first_full]]
    else:
        steps = [[]] * 5
        mod_parts = [scatter_pieces(mod_keep, mod_send)]
        qkv_full = lax.all_gather(
            query_key_value_weight.reshape(feat, 3 * cols), "fsdp", axis=0, tiled=True
        )
        proj_full = lax.all_gather(attention_output_weight.T, "fsdp", axis=0, tiled=True)
        first_full = lax.all_gather(expand_weight, "fsdp", axis=0, tiled=True)
        second_full = lax.all_gather(contract_weight.T, "fsdp", axis=0, tiled=True)

    qkv_bias, proj_bias, second_bias, hidden_bias = call(
        functools.partial(bias_kernel, latents=latents, feat=feat, tp=tp_count),
        "biases",
        [((1, 3 * cols), F32), ((1, width), F32), ((1, width), F32), ((1, hidden), F32)],
        cond_got,
        [rank, tp_rank],
        scratch=[pltpu.VMEM((count, 16, 128), F32)],
        ordered=[mod_send],
        flops=1e9,
    )
    mod, attn_rows = call(
        first_norm_kernel,
        "first_norm",
        [((mods, width), F32), ((tokens, width), BF)],
        [*x_blocks, *mod_parts],
        ordered=[hidden_bias, *steps[0]],
    )
    pair = ((2 * rows, width), BF)
    qkv, att, keep, send = call(
        functools.partial(attn_kernel, latents=latents),
        "attention",
        [((tokens, 3 * cols), BF), ((tokens, cols), BF), pair, pair],
        [attn_rows, qkv_full, proj_full, qkv_bias],
        ordered=steps[1],
    )
    branch_parts = tp_scatter(keep, send, steps[2])
    grad_rows, fc2_part = call(
        gate_grad_kernel,
        "gate_grad",
        [((tokens, width), BF), ((1, width), F32)],
        [*x_blocks, mod],
        ordered=[branch_parts[0], *steps[3]],
        flops=1e9,
    )
    branch, middle, mlp_in = call(
        middle_kernel,
        "middle",
        [block_f32, block_f32, block],
        [x_own, *branch_parts, proj_bias, mod],
        ordered=[fc2_part, *steps[4]],
    )
    m_blocks = tp_gather(mlp_in)
    act, pre, mlp_rows, keep, send = call(
        mlp_kernel,
        "mlp",
        [((tokens, hidden), BF)] * 2 + [((tokens, width), BF), pair, pair],
        [*m_blocks, grad_rows, first_full, second_full, hidden_bias],
    )
    first_done = []
    if direct:
        blocks = [((half, feat, hidden), BF)] * 2
        first_keep, first_send, fc1_part = call(
            functools.partial(mlp_grad_kernel, step=1),
            "first_grad",
            blocks + [((1, hidden), F32)],
            [mlp_rows, pre],
            [rank],
            ordered=[send],
            flops=2e9,
        )
        first_done = [fc1_part]
    grad_in = tp_scatter(keep, send, first_done)
    out_keep, out_send, gates = call(
        functools.partial(mlp_out_kernel, latents=latents),
        "mlp_out",
        [pair, pair, ((8, width), F32)],
        [act, second_full, *x_blocks, second_bias],
        ordered=[grad_in[0]],
        flops=1.5e9,
    )
    if direct:
        second_keep, second_send = call(
            functools.partial(mlp_grad_kernel, step=1),
            "second_grad",
            blocks,
            [grad_rows, act],
            [rank],
            ordered=[out_send],
            flops=2e9,
        )
        first_half = halve(first_keep, first_send, 1)
        second_sent = call(
            copy_kernel, "second_sent", blocks[:1], [second_send], ordered=[first_half[1]]
        )[0]
        steps = [[first_half[1], second_sent]]
    else:
        first_sum = lax.psum_scatter(
            dot(mlp_rows, pre, (0, 0)), "fsdp", scatter_dimension=0, tiled=True
        )
        second_sum = lax.psum_scatter(
            dot(grad_rows, act, (0, 0)), "fsdp", scatter_dimension=0, tiled=True
        )
        fc1_part = jnp.sum(pre.astype(F32), axis=0, keepdims=True)
        steps = [[]]
        second_keep = fc1_part

    grad_middle, grad_attn, sums = call(
        middle_back_kernel,
        "middle_back",
        [block_f32, block, ((8, width), F32)],
        [x_own, middle, branch, *grad_in, mod],
        ordered=[second_keep],
    )
    a_blocks = tp_gather(grad_attn)
    back_rows, grads, keep, send, qkv_part = call(
        functools.partial(attn_back_kernel, latents=latents),
        "attention_back",
        [((tokens, width), BF), ((tokens, 3 * cols), BF), pair, pair, ((1, 3 * cols), F32)],
        [*a_blocks, qkv_full, proj_full, qkv],
        ordered=steps[0],
    )
    grad_in = tp_scatter(keep, send)
    if direct:
        attn_keep, attn_send = call(
            attn_grad_kernel,
            "attn_weight_grad",
            [((half, feat, 4 * cols), BF)] * 2,
            [attn_rows, grads, back_rows, att],
            [rank],
            ordered=[grad_in[0]],
            flops=6e9,
        )
    else:
        qkv_sum = lax.psum_scatter(
            dot(attn_rows, grads, (0, 0)), "fsdp", scatter_dimension=0, tiled=True
        ).reshape(feat, 3, cols)
        proj_sum = lax.psum_scatter(
            dot(back_rows, att, (0, 0)), "fsdp", scatter_dimension=0, tiled=True
        ).T

    inputs_grad, pack = call(
        input_back_kernel,
        "input_back",
        [block_f32, ((16, width), BF)],
        [x_own, grad_middle, *grad_in, mod, sums, gates, fc2_part, fc1_part, qkv_part],
        scratch=[pltpu.VMEM((16, width), F32)],
    )
    tail = [[]] * 3
    if direct:
        first_one = halve(*first_half, 2, [pack])
        first_sum = last_sum(*first_one, 4)
        second_half = halve(second_keep, second_sent, 1, [pack])
        tail[0] = [first_one[1], second_half[1]]
    packs = [pack] + [swap(pack, "tp", d) for d in range(1, tp_count)]
    spread_keep, spread_send = call(
        functools.partial(spread_kernel, latents=latents, feat=feat),
        "spread",
        [((half, 16, width), BF)] * 2,
        packs,
        [rank, tp_rank],
        scratch=[pltpu.VMEM((tp_count, 16, width), F32), pltpu.VMEM((16, width), F32)],
        ordered=tail[0],
    )
    spread_got = None
    if direct:
        spread_got = swap(spread_send, "fsdp", 1)
        attn_half = halve(attn_keep, attn_send, 1, [spread_got])
        attn_own_sum, attn_out = halve(*attn_half, 2)
        qkv_sum, proj_sum = call(
            attn_add_kernel,
            "attn_sum",
            [((3, feat, cols), F32), ((cols, feat), F32)],
            [attn_own_sum, swap(attn_out, "fsdp", 4)],
        )
        qkv_sum = qkv_sum.transpose(1, 0, 2)
        second_one = halve(*second_half, 2, [spread_got])
        second_sum = last_sum(*second_one, 4)
        tail[1] = [attn_half[1], second_one[1]]
        tail[2] = [attn_out]
    silu_keep, silu_send, grad_mod_all, bias_grads = call(
        functools.partial(silu_kernel, latents=latents),
        "silu_columns",
        [((half, 8, 128), F32)] * 2
        + [((count * latents, 6 * width), BF), ((1, width), F32)],
        [*exchange(spread_keep, spread_send, tail[1], spread_got), ada_weight],
        scratch=[
            pltpu.VMEM((6, count * latents, width), F32),
            pltpu.VMEM((count, 8, 128), F32),
        ],
        ordered=tail[2],
    )
    mlp_parts = tp_scatter(out_keep, out_send, [silu_send])
    output = call(
        output_kernel, "output", [block], [middle, *mlp_parts, second_bias, mod]
    )[0]
    cond_grad = call(
        functools.partial(cond_kernel, latents=latents, feat=feat),
        "cond_grad",
        [((latents, width), F32)],
        [*exchange(silu_keep, silu_send), conditioning],
        [rank],
        scratch=[pltpu.VMEM((count, 8, 128), F32)],
    )[0]
    ada_weight_grad = dot(cond_cols, grad_mod_all, (0, 0))
    bias_grads = bias_grads.reshape(width)
    ada_bias_grad = jnp.sum(
        lax.dynamic_slice_in_dim(grad_mod_all, rank * mod_part, mod_part, 1).astype(F32), axis=0
    )

    return (
        output.reshape(latents, positions, width).transpose(1, 0, 2),
        inputs_grad.reshape(latents, positions, width).transpose(1, 0, 2),
        cond_grad,
        ada_weight_grad,
        ada_bias_grad,
        qkv_sum,
        bias_grads[: 2 * feat].reshape(2, feat),
        proj_sum,
        bias_grads[2 * feat : 3 * feat],
        first_sum,
        bias_grads[4 * feat : 4 * feat + hidden_part],
        second_sum.T,
        bias_grads[3 * feat : 4 * feat],
    )


def solution(mesh):
    return jax.shard_map(
        shards,
        mesh=mesh,
        in_specs=(
            P("tp", "fsdp", None),
            P("fsdp", None),
            P("fsdp", None),
            P("fsdp"),
            P("fsdp", None, "tp"),
            P(None, "fsdp"),
            P("tp", "fsdp"),
            P("fsdp"),
            P("fsdp", "tp"),
            P("fsdp"),
            P("tp", "fsdp"),
            P("fsdp"),
            P("tp", "fsdp", None),
        ),
        out_specs=(
            P("tp", "fsdp", None),
            P("tp", "fsdp", None),
            P("fsdp", None),
            P("fsdp", None),
            P("fsdp"),
            P("fsdp", None, "tp"),
            P(None, "fsdp"),
            P("tp", "fsdp"),
            P("fsdp"),
            P("fsdp", "tp"),
            P("fsdp"),
            P("tp", "fsdp"),
            P("fsdp"),
        ),
        check_vma=False,
    )
```

```python
import functools
import math

import jax
import jax.numpy as jnp
from jax import lax
from jax.experimental import pallas as pl
from jax.experimental.pallas import tpu as pltpu
from jax.sharding import PartitionSpec as P

HEAD = 64
EPS = 1e-06
BF = jnp.bfloat16
F32 = jnp.float32
FACTOR = 1.0 / math.sqrt(HEAD)
CURVE = math.sqrt(2.0 / math.pi)
CUBIC = 0.044715


def call(kernel, name, outs, args, scalars=(), scratch=(), ordered=(), flops=1, fetch=False):
    space = pltpu.HBM if fetch else pltpu.VMEM
    in_specs = (
        [pl.BlockSpec(memory_space=pltpu.SMEM)] * len(scalars)
        + [pl.BlockSpec(memory_space=pl.ANY)] * len(ordered)
        + [pl.BlockSpec(memory_space=space)] * len(args)
    )
    skip = len(scalars)
    first = skip + len(ordered)

    def body(*refs):
        if not fetch:
            kernel(*refs[:skip], *refs[first:])
            return
        *refs, sems = refs
        held = refs[len(refs) - len(args) :]
        copies = [
            pltpu.make_async_copy(source, target, sems.at[i])
            for i, (source, target) in enumerate(zip(refs[first : first + len(args)], held))
        ]
        for copy in copies:
            copy.start()
        for copy in copies:
            copy.wait()
        kernel(*refs[:skip], *held, *refs[first + len(args) : len(refs) - len(args)])

    extra = []
    if fetch:
        extra = [pltpu.VMEM(a.shape, a.dtype) for a in args]
        extra.append(pltpu.SemaphoreType.DMA((len(args),)))
    return pl.pallas_call(
        body,
        out_shape=[jax.ShapeDtypeStruct(shape, dtype) for shape, dtype in outs],
        in_specs=in_specs,
        out_specs=[pl.BlockSpec(memory_space=pltpu.VMEM)] * len(outs),
        scratch_shapes=[*scratch, *extra],
        compiler_params=pltpu.CompilerParams(vmem_limit_bytes=14 * 1024 * 1024),
        cost_estimate=pl.CostEstimate(flops=int(flops), bytes_accessed=1, transcendentals=0),
        name=name,
    )(*[s.reshape(1).astype(jnp.int32) for s in scalars], *ordered, *args)


def dot(a, b, over=(1, 0)):
    return lax.dot_general(
        a, b, (((over[0],), (over[1],)), ((), ())), preferred_element_type=F32
    )


def normed(v):
    centered = v - jnp.mean(v, axis=-1, keepdims=True)
    scale = lax.rsqrt(jnp.mean(centered * centered, axis=-1, keepdims=True) + EPS)
    return centered * scale, scale


def norm_back(n, scale, grad):
    mean = jnp.mean(grad, axis=-1, keepdims=True)
    along = jnp.mean(grad * n, axis=-1, keepdims=True)
    return (grad - mean - n * along) * scale


def swap(block, axis, offset):
    count = lax.axis_size(axis)
    return lax.ppermute(block, axis, [(i, i ^ offset) for i in range(count)])


def tp_gather(rows):
    far = swap(rows, "tp", 2)
    near = swap(rows, "tp", 1)
    return [rows, near, far, swap(far, "tp", 1)]


def near_rows_kernel(keep, got, own, out):
    rows = own.shape[0]
    own[...] = keep[:rows].astype(F32) + got[:rows].astype(F32)
    out[...] = (keep[rows:].astype(F32) + got[rows:].astype(F32)).astype(BF)


def tp_scatter(keep, send, ordered=()):
    got = swap(send, "tp", 1)
    rows, cols = keep.shape
    own, out = call(
        near_rows_kernel,
        "near_rows",
        [((rows // 2, cols), F32), ((rows // 2, cols), BF)],
        [keep, got],
        ordered=ordered,
    )
    return [own, swap(out, "tp", 2)]


def put_piece(rank, k, value, keep, send):
    to = jnp.bitwise_xor(rank[0], k)

    @pl.when(to % 2 == 0)
    def _():
        keep[to // 2] = value

    @pl.when(to % 2 == 1)
    def _():
        send[to // 2] = value


def pack_kernel(rank, cond, bias, keep, send, scr):
    count = 2 * keep.shape[0]
    latents = cond.shape[0]
    feat = cond.shape[1] // count
    value = cond[...].astype(F32)
    act = (value / (1.0 + jnp.exp(-value))).astype(BF).astype(F32)
    row = bias[...].astype(F32).reshape(1, bias.shape[0])
    scr[...] = jnp.zeros_like(scr)
    for r in range(bias.shape[0] // feat):
        scr[latents + r : latents + r + 1, 0:feat] = row[:, r * feat : (r + 1) * feat]
    for k in range(count):
        scr[0:latents, 0:feat] = act[:, k * feat : (k + 1) * feat]
        put_piece(rank, k, scr[...], keep, send)


def pair_kernel(keep, got, *outs):
    for z, out in enumerate(outs):
        out[0] = keep[z]
        out[1] = got[z]


def exchange(keep, send, ordered=(), got=None):
    size = keep.shape[0]
    piece = keep.shape[1:]
    if size != 4:
        count = 2 * size
        order = jnp.bitwise_xor(jnp.arange(count), lax.axis_index("fsdp"))
        whole = jnp.stack([keep, send], axis=1).reshape(count, *piece)
        got = lax.all_to_all(
            jnp.take(whole, order, axis=0), "fsdp", split_axis=0, concat_axis=0, tiled=True
        )
        return [jnp.take(got, order, axis=0)]
    got = swap(send, "fsdp", 1) if got is None else got
    pairs = call(
        pair_kernel, "pairs", [((2, *piece), keep.dtype)] * size, [keep, got], ordered=ordered
    )
    return [pairs[0]] + [swap(pairs[z], "fsdp", 2 * z) for z in range(1, size)]


def pick(arrays, k):
    per = arrays[0].shape[0]
    return arrays[k // per].at[k % per]


def attn_own_kernel(qkv, proj, out):
    cols = qkv.shape[2]
    for j in range(3):
        out[:, j * cols : (j + 1) * cols] = qkv[j]
    out[:, 3 * cols :] = proj[...].T


def copy_kernel(value, out):
    out[...] = value[...]


def join_kernel(a, b, out):
    half = out.shape[0] // 2
    if len(a.shape) == 2:
        out[0] = a[...]
        out[1] = b[...]
    else:
        out[:half] = a[...]
        out[half:] = b[...]


def join(a, b, ordered=()):
    size = 1 if a.ndim == 2 else a.shape[0]
    shape = (2 * size, *a.shape[-2:])
    return call(join_kernel, "join", [(shape, a.dtype)], [a, b], ordered=ordered)[0]


def gather_steps(own, ordered=((), ())):
    two = join(own, swap(own, "fsdp", 4), ordered[0])
    four = join(two, swap(two, "fsdp", 2), ordered[1])
    return two, four, swap(four, "fsdp", 1)


def mod_kernel(*refs):
    *got, ada, bias, keep, send, cols_out, scr, pieces = refs
    count = pieces.shape[0]
    feat = ada.shape[0]
    latents = scr.shape[0] // count
    for k in range(count):
        scr[k * latents : (k + 1) * latents, :] = pick(got, k)[0:latents, :]
    cols = scr[:, 0:feat].astype(BF)
    cols_out[...] = cols
    width = ada.shape[1] // 6
    pieces[...] = jnp.zeros_like(pieces)
    for j in range(6):
        at = slice(j * width, (j + 1) * width)
        part = dot(cols, ada[:, at]) + bias[:, at]
        for k in range(count):
            for l in range(latents):
                pieces[k, 6 * l + j : 6 * l + j + 1, :] = part[k * latents + l : k * latents + l + 1]
    for place, z in enumerate((0, 2, 1, 3) if count == 8 else range(count // 2)):
        keep[place] = pieces[2 * z].astype(BF)
        send[place] = pieces[2 * z + 1].astype(BF)


def bias_kernel(rank, tp_rank, *refs, latents, feat, tp):
    *got, qkv_out, proj_out, second_out, hidden_out, scr = refs
    count = scr.shape[0]
    for k in range(count):
        scr[jnp.bitwise_xor(rank[0], k)] = pick(got, k)[...]
    per = count // tp
    first = tp_rank[0] * per
    cols = per * feat
    qkv_out[...] = jnp.zeros_like(qkv_out)
    at = latents
    for i in range(per):
        f = first + i
        here = slice(i * feat, (i + 1) * feat)
        qkv_out[0:1, here] = scr[f, at : at + 1, 0:feat]
        qkv_out[0:1, 2 * cols + i * feat : 2 * cols + (i + 1) * feat] = scr[
            f, at + 1 : at + 2, 0:feat
        ]
        for r in range(tp):
            lane = (i * tp + r) * feat
            hidden_out[0:1, lane : lane + feat] = scr[f, at + 4 + r : at + 5 + r, 0:feat]
    for f in range(count):
        here = slice(f * feat, (f + 1) * feat)
        proj_out[0:1, here] = scr[f, at + 2 : at + 3, 0:feat]
        second_out[0:1, here] = scr[f, at + 3 : at + 4, 0:feat]


def assemble_kernel(rank, mine, other, *outs):
    rows = mine.shape[1]
    for i, z in enumerate((0, 2, 1, 3)):
        for x, blocks in enumerate((mine, other)):
            at = jnp.bitwise_xor(rank[0], 2 * z + x) * rows
            at = pl.ds(pl.multiple_of(at, rows), rows)
            lane = 0
            for out in outs:
                out[at, :] = blocks[i, :, lane : lane + out.shape[1]]
                lane += out.shape[1]


def first_norm_kernel(x0, x1, x2, x3, *refs):
    *got, mod_out, out = refs
    mod = got[0][...].astype(F32)
    for part in got[1:]:
        mod = mod + part[...].astype(F32)
    mod = mod.reshape(mod.shape[-2:])
    mod_out[...] = mod[0 : mod_out.shape[0]]
    latents = mod_out.shape[0] // 6
    part = x0.shape[0] // (2 * latents)
    whole = out.shape[0] // latents
    for b, block in enumerate((x0, x1, x2, x3)):
        for l in range(latents):
            n, _ = normed(block[l * part : (l + 1) * part, :].astype(F32))
            shift, scale = mod[6 * l : 6 * l + 1], mod[6 * l + 1 : 6 * l + 2]
            out[l * whole + b * part : l * whole + (b + 1) * part, :] = (
                n * (1.0 + scale) + shift
            ).astype(BF)


def gate_grad_kernel(x0, x1, x2, x3, mod, out, bias_out):
    latents = mod.shape[0] // 6
    rows = x0.shape[0] // 2
    part = rows // latents
    total = jnp.zeros((1, mod.shape[1]), F32)
    for b, block in enumerate((x0, x1, x2, x3)):
        for l in range(latents):
            cot = block[rows + l * part : rows + (l + 1) * part, :].astype(F32)
            value = (cot * mod[6 * l + 5 : 6 * l + 6, :]).astype(BF)
            out[b * rows + l * part : b * rows + (l + 1) * part, :] = value
            if b == 0:
                total = total + jnp.sum(value.astype(F32), axis=0, keepdims=True)
    bias_out[...] = total


def unpack_rows(blocks, rows, latents):
    part = blocks[0].shape[0] // latents
    whole = part * len(blocks)
    for b, block in enumerate(blocks):
        for l in range(latents):
            rows[l * whole + b * part : l * whole + (b + 1) * part, :] = block[
                l * part : (l + 1) * part, :
            ]


def put_parts(value, keep, send, latent):
    part = value.shape[0] // 4
    rows = keep.shape[0] // 2
    for b in range(4):
        out = send if b % 2 else keep
        at = (b // 2) * rows + latent * part
        out[at : at + part, :] = value[b * part : (b + 1) * part]


def softmax(q, k):
    scores = dot(q, k, (1, 1)) * FACTOR
    weights = jnp.exp(scores - jnp.max(scores, axis=-1, keepdims=True))
    return weights * (1.0 / jnp.sum(weights, axis=-1, keepdims=True))


def attn_kernel(rows, qkv_w, proj_w, bias, qkv, att, keep, send, *, latents):
    cols = proj_w.shape[1]
    size = rows.shape[0] // latents
    for l in range(latents):
        here = slice(l * size, (l + 1) * size)
        projected = (dot(rows[here, :], qkv_w[...]) + bias[...]).astype(BF)
        qkv[here, :] = projected
        mixed = []
        for h in range(cols // HEAD):
            q, k, v = [
                projected[:, j * cols + h * HEAD : j * cols + (h + 1) * HEAD] for j in range(3)
            ]
            mixed.append(dot(softmax(q, k).astype(BF), v))
        attended = jnp.concatenate(mixed, axis=1).astype(BF)
        att[here, :] = attended
        put_parts(dot(attended, proj_w[...], (1, 1)).astype(BF), keep, send, l)


def middle_kernel(x, p0, p1, bias, mod, branch_out, middle_out, out):
    latents = mod.shape[0] // 6
    rows = out.shape[0] // latents
    for l in range(latents):
        here = slice(l * rows, (l + 1) * rows)
        branch = bias[...] + p0[here, :] + p1[here, :].astype(F32)
        branch_out[here, :] = branch
        gate = mod[6 * l + 2 : 6 * l + 3, :]
        middle = x[here, :].astype(F32) + gate * branch
        middle_out[here, :] = middle
        n, _ = normed(middle)
        shift = mod[6 * l + 3 : 6 * l + 4, :]
        scale = mod[6 * l + 4 : 6 * l + 5, :]
        out[here, :] = (n * (1.0 + scale) + shift).astype(BF)


def mlp_kernel(
    x0, x1, x2, x3, grads, first, second, bias, act_out, pre_out, x_out, keep, send
):
    rows = x0.shape[0]
    for b, x in enumerate((x0, x1, x2, x3)):
        here = slice(b * rows, (b + 1) * rows)
        x_out[here, :] = x[...]
        v = dot(x[...], first[...]) + bias[...]
        square = v * v
        t = jnp.tanh(CURVE * v * (1.0 + CUBIC * square))
        act_out[here, :] = (0.5 * v * (1.0 + t)).astype(BF)
        slope = 0.5 * (1.0 + t) + 0.5 * v * (1.0 - t * t) * CURVE * (1.0 + 3.0 * CUBIC * square)
        pre = (dot(grads[here, :], second[...]) * slope).astype(BF)
        pre_out[here, :] = pre
        at = (b // 2) * rows
        out = send if b % 2 else keep
        out[at : at + rows, :] = dot(pre, first[...], (1, 1)).astype(BF)


def store_grad(rank, product, keep, send, cols, step):
    rows = keep.shape[1]
    for half in range(2):

        @pl.when((rank[0] // step) % 2 == half)
        def _(half=half):
            for k in range(2 * keep.shape[0]):
                to = jnp.bitwise_xor(rank[0], k)
                if step == 1:
                    place = (to // 2 % 2) * 2 + to // 4
                else:
                    place = (to // 4) * 2 + to % 2
                target = keep if (k // step) % 2 == half else send
                target[place, :, cols] = product[k * rows : (k + 1) * rows]


def mlp_grad_kernel(rank, left, right, keep, send, *bias_out, step):
    product = dot(left[...], right[...], (0, 0)).astype(BF)
    store_grad(rank, product, keep, send, slice(0, right.shape[1]), step)
    if bias_out:
        bias_out[0][...] = jnp.sum(right[...].astype(F32), axis=0, keepdims=True)


def mlp_out_kernel(act, second, x0, x1, x2, x3, bias, keep, send, sums, *, latents):
    rows = keep.shape[0] // 2
    part = rows // latents
    sums[...] = jnp.zeros_like(sums)
    for b, x in enumerate((x0, x1, x2, x3)):
        at = (b // 2) * rows
        out = send if b % 2 else keep
        value = dot(act[b * rows : (b + 1) * rows, :], second[...], (1, 1))
        out[at : at + rows, :] = value.astype(BF)
        if b == 0:
            value = value + bias[...]
        grad = value * x[rows:, :].astype(F32)
        for l in range(latents):
            sums[l : l + 1, :] += jnp.sum(
                grad[l * part : (l + 1) * part], axis=0, keepdims=True
            )


def output_kernel(middle, p0, p1, bias, mod, out):
    latents = mod.shape[0] // 6
    rows = middle.shape[0] // latents
    for l in range(latents):
        here = slice(l * rows, (l + 1) * rows)
        branch = bias[...] + p0[here, :] + p1[here, :].astype(F32)
        out[here, :] = (middle[here, :] + mod[6 * l + 5 : 6 * l + 6, :] * branch).astype(BF)


def middle_back_kernel(x, middle, branch, p0, p1, mod, grad_out, out, sums):
    latents = mod.shape[0] // 6
    width = middle.shape[1]
    size = middle.shape[0]
    rows = size // latents
    total = jnp.zeros((1, width), F32)
    for l in range(latents):
        here = slice(l * rows, (l + 1) * rows)
        grad = p0[here, :] + p1[here, :].astype(F32)
        cot = x[size + l * rows : size + (l + 1) * rows, :].astype(F32)
        n, scale = normed(middle[here, :])
        sums[3 * l + 1 : 3 * l + 2, :] = jnp.sum(grad, axis=0, keepdims=True)
        sums[3 * l + 2 : 3 * l + 3, :] = jnp.sum(grad * n, axis=0, keepdims=True)
        factor = 1.0 + mod[6 * l + 4 : 6 * l + 5, :]
        whole = cot + norm_back(n, scale, grad * factor)
        grad_out[here, :] = whole
        sums[3 * l : 3 * l + 1, :] = jnp.sum(whole * branch[here, :], axis=0, keepdims=True)
        low = (whole * mod[6 * l + 2 : 6 * l + 3, :]).astype(BF)
        out[here, :] = low
        total = total + jnp.sum(low.astype(F32), axis=0, keepdims=True)
    sums[3 * latents : 3 * latents + 1, :] = total


def attn_back_kernel(
    g0, g1, g2, g3, qkv_w, proj_w, qkv, rows, grads, keep, send, bias_out, *, latents
):
    unpack_rows([g0, g1, g2, g3], rows, latents)
    cols = proj_w.shape[1]
    size = rows.shape[0] // latents
    for l in range(latents):
        here = slice(l * size, (l + 1) * size)
        back = dot(rows[here, :], proj_w[...]).astype(BF)
        projected = qkv[here, :]
        found = [[], [], []]
        for h in range(cols // HEAD):
            q, k, v = [
                projected[:, j * cols + h * HEAD : j * cols + (h + 1) * HEAD] for j in range(3)
            ]
            up = back[:, h * HEAD : (h + 1) * HEAD]
            probs = softmax(q, k)
            grad_probs = dot(up, v, (1, 1))
            inner = jnp.sum(probs * grad_probs, axis=-1, keepdims=True)
            scores = (probs * (grad_probs - inner)).astype(BF)
            found[0].append(dot(scores, k) * FACTOR)
            found[1].append(dot(scores, q, (0, 0)) * FACTOR)
            found[2].append(dot(probs.astype(BF), up, (0, 0)))
        grad = jnp.concatenate(found[0] + found[1] + found[2], axis=1).astype(BF)
        grads[here, :] = grad
        part = jnp.sum(grad.astype(F32), axis=0, keepdims=True)
        total = part if l == 0 else total + part
        put_parts(dot(grad, qkv_w[...], (1, 1)).astype(BF), keep, send, l)
    bias_out[...] = total


def attn_grad_kernel(rank, rows, grads, back, att, keep, send):
    cut = grads.shape[1]
    product = dot(rows[...], grads[...], (0, 0)).astype(BF)
    store_grad(rank, product, keep, send, slice(0, cut), 1)
    product = dot(back[...], att[...], (0, 0)).astype(BF)
    store_grad(rank, product, keep, send, slice(cut, keep.shape[2]), 1)


def input_back_kernel(
    x, grad_middle, p0, p1, mod, sums, gates, fc2, fc1, qkv, out, pack, scr
):
    latents = mod.shape[0] // 6
    rows = out.shape[0] // latents
    cols = qkv.shape[1] // 3
    scr[...] = jnp.zeros_like(scr)
    for l in range(latents):
        here = slice(l * rows, (l + 1) * rows)
        grad = p0[here, :] + p1[here, :].astype(F32)
        n, scale = normed(x[here, :].astype(F32))
        scr[6 * l : 6 * l + 1, :] = jnp.sum(grad, axis=0, keepdims=True)
        scr[6 * l + 1 : 6 * l + 2, :] = jnp.sum(grad * n, axis=0, keepdims=True)
        scr[6 * l + 2 : 6 * l + 5, :] = sums[3 * l : 3 * l + 3, :]
        scr[6 * l + 5 : 6 * l + 6, :] = gates[l : l + 1, :]
        factor = 1.0 + mod[6 * l + 1 : 6 * l + 2, :]
        out[here, :] = grad_middle[here, :] + norm_back(n, scale, grad * factor)
    at = 6 * latents
    scr[at : at + 1, :] = sums[3 * latents : 3 * latents + 1, :]
    scr[at + 1 : at + 2, :] = fc2[...]
    scr[at + 2 : at + 3, :] = fc1[...]
    scr[at + 3 : at + 4, 0:cols] = qkv[:, 0:cols]
    scr[at + 3 : at + 4, cols : 2 * cols] = qkv[:, 2 * cols :]
    pack[...] = scr[...].astype(BF)


def spread_kernel(
    rank, tp_rank, k0, k1, k2, k3, keep, send, parts, total, *, latents, feat
):
    count = 2 * keep.shape[0]
    packs = (k0, k1, k2, k3)
    per = count // len(packs)
    cols = per * feat
    mods = 6 * latents
    summed = jnp.zeros(k0.shape, F32)
    for d, pack in enumerate(packs):
        value = pack[...].astype(F32)
        parts[jnp.bitwise_xor(tp_rank[0], d)] = value
        summed = summed + value
    total[...] = summed
    row = slice(mods, mods + 1)
    total[row, :] = jnp.zeros((1, k0.shape[1]), F32)
    for k in range(count):
        t, i = k // per, k % per
        here = slice(k * feat, (k + 1) * feat)
        total[row, 0:feat] = parts[t, mods + 3 : mods + 4, i * feat : (i + 1) * feat]
        total[row, feat : 2 * feat] = parts[
            t, mods + 3 : mods + 4, cols + i * feat : cols + (i + 1) * feat
        ]
        total[row, 2 * feat : 3 * feat] = summed[mods : mods + 1, here]
        total[row, 3 * feat : 4 * feat] = summed[mods + 1 : mods + 2, here]
        total[row, 4 * feat : 8 * feat] = parts[
            t, mods + 2 : mods + 3, 4 * i * feat : 4 * (i + 1) * feat
        ]
        put_piece(rank, k, total[...].astype(BF), keep, send)


def silu_kernel(*refs, latents):
    *got, ada, keep, send, grads, bias_out, scr, out_scr = refs
    width = ada.shape[1] // 6
    feat = ada.shape[0]
    count = scr.shape[1] // latents
    mods = 6 * latents
    bias = jnp.zeros((1, width), F32)
    for k in range(count):
        value = pick(got, k)[...].astype(F32)
        bias = bias + value[mods : mods + 1]
        for l in range(latents):
            for j in range(6):
                scr[j, k * latents + l : k * latents + l + 1, :] = value[6 * l + j : 6 * l + j + 1]
    bias_out[...] = bias
    total = jnp.zeros((count * latents, feat), F32)
    for j in range(6):
        at = slice(j * width, (j + 1) * width)
        rows = scr[j].astype(BF)
        grads[:, at] = rows
        total = total + dot(rows, ada[:, at], (1, 1))
    out_scr[...] = jnp.zeros_like(out_scr)
    for k in range(count):
        out_scr[k, 0:latents, 0:feat] = total[k * latents : (k + 1) * latents]
    for z in range(count // 2):
        keep[z] = out_scr[2 * z]
        send[z] = out_scr[2 * z + 1]


def cond_kernel(rank, *refs, latents, feat):
    *got, cond, out, scr = refs
    count = scr.shape[0]
    for k in range(count):
        scr[jnp.bitwise_xor(rank[0], k)] = pick(got, k)[...]
    value = cond[...].astype(F32)
    gate = 1.0 / (1.0 + jnp.exp(-value))
    slope = gate * (1.0 + value * (1.0 - gate))
    for k in range(count):
        here = slice(k * feat, (k + 1) * feat)
        out[:, here] = scr[k, 0:latents, 0:feat] * slope[:, here]


def scatter_pieces(keep, send):
    count = 2 * keep.shape[0]
    order = jnp.bitwise_xor(jnp.arange(count), lax.axis_index("fsdp"))
    whole = jnp.stack([keep, send], axis=1).reshape(count, *keep.shape[1:]).astype(F32)
    whole = jnp.take(whole, order, axis=0)
    return lax.psum_scatter(whole, "fsdp", scatter_dimension=0, tiled=False)


def halve_kernel(keep, got, own, out):
    half = own.shape[0]
    for i in range(half):
        own[i] = keep[i].astype(F32) + got[i].astype(F32)
        out[i] = (keep[half + i].astype(F32) + got[half + i].astype(F32)).astype(BF)


def halve(keep, send, offset, ordered=()):
    got = swap(send, "fsdp", offset)
    shape = (keep.shape[0] // 2, *keep.shape[1:])
    outs = [(shape, F32), (shape, BF)]
    return call(halve_kernel, "halve", outs, [keep, got], ordered=ordered)


def add_kernel(own, got, out):
    out[...] = own[...] + got[...].astype(F32)


def last_sum(own, out, offset):
    got = swap(out, "fsdp", offset)
    total = call(add_kernel, "last_sum", [(own.shape, F32)], [own, got])[0]
    return total.reshape(own.shape[1:])


def attn_add_kernel(own, got, qkv, proj):
    cols = qkv.shape[2]
    for j in range(3):
        here = slice(j * cols, (j + 1) * cols)
        qkv[j] = own[0, :, here] + got[0, :, here].astype(F32)
    here = slice(3 * cols, 4 * cols)
    proj[...] = (own[0, :, here] + got[0, :, here].astype(F32)).T


def shards(
    inputs,
    conditioning,
    ada_weight,
    ada_bias,
    query_key_value_weight,
    qv_bias,
    attention_output_weight,
    attention_output_bias,
    expand_weight,
    hidden_layer_bias,
    contract_weight,
    contract_bias,
    out_cotangent,
):
    tp_rank = lax.axis_index("tp")
    tp_count = lax.axis_size("tp")
    rank = lax.axis_index("fsdp")
    count = lax.axis_size("fsdp")
    positions, latents, width = inputs.shape
    feat = ada_weight.shape[0]
    cols = query_key_value_weight.shape[2]
    hidden = expand_weight.shape[1]
    hidden_part = hidden_layer_bias.shape[0]
    mod_part = ada_bias.shape[0]
    rows = positions * latents
    tokens = rows * tp_count
    mods = 6 * latents
    direct = count == 8
    block = ((rows, width), BF)
    block_f32 = ((rows, width), F32)

    qkv_own = query_key_value_weight.transpose(1, 0, 2)
    first_ops = []
    if direct:
        attn_own = call(
            attn_own_kernel,
            "attn_own",
            [((feat, 4 * cols), BF)],
            [qkv_own, attention_output_weight],
            fetch=True,
        )[0]
        first_ops = [attn_own]
        attn_two = join(attn_own, swap(attn_own, "fsdp", 4))

    half = count // 2
    bias_own = jnp.concatenate(
        [qv_bias.reshape(-1), attention_output_bias, contract_bias, hidden_layer_bias]
    )
    cond_keep, cond_send = call(
        pack_kernel,
        "pack_conditioning",
        [((half, 16, 128), F32)] * 2,
        [conditioning, bias_own],
        [rank],
        scratch=[pltpu.VMEM((16, 128), F32)],
        ordered=first_ops,
    )
    cond_got = exchange(cond_keep, cond_send, [attn_two] if direct else ())

    bias_row = lax.dynamic_update_slice(
        jnp.zeros((1, mod_part * count), F32),
        ada_bias.astype(F32).reshape(1, mod_part),
        (0, rank * mod_part),
    )
    mod_keep, mod_send, cond_cols = call(
        mod_kernel,
        "modulation",
        [((half, 16, width), BF)] * 2 + [((count * latents, feat), BF)],
        [*cond_got, ada_weight, bias_row],
        scratch=[
            pltpu.VMEM((count * latents, 128), F32),
            pltpu.VMEM((count, 16, width), F32),
        ],
    )
    x_own = jnp.stack([inputs.transpose(1, 0, 2), out_cotangent.transpose(1, 0, 2)])
    x_own = x_own.reshape(2 * rows, width)
    x_own = call(
        copy_kernel, "tokens", [((2 * rows, width), BF)], [x_own], ordered=cond_got
    )[0]
    x_blocks = tp_gather(x_own)

    if direct:
        half_one = halve(mod_keep, mod_send, 1)
        half_two = halve(*half_one, 2)
        mod_parts = [half_two[0], swap(half_two[1], "fsdp", 4)]
        attn_four = join(attn_two, swap(attn_two, "fsdp", 2), [mod_send])
        attn_other = swap(attn_four, "fsdp", 1)
        first_own = call(
            copy_kernel,
            "first_own",
            [((feat, hidden), BF)],
            [expand_weight],
            ordered=[mod_send],
            fetch=True,
        )[0]
        first_two, first_four, first_other = gather_steps(first_own, ([half_two[1]], [mod_parts[1]]))
        second_own = call(
            copy_kernel,
            "second_own",
            [((feat, hidden), BF)],
            [contract_weight.T],
            ordered=[first_four],
            fetch=True,
        )[0]
        second_two, second_four, second_other = gather_steps(second_own)
        qkv_full, proj_full = call(
            assemble_kernel,
            "attn_weights",
            [((width, 3 * cols), BF), ((width, cols), BF)],
            [attn_four, attn_other],
            [rank],
        )
        first_full = call(
            assemble_kernel,
            "first_weights",
            [((width, hidden), BF)],
            [first_four, first_other],
            [rank],
        )[0]
        second_full = call(
            assemble_kernel,
            "second_weights",
            [((width, hidden), BF)],
            [second_four, second_other],
            [rank],
        )[0]
        steps = [[attn_four], [first_four], [second_two], [], [second_four, first_full]]
    else:
        steps = [[]] * 5
        mod_parts = [scatter_pieces(mod_keep, mod_send)]
        qkv_full = lax.all_gather(
            query_key_value_weight.reshape(feat, 3 * cols), "fsdp", axis=0, tiled=True
        )
        proj_full = lax.all_gather(attention_output_weight.T, "fsdp", axis=0, tiled=True)
        first_full = lax.all_gather(expand_weight, "fsdp", axis=0, tiled=True)
        second_full = lax.all_gather(contract_weight.T, "fsdp", axis=0, tiled=True)

    qkv_bias, proj_bias, second_bias, hidden_bias = call(
        functools.partial(bias_kernel, latents=latents, feat=feat, tp=tp_count),
        "biases",
        [((1, 3 * cols), F32), ((1, width), F32), ((1, width), F32), ((1, hidden), F32)],
        cond_got,
        [rank, tp_rank],
        scratch=[pltpu.VMEM((count, 16, 128), F32)],
        ordered=[cond_cols],
        flops=1e9,
    )
    mod, attn_rows = call(
        first_norm_kernel,
        "first_norm",
        [((mods, width), F32), ((tokens, width), BF)],
        [*x_blocks, *mod_parts],
        ordered=[hidden_bias, *steps[0]],
    )
    pair = ((2 * rows, width), BF)
    qkv, att, keep, send = call(
        functools.partial(attn_kernel, latents=latents),
        "attention",
        [((tokens, 3 * cols), BF), ((tokens, cols), BF), pair, pair],
        [attn_rows, qkv_full, proj_full, qkv_bias],
        ordered=steps[1],
    )
    branch_parts = tp_scatter(keep, send, steps[2])
    grad_rows, fc2_part = call(
        gate_grad_kernel,
        "gate_grad",
        [((tokens, width), BF), ((1, width), F32)],
        [*x_blocks, mod],
        ordered=[branch_parts[0], *steps[3]],
        flops=1e9,
    )
    branch, middle, mlp_in = call(
        middle_kernel,
        "middle",
        [block_f32, block_f32, block],
        [x_own, *branch_parts, proj_bias, mod],
        ordered=[fc2_part, *steps[4]],
    )
    m_blocks = tp_gather(mlp_in)
    act, pre, mlp_rows, keep, send = call(
        mlp_kernel,
        "mlp",
        [((tokens, hidden), BF)] * 2 + [((tokens, width), BF), pair, pair],
        [*m_blocks, grad_rows, first_full, second_full, hidden_bias],
    )
    first_done = []
    if direct:
        blocks = [((half, feat, hidden), BF)] * 2
        first_keep, first_send, fc1_part = call(
            functools.partial(mlp_grad_kernel, step=1),
            "first_grad",
            blocks + [((1, hidden), F32)],
            [mlp_rows, pre],
            [rank],
            ordered=[send],
            flops=2e9,
        )
        first_done = [fc1_part]
    grad_in = tp_scatter(keep, send, first_done)
    out_keep, out_send, gates = call(
        functools.partial(mlp_out_kernel, latents=latents),
        "mlp_out",
        [pair, pair, ((8, width), F32)],
        [act, second_full, *x_blocks, second_bias],
        ordered=[grad_in[0]],
        flops=1.5e9,
    )
    if direct:
        second_keep, second_send = call(
            functools.partial(mlp_grad_kernel, step=1),
            "second_grad",
            blocks,
            [grad_rows, act],
            [rank],
            ordered=[out_send],
            flops=2e9,
        )
        first_half = halve(first_keep, first_send, 1)
        second_sent = call(
            copy_kernel, "second_sent", blocks[:1], [second_send], ordered=[first_half[1]]
        )[0]
        steps = [[first_half[1], second_sent]]
    else:
        first_sum = lax.psum_scatter(
            dot(mlp_rows, pre, (0, 0)), "fsdp", scatter_dimension=0, tiled=True
        )
        second_sum = lax.psum_scatter(
            dot(grad_rows, act, (0, 0)), "fsdp", scatter_dimension=0, tiled=True
        )
        fc1_part = jnp.sum(pre.astype(F32), axis=0, keepdims=True)
        steps = [[]]
        second_keep = fc1_part

    grad_middle, grad_attn, sums = call(
        middle_back_kernel,
        "middle_back",
        [block_f32, block, ((8, width), F32)],
        [x_own, middle, branch, *grad_in, mod],
        ordered=[second_keep],
    )
    a_blocks = tp_gather(grad_attn)
    mlp_parts = tp_scatter(out_keep, out_send, [a_blocks[2]])
    back_rows, grads, keep, send, qkv_part = call(
        functools.partial(attn_back_kernel, latents=latents),
        "attention_back",
        [((tokens, width), BF), ((tokens, 3 * cols), BF), pair, pair, ((1, 3 * cols), F32)],
        [*a_blocks, qkv_full, proj_full, qkv],
        ordered=[mlp_parts[0], *steps[0]],
    )
    output = call(
        output_kernel, "output", [block], [middle, *mlp_parts, second_bias, mod]
    )[0]
    grad_in = tp_scatter(keep, send)
    if direct:
        attn_keep, attn_send = call(
            attn_grad_kernel,
            "attn_weight_grad",
            [((half, feat, 4 * cols), BF)] * 2,
            [attn_rows, grads, back_rows, att],
            [rank],
            ordered=[grad_in[0], output],
            flops=6e9,
        )
    else:
        qkv_sum = lax.psum_scatter(
            dot(attn_rows, grads, (0, 0)), "fsdp", scatter_dimension=0, tiled=True
        ).reshape(feat, 3, cols)
        proj_sum = lax.psum_scatter(
            dot(back_rows, att, (0, 0)), "fsdp", scatter_dimension=0, tiled=True
        ).T

    inputs_grad, pack = call(
        input_back_kernel,
        "input_back",
        [block_f32, ((16, width), BF)],
        [x_own, grad_middle, *grad_in, mod, sums, gates, fc2_part, fc1_part, qkv_part],
        scratch=[pltpu.VMEM((16, width), F32)],
    )
    tail = [[]] * 3
    if direct:
        first_one = halve(*first_half, 2, [pack])
        first_sum = last_sum(*first_one, 4)
        second_half = halve(second_keep, second_sent, 1, [pack])
        tail[0] = [first_one[1], second_half[1]]
    packs = [pack] + [swap(pack, "tp", d) for d in range(1, tp_count)]
    spread_keep, spread_send = call(
        functools.partial(spread_kernel, latents=latents, feat=feat),
        "spread",
        [((half, 16, width), BF)] * 2,
        packs,
        [rank, tp_rank],
        scratch=[pltpu.VMEM((tp_count, 16, width), F32), pltpu.VMEM((16, width), F32)],
        ordered=tail[0],
    )
    spread_got = None
    if direct:
        spread_got = swap(spread_send, "fsdp", 1)
        attn_half = halve(attn_keep, attn_send, 1, [spread_got])
        attn_own_sum, attn_out = halve(*attn_half, 2)
        qkv_sum, proj_sum = call(
            attn_add_kernel,
            "attn_sum",
            [((3, feat, cols), F32), ((cols, feat), F32)],
            [attn_own_sum, swap(attn_out, "fsdp", 4)],
        )
        qkv_sum = qkv_sum.transpose(1, 0, 2)
        second_one = halve(*second_half, 2, [spread_got])
        tail[1] = [attn_half[1], second_one[1]]
        tail[2] = [attn_out]
    silu_keep, silu_send, grad_mod_all, bias_grads = call(
        functools.partial(silu_kernel, latents=latents),
        "silu_columns",
        [((half, 8, 128), F32)] * 2
        + [((count * latents, 6 * width), BF), ((1, width), F32)],
        [*exchange(spread_keep, spread_send, tail[1], spread_got), ada_weight],
        scratch=[
            pltpu.VMEM((6, count * latents, width), F32),
            pltpu.VMEM((count, 8, 128), F32),
        ],
        ordered=tail[2],
    )
    if direct:
        second_last = call(
            copy_kernel,
            "second_last",
            [(second_one[1].shape, BF)],
            [second_one[1]],
            ordered=[silu_send],
        )[0]
        second_sum = last_sum(second_one[0], second_last, 4)
    cond_grad = call(
        functools.partial(cond_kernel, latents=latents, feat=feat),
        "cond_grad",
        [((latents, width), F32)],
        [*exchange(silu_keep, silu_send), conditioning],
        [rank],
        scratch=[pltpu.VMEM((count, 8, 128), F32)],
    )[0]
    ada_weight_grad = dot(cond_cols, grad_mod_all, (0, 0))
    bias_grads = bias_grads.reshape(width)
    ada_bias_grad = jnp.sum(
        lax.dynamic_slice_in_dim(grad_mod_all, rank * mod_part, mod_part, 1).astype(F32), axis=0
    )

    return (
        output.reshape(latents, positions, width).transpose(1, 0, 2),
        inputs_grad.reshape(latents, positions, width).transpose(1, 0, 2),
        cond_grad,
        ada_weight_grad,
        ada_bias_grad,
        qkv_sum,
        bias_grads[: 2 * feat].reshape(2, feat),
        proj_sum,
        bias_grads[2 * feat : 3 * feat],
        first_sum,
        bias_grads[4 * feat : 4 * feat + hidden_part],
        second_sum.T,
        bias_grads[3 * feat : 4 * feat],
    )


def solution(mesh):
    return jax.shard_map(
        shards,
        mesh=mesh,
        in_specs=(
            P("tp", "fsdp", None),
            P("fsdp", None),
            P("fsdp", None),
            P("fsdp"),
            P("fsdp", None, "tp"),
            P(None, "fsdp"),
            P("tp", "fsdp"),
            P("fsdp"),
            P("fsdp", "tp"),
            P("fsdp"),
            P("tp", "fsdp"),
            P("fsdp"),
            P("tp", "fsdp", None),
        ),
        out_specs=(
            P("tp", "fsdp", None),
            P("tp", "fsdp", None),
            P("fsdp", None),
            P("fsdp", None),
            P("fsdp"),
            P("fsdp", None, "tp"),
            P(None, "fsdp"),
            P("tp", "fsdp"),
            P("fsdp"),
            P("fsdp", "tp"),
            P("fsdp"),
            P("tp", "fsdp"),
            P("fsdp"),
        ),
        check_vma=False,
    )
```
